32 devices in a mesh: section: 2 (over x), dp: 4 (over z), tensor: 4 (over y, core).
Axes of the slice: x: 2, y: 2, z: 4, core: 2. Of those that a mesh axis runs over, the one named last changes fastest.
Arguments:
- hidden: bfloat16 [8, 1024, 768], P('dp', 'tensor'), may hold values from -6 to 6
- cotangent: bfloat16 [8, 1024, 768], P('dp', 'tensor'), may hold values from -6 to 6
- pair_lengths: int32 [8], P('dp'), may hold values from 256 to 1024, as said below
- query_lengths: int32 [8], P('dp'), may hold values from 1 to 256, as said below
- buckets: int32 [2047], replicated, may hold values from 0 to 31
- qkv_weight: bfloat16 [2, 768, 3, 768], P('section', None, None, 'tensor'), may hold values from -0.21875 to 0.21875
- qv_bias: float32 [2, 2, 768], P('section', None, 'tensor'), may hold values from -3 to 3
- out_weight: bfloat16 [2, 768, 768], P('section', 'tensor'), may hold values from -1.25 to 1.25
- up_weight: bfloat16 [2, 768, 3072], P('section', None, 'tensor'), may hold values from -0.21875 to 0.21875
- ffn_bias: float32 [2, 3072], P('section', 'tensor'), may hold values from -3 to 3
- down_weight: bfloat16 [2, 3072, 768], P('section', 'tensor'), may hold values from -0.109375 to 0.109375
- norm_gains: float32 [2, 2, 768], P('section'), may hold values from 0.5 to 1.5
- vectors: float32 [2, 4, 768], P('section'), may hold values from -3 to 3
- bias_table: float32 [2, 12, 64], P('section', 'tensor'), may hold values from -5 to 5
Outputs:
- edges: float32 [2, 8, 1024, 768], P('section', 'dp', 'tensor')
- qkv_weight_grad: float32 [2, 768, 3, 768], P('section', None, None, 'tensor')
- qv_bias_grad: float32 [2, 2, 768], P('section', None, 'tensor')
- out_weight_grad: float32 [2, 768, 768], P('section', 'tensor')
- up_weight_grad: float32 [2, 768, 3072], P('section', None, 'tensor')
- ffn_bias_grad: float32 [2, 3072], P('section', 'tensor')
- down_weight_grad: float32 [2, 3072, 768], P('section', 'tensor')
- gain_grad: float32 [2, 2, 768], P('section', None, 'tensor')
- vector_grad: float32 [2, 4, 768], P('section', None, 'tensor')
- table_grad: float32 [2, 12, 64], P('section', 'tensor')
The draws below stay inside these ranges and needn't reach their ends.
Inputs may be any that keep to these rules, and one draw needn't show every extreme that they name: `pair_lengths`: in each group of 2 consecutive pairs one, drawn from the seed, has all 1024 tokens live. `query_lengths`: A query is never longer than the shortest pair.
All inputs are finite; a program needn't handle non-finite values.
Results may differ from the reference program's by a relative error of at most 0.019.
Values may be sent and summed in bfloat16 or wider, within the bound.
No kernel may reach another device: no remote copies, remote signals or barrier semaphores. Data moves between devices by JAX's collectives and lax.ppermute only.
A program may use at most 320 MiB of HBM per device.

```python
import jax
import jax.numpy as jnp
from jax import lax

D = 768
H = 12
FF = 3072
NB = 32
LEN = 1024
PAIRS_DEV = 2
PAIRS = 8
N_SECTION = 2


def draw_pair_lengths(key, part):
    key = jax.random.fold_in(key, 11)
    first_key, second_key = jax.random.split(key)
    spread = jax.random.randint(first_key, (PAIRS,), LEN // 4, LEN + 1)
    groups = PAIRS // PAIRS_DEV
    chosen = jax.random.randint(second_key, (groups,), 0, PAIRS_DEV)
    within = jnp.arange(PAIRS, dtype=jnp.int32) % PAIRS_DEV
    owner = jnp.repeat(chosen, PAIRS_DEV, total_repeat_length=PAIRS)
    return jnp.where(within == owner, LEN, spread).astype(jnp.int32)


def draw_query_lengths(key, part):
    key = jax.random.fold_in(key, 23)
    first_key, second_key = jax.random.split(key)
    spread = jax.random.randint(first_key, (PAIRS,), 1, LEN // 4 + 1)
    chosen = jax.random.randint(second_key, (), 0, PAIRS)
    places = jnp.arange(PAIRS, dtype=jnp.int32)
    return jnp.where(places == chosen, LEN // 4, spread).astype(jnp.int32)


def plant(result, stream_key, least, top_value):
    longest = result.shape.index(max(result.shape))
    spots = []
    for shift in (0, 1):
        where = [jax.random.randint(jax.random.fold_in(stream_key, axis), (), 0, length) for axis, length in enumerate(result.shape)]
        where[longest] = (where[longest] + shift) % result.shape[longest]
        spots.append(tuple(where))
    return result.at[spots[0]].set(least).at[spots[1]].set(top_value)


def steps_of(rng, extent, shards, smallest, high):
    level = 1.0
    for dim, blocks in shards:
        steps = jax.random.uniform(jax.random.fold_in(jax.random.fold_in(rng, 6), dim), (blocks,), jnp.float32, smallest / len(shards), high / len(shards))
        level = level * jnp.repeat(jnp.exp(steps), extent[dim] // blocks).reshape((-1,) + (1,) * (len(extent) - 1 - dim))
    return level


def bell_draw(stream_key, extent, deviation, limit, shards=(), kind=jnp.bfloat16):
    array = deviation * jax.random.normal(stream_key, extent, jnp.float32)
    if shards:
        array = array * steps_of(stream_key, extent, shards, -0.22, 0.18)
    return jnp.clip(array, -limit, limit).astype(kind)


def setup_inputs(seed: int = 0) -> dict:
    key_of = jax.random.split(jax.random.key(seed), 15)
    hidden = bell_draw(key_of[0], (PAIRS, LEN, D), 1.0, 6.0, ((0, 4), (1, 4)))
    cotangent = bell_draw(key_of[1], (PAIRS, LEN, D), 1.0, 6.0, ((0, 4), (1, 4)))
    pair_lengths = draw_pair_lengths(jax.random.fold_in(key_of[14], 71), 0)
    query_lengths = draw_query_lengths(jax.random.fold_in(key_of[14], 71), 0)
    buckets = plant(jax.random.randint(key_of[4], (2 * LEN - 1,), 0, NB), jax.random.fold_in(key_of[4], 1), 0, NB - 1).astype(jnp.int32)
    qkv_weight = bell_draw(key_of[5], (N_SECTION, D, 3, D), D ** -0.5, 0.21875, ((0, 2), (3, 4)))
    qv_bias = bell_draw(key_of[6], (N_SECTION, 2, D), 0.5, 3.0, ((0, 2), (2, 4)), jnp.float32)
    out_weight = bell_draw(key_of[7], (N_SECTION, D, D), (max(D * 32 // LEN, 1)) ** -0.5, 1.25, ((0, 2), (1, 4)))
    up_weight = bell_draw(key_of[8], (N_SECTION, D, FF), D ** -0.5, 0.21875, ((0, 2), (2, 4)))
    ffn_bias = bell_draw(key_of[9], (N_SECTION, FF), 0.5, 3.0, ((0, 2), (1, 4)), jnp.float32)
    down_weight = bell_draw(key_of[10], (N_SECTION, FF, D), FF ** -0.5, 0.109375, ((0, 2), (1, 4)))
    norm_gains = jnp.clip(1.0 + 0.1 * jax.random.normal(key_of[11], (N_SECTION, 2, D), jnp.float32), 0.5, 1.5)
    vectors = bell_draw(key_of[12], (N_SECTION, 4, D), 0.5, 3.0, ((0, 2),), jnp.float32)
    bias_table = bell_draw(key_of[13], (N_SECTION, H, 2 * NB), 1.0, 5.0, ((0, 2), (1, 4)), jnp.float32)
    return dict(hidden=hidden, cotangent=cotangent, pair_lengths=pair_lengths, query_lengths=query_lengths, buckets=buckets, qkv_weight=qkv_weight, qv_bias=qv_bias, out_weight=out_weight, up_weight=up_weight, ffn_bias=ffn_bias, down_weight=down_weight, norm_gains=norm_gains, vectors=vectors, bias_table=bias_table)


epsilon = 1e-05
scaling = 0.125
negative = -1e+30
highest = lax.Precision.HIGHEST

@jax.custom_vjp
def low(v):
    return lax.optimization_barrier(v.astype(jnp.bfloat16)).astype(jnp.float32)

@jax.custom_vjp
def low_back(v):
    return v

def low_keep(v):
    return (low(v), None)

def low_pass(kept, grad):
    return (grad,)

def back_keep(v):
    return (v, None)

def back_low(kept, grad):
    return (low(grad),)
low.defvjp(low_keep, low_pass)
low_back.defvjp(back_keep, back_low)

def norm_apply(values, gain, shift):
    centre = lax.optimization_barrier(jnp.mean(values, -1, keepdims=True))
    centred = values - centre
    spread = lax.optimization_barrier(jnp.mean(centred * centred, -1, keepdims=True))
    return centred * lax.rsqrt(spread + epsilon) * gain + shift

def relative_bias(table, buckets, query_len, total):
    places = jnp.arange(total, dtype=jnp.int32)
    offsets = (places[:, None] - places[None, :] + (total - 1)).astype(jnp.int32)
    kinds = table.shape[1] // 2
    index = buckets[offsets].astype(jnp.int32)
    within = table[:, index]
    across = table[:, index + kinds]
    side = places >= query_len
    crossing = side[:, None] != side[None, :]
    return jnp.where(crossing[None], across, within)

def layer(params, which, inputs, buckets, pair_len, query_len):
    qkv_w, qv_b, out_w, up_w, up_b, down_w, gains, shifts, table = [item[which] for item in params]
    total, model = inputs.shape
    heads = table.shape[0]
    head_size = model // heads
    mixed = jnp.dot(low(inputs), qkv_w.reshape(model, 3 * model), precision=highest).reshape(total, 3, model)
    queries = low(low_back(mixed[:, 0] + qv_b[0])).reshape(total, heads, head_size)
    key_rows = low(low_back(mixed[:, 1])).reshape(total, heads, head_size)
    value_rows = low(low_back(mixed[:, 2] + qv_b[1])).reshape(total, heads, head_size)
    scores = jnp.einsum('ihd,jhd->hij', queries, key_rows, precision=highest) * scaling
    scores = low_back(scores + relative_bias(table, buckets, query_len, total))
    live = jnp.arange(total, dtype=jnp.int32) < pair_len
    scores = jnp.where(live[None, None, :], scores, negative)
    log_total = jax.nn.logsumexp(scores, axis=-1, keepdims=True)
    probs = low(jnp.exp(scores - log_total))
    attended = jnp.einsum('hij,jhd->ihd', probs, value_rows, precision=highest).reshape(total, model)
    attended = low(low_back(attended))
    branch = low_back(jnp.dot(attended, out_w, precision=highest) + shifts[0])
    normed = norm_apply(inputs + branch, gains[0], shifts[1])
    hidden_units = low_back(jnp.dot(low(normed), up_w, precision=highest) + up_b)
    active = low(jax.nn.gelu(hidden_units, approximate=False))
    second = low_back(jnp.dot(active, down_w, precision=highest) + shifts[2])
    return norm_apply(normed + second, gains[1], shifts[3])

def reference(hidden, cotangent, pair_lengths, query_lengths, buckets, qkv_weight, qv_bias, out_weight, up_weight, ffn_bias, down_weight, norm_gains, vectors, bias_table):
    params = (qkv_weight.astype(jnp.float32), qv_bias.astype(jnp.float32), out_weight.astype(jnp.float32), up_weight.astype(jnp.float32), ffn_bias.astype(jnp.float32), down_weight.astype(jnp.float32), norm_gains.astype(jnp.float32), vectors.astype(jnp.float32), bias_table.astype(jnp.float32))
    inputs = hidden.astype(jnp.float32)

    def whole(params, inputs):

        def one_pair(tokens, pair_len, query_len):
            middle = layer(params, 0, tokens, buckets, pair_len, query_len)
            return layer(params, 1, middle, buckets, pair_len, query_len)
        stored_pair = jax.checkpoint(one_pair)

        def step(carry, item):
            return (carry, stored_pair(item[0], item[1], item[2]))
        _, outputs = lax.scan(step, jnp.zeros((), jnp.float32), (inputs, pair_lengths, query_lengths))
        return outputs
    outputs, pullback = jax.vjp(whole, params, inputs)
    grads, grad_inputs = pullback(cotangent.astype(jnp.float32))
    edges = jnp.stack([grad_inputs, outputs])
    return (edges, grads[0], grads[1], grads[2], grads[3], grads[4], grads[5], grads[6], grads[7], grads[8])
```

```python
import functools

import jax
import jax.numpy as jnp
from jax import lax
from jax.experimental import pallas as pl
from jax.experimental.pallas import tpu as pltpu
from jax.sharding import PartitionSpec as P


f32 = jnp.float32
bf16 = jnp.bfloat16
EPS = 1e-05
HEAD = 64
NEG = -1e30
SWAP_Y = [(0, 2), (2, 0), (1, 3), (3, 1)]
SWAP_C = [(0, 1), (1, 0), (2, 3), (3, 2)]
NT = (((1,), (1,)), ((), ()))
TN = (((0,), (0,)), ((), ()))
NN = (((1,), (0,)), ((), ()))
KEY_BASE = (0, 512, 256, 768)
TILE_BASE = (0, 128, 512, 640)
STRIP = 1664
SPAN = STRIP + 128
MIB = 2**20


def cost(us, flops=0):
    return pl.CostEstimate(flops=flops, bytes_accessed=int(us * 3.4e6), transcendentals=0)


def dotf(a, b, dims=NN):
    return lax.dot_general(a, b, dims, preferred_element_type=f32)


def swap_y(value):
    return lax.ppermute(value, "tensor", SWAP_Y)


def swap_c(value):
    return lax.ppermute(value, "tensor", SWAP_C)


def make_strip(window_ref, h, kind, strip_ref):
    blocks = STRIP // 128
    lane = lax.broadcasted_iota(jnp.int32, (8, 128), 1)
    row = lax.broadcasted_iota(jnp.int32, (8, 128), 0)

    def rolled(first):
        seg = window_ref[0, h, kind : kind + 1, first : first + 128]
        seg = pltpu.roll(jnp.broadcast_to(seg, (8, 128)), 0, 1, stride=1, stride_axis=0)
        return [pltpu.roll(seg, 8 * q, 1) if q else seg for q in range(16)]

    high = rolled(128 * blocks)
    for a in range(blocks):
        low = rolled(128 * (blocks - 1 - a))
        for q in range(16):
            rows = slice(128 * a + 8 * q, 128 * a + 8 * q + 8)
            strip_ref[h, kind, rows, :] = jnp.where(lane >= row + 8 * q, high[q], low[q])
        high = low


def sum_strip(strip_ref, h, kind, held_ref):
    blocks = STRIP // 128
    lane = lax.broadcasted_iota(jnp.int32, (8, 128), 1)
    carry = jnp.zeros((8, 128), f32)
    for a in reversed(range(blocks)):
        low, high = jnp.zeros((8, 128), f32), jnp.zeros((8, 128), f32)
        for q in range(16):
            part = strip_ref[h, kind, 128 * a + 8 * q : 128 * a + 8 * q + 8, :]
            if q:
                part = pltpu.roll(part, 128 - 8 * q, 1)
            stays = lane < 128 - 8 * q
            high += jnp.where(stays, part, 0.0)
            low += jnp.where(stays, 0.0, part)
        first = 128 * (blocks - 1 - a)
        held_ref[0, h, kind, :, first : first + 128] = low + carry
        carry = high
    held_ref[0, h, kind, :, 128 * blocks : 128 * blocks + 128] = carry


def lane_mask(rows, which):
    lane = lax.broadcasted_iota(jnp.int32, (rows, 128), 1)
    return (lane < HEAD) if which == 0 else (lane >= HEAD)


def cross_mask(qlen, core, tile, kb):
    key_low = KEY_BASE[kb] == 0
    row_low = tile < 2
    if not key_low and not row_low:
        return None
    shape = (256, 128)
    if row_low:
        first = 256 * core + 128 * tile
        row_side = first + lax.broadcasted_iota(jnp.int32, shape, 1) < qlen
    if key_low:
        key_side = lax.broadcasted_iota(jnp.int32, shape, 0) < qlen
    if row_low and key_low:
        return row_side != key_side
    return row_side if row_low else key_side


def strip_rows(tile, kb):
    first = KEY_BASE[kb] - TILE_BASE[tile] + 640
    return slice(first, first + 256)


def score_block(info_ref, keys, query, strip_ref, h, ib, kb):
    qlen, core, plen = info_ref[0], info_ref[1], info_ref[2]
    raw = dotf(keys, query, NT)
    parts = []
    for u in (0, 1):
        tile = 2 * ib + u
        rows = strip_rows(tile, kb)
        bias = strip_ref[h, 0, rows, :]
        cross = cross_mask(qlen, core, tile, kb)
        if cross is not None:
            bias = jnp.where(cross, strip_ref[h, 1, rows, :], bias)
        parts.append(raw[:, 128 * u : 128 * u + 128] + bias)
    scores = jnp.concatenate(parts, 1)
    if kb != 0:
        live = KEY_BASE[kb] + lax.broadcasted_iota(jnp.int32, (256, 256), 0) < plen
        scores = jnp.where(live, scores, NEG)
    return scores


def whole(core, own, other):
    return jnp.concatenate([jnp.where(core == 0, own, other), jnp.where(core == 0, other, own)], 0)


def forward_kernel(
    info_ref, q_ref, k_ref, v_ref, ko_ref, vo_ref, win_ref, o_ref, lse_ref, strip_ref
):
    core = info_ref[1]
    for h in range(2):
        for kind in range(2):
            make_strip(win_ref, h, kind, strip_ref)
    keys = whole(core, k_ref[...], ko_ref[...])
    values = whole(core, v_ref[...], vo_ref[...])
    one = jnp.ones_like(values)
    turned = [jnp.where(lane_mask(1024, h), values, one).T for h in range(2)]
    for ib in range(2):
        rows = slice(256 * ib, 256 * ib + 256)
        query = q_ref[rows, :] * jnp.asarray(0.125, bf16)
        outs = []
        for h in range(2):
            one = jnp.where(lane_mask(256, h), query, jnp.zeros_like(query))
            blocks = [
                score_block(
                    info_ref, keys[256 * kb : 256 * kb + 256], one, strip_ref, h, ib, kb
                )
                for kb in range(4)
            ]
            top = functools.reduce(
                jnp.maximum, [jnp.max(s, 0, keepdims=True) for s in blocks]
            )
            mixed = None
            for kb in range(4):
                probs = jnp.exp(blocks[kb] - top).astype(bf16)
                part = dotf(turned[h][:, 256 * kb : 256 * kb + 256], probs)
                mixed = part if mixed is None else mixed + part
            total = mixed[HEAD * (1 - h) : HEAD * (1 - h) + 1, :]
            lse_ref[0, h : h + 1, rows] = top + jnp.log(total)
            outs.append(mixed[HEAD * h : HEAD * h + HEAD, :] / total)
        o_ref[rows, :] = jnp.concatenate(outs, 0).T.astype(bf16)


def kv_blocks(groups, first=0):
    half = groups // 2
    return [
        pl.BlockSpec((512, 128), lambda i, s: (0, i + first)),
        pl.BlockSpec((512, 128), lambda i, s: (0, i + first + groups)),
        pl.BlockSpec((512, 128), lambda i, s: (0, (i + first + half) % groups)),
        pl.BlockSpec((512, 128), lambda i, s: (0, (i + first + half) % groups + groups)),
    ]


def attend_forward(info, q, kv, kv_other, window):
    groups = q.shape[1] // 128
    block = pl.BlockSpec((512, 128), lambda i, s: (0, i))
    return pl.pallas_call(
        forward_kernel,
        grid_spec=pltpu.PrefetchScalarGridSpec(
            num_scalar_prefetch=1,
            grid=(groups,),
            in_specs=[
                block,
                *kv_blocks(groups),
                pl.BlockSpec((1, 2, 2, SPAN), lambda i, s: (i, 0, 0, 0)),
            ],
            out_specs=[block, pl.BlockSpec((1, 2, 512), lambda i, s: (i, 0, 0))],
            scratch_shapes=[pltpu.VMEM((2, 2, STRIP, 128), f32)],
        ),
        out_shape=[
            jax.ShapeDtypeStruct((512, 128 * groups), bf16),
            jax.ShapeDtypeStruct((groups, 2, 512), f32),
        ],
        compiler_params=pltpu.CompilerParams(vmem_limit_bytes=40 * MIB),
        cost_estimate=cost(17),
        name="attend_forward",
    )(info, q, kv, kv, kv_other, kv_other, window)


def backward_kernel(with_table, *refs):
    info_ref, q_ref, k_ref, v_ref, ko_ref, vo_ref, do_ref, lse_ref, win_ref = refs[:9]
    dq_ref, dk_ref, dv_ref, dko_ref, dvo_ref, *rest = refs[9:]
    qlen, core = info_ref[0], info_ref[1]
    strip_ref = rest[-1]
    for h in range(2):
        for kind in range(2):
            make_strip(win_ref, h, kind, strip_ref)
    if with_table:
        held_ref, strip_grad_ref = rest[:2]
        strip_grad_ref[...] = jnp.zeros_like(strip_grad_ref)
    keys = whole(core, k_ref[...], ko_ref[...])
    values = whole(core, v_ref[...], vo_ref[...])
    keys_turned = keys.T
    key_grads = [jnp.zeros((256, 128), f32) for _ in range(4)]
    value_grads = [jnp.zeros((256, 128), f32) for _ in range(4)]
    for ib in range(2):
        rows = slice(256 * ib, 256 * ib + 256)
        query = q_ref[rows, :] * jnp.asarray(0.125, bf16)
        grad = do_ref[rows, :]
        query_grads = []
        for h in range(2):
            mask = lane_mask(256, h)
            one = jnp.where(mask, query, jnp.zeros_like(query))
            grad_one = jnp.where(mask, grad, jnp.zeros_like(grad))
            log_total = lse_ref[0, h : h + 1, rows]
            probs, terms = [], []
            row_term = 0.0
            for kb in range(4):
                kr = slice(256 * kb, 256 * kb + 256)
                scores = score_block(info_ref, keys[kr], one, strip_ref, h, ib, kb)
                part = jnp.exp(scores - log_total)
                term = part * dotf(values[kr], grad_one, NT)
                row_term = row_term + jnp.sum(term, 0, keepdims=True)
                value_grads[kb] = value_grads[kb] + dotf(part.astype(bf16), grad_one)
                probs.append(part)
                terms.append(term)
            flat = None
            for kb in range(4):
                kr = slice(256 * kb, 256 * kb + 256)
                grad_scores = (terms[kb] - probs[kb] * row_term).astype(bf16)
                key_grads[kb] = key_grads[kb] + dotf(grad_scores, one)
                part = dotf(keys_turned[:, kr], grad_scores)
                flat = part if flat is None else flat + part
                if with_table:
                    for u in (0, 1):
                        tile = 2 * ib + u
                        where = strip_rows(tile, kb)
                        part = grad_scores[:, 128 * u : 128 * u + 128].astype(f32)
                        strip_grad_ref[h, 0, where, :] += part
                        cross = cross_mask(qlen, core, tile, kb)
                        if cross is not None:
                            strip_grad_ref[h, 1, where, :] += jnp.where(cross, part, 0.0)
            query_grads.append(flat[HEAD * h : HEAD * h + HEAD, :])
        dq_ref[rows, :] = (jnp.concatenate(query_grads, 0).T * 0.125).astype(bf16)
    for grads, own_ref, other_ref in (
        (key_grads, dk_ref, dko_ref),
        (value_grads, dv_ref, dvo_ref),
    ):
        first = jnp.concatenate(grads[:2], 0)
        second = jnp.concatenate(grads[2:], 0)
        own_ref[...] = jnp.where(core == 0, first, second)
        other_ref[...] = jnp.where(core == 0, second, first).astype(bf16)
    if with_table:
        for h in range(2):
            for kind in range(2):
                sum_strip(strip_grad_ref, h, kind, held_ref)


def attend_backward(info, q, kv, kv_other, grad, lse, window, with_table, first, count):
    groups = q.shape[1] // 128
    block = pl.BlockSpec((512, 128), lambda i, s: (0, i + first))
    rows = lambda kind: jax.ShapeDtypeStruct((512, 128 * count), kind)
    out_specs = [pl.BlockSpec((512, 128), lambda i, s: (0, i))] * 5
    out_shape = [rows(bf16), rows(f32), rows(f32), rows(bf16), rows(bf16)]
    scratch = [pltpu.VMEM((2, 2, STRIP, 128), f32)]
    if with_table:
        out_specs.append(pl.BlockSpec((1, 2, 2, 8, SPAN), lambda i, s: (i, 0, 0, 0, 0)))
        out_shape.append(jax.ShapeDtypeStruct((count, 2, 2, 8, SPAN), f32))
        scratch = scratch * 2
    return pl.pallas_call(
        functools.partial(backward_kernel, with_table),
        grid_spec=pltpu.PrefetchScalarGridSpec(
            num_scalar_prefetch=1,
            grid=(count,),
            in_specs=[
                block,
                *kv_blocks(groups, first),
                block,
                pl.BlockSpec((1, 2, 512), lambda i, s: (i + first, 0, 0)),
                pl.BlockSpec((1, 2, 2, SPAN), lambda i, s: (i + first, 0, 0, 0)),
            ],
            out_specs=out_specs,
            scratch_shapes=scratch,
        ),
        out_shape=out_shape,
        compiler_params=pltpu.CompilerParams(vmem_limit_bytes=48 * MIB),
        cost_estimate=cost(30),
        name="attend_backward",
    )(info, q, kv, kv, kv_other, kv_other, grad, lse, window)


def norm_parts(values):
    centre = jnp.mean(values, -1, keepdims=True)
    centred = values - centre
    scale = lax.rsqrt(jnp.mean(centred * centred, -1, keepdims=True) + EPS)
    return centred * scale, scale


def norm_back(grad, gain, normal, scale):
    scaled = grad * gain
    return scale * (
        scaled
        - jnp.mean(scaled, -1, keepdims=True)
        - normal * jnp.mean(scaled * normal, -1, keepdims=True)
    )


def normal_cdf(units):
    size = jnp.abs(units)
    t = 1.0 / (1.0 + (0.3275911 * 0.5**0.5) * size)
    bell = jnp.exp(-0.5 * units * units)
    poly = 0.5 * 1.061405429
    for coef in (-1.453152027, 1.421413741, -0.284496736, 0.254829592):
        poly = poly * t + 0.5 * coef
    tail = poly * t * bell
    return jnp.where(units >= 0, 1.0 - tail, tail), bell


def ffn_forward_kernel(
    keep,
    att_ref,
    x_ref,
    out_ref,
    up_ref,
    up_far_ref,
    down_ref,
    down_far_ref,
    bias_ref,
    gain_ref,
    shift_ref,
    result_ref,
    *rest,
):
    if keep:
        (
            low_ref,
            active_ref,
            slope_ref,
            n_one_ref,
            s_one_ref,
            n_two_ref,
            s_two_ref,
            normed_low,
            total,
        ) = rest
    else:
        normed_low, total = rest
    i = pl.program_id(0)

    @pl.when(i == 0)
    def _():
        before = x_ref[...].astype(f32) + (dotf(att_ref[...], out_ref[...]) + shift_ref[0:1, :])
        normal, scale = norm_parts(before)
        normed = normal * gain_ref[0:1, :] + shift_ref[1:2, :]
        normed_low[...] = normed.astype(bf16)
        total[...] = normed + shift_ref[2:3, :]
        if keep:
            n_one_ref[...] = normal
            s_one_ref[...] = scale
            low_ref[...] = normed_low[...]

    near = i < 2
    width = up_ref.shape[2]
    step = 256
    add = None
    for first in range(0, width, step):
        cols = slice(first, first + step)
        up = jnp.where(near, up_ref[0, :, cols], up_far_ref[0, :, cols])
        down = jnp.where(near, down_ref[0, cols, :], down_far_ref[0, cols, :])
        units = dotf(normed_low[...], up) + bias_ref[0, :, cols]
        side, bell = normal_cdf(units)
        active = (units * side).astype(bf16)
        if keep:
            active_ref[:, cols] = active
            slope_ref[:, cols] = (side + units * bell * 0.3989422804014327).astype(bf16)
        part = dotf(active, down)
        add = part if add is None else add + part
    total[...] += add

    @pl.when(i == pl.num_programs(0) - 1)
    def _():
        normal, scale = norm_parts(total[...])
        result = normal * gain_ref[1:2, :] + shift_ref[3:4, :]
        result_ref[...] = result.astype(result_ref.dtype)
        if keep:
            n_two_ref[...] = normal
            s_two_ref[...] = scale


def near_far(rows, cols):
    return [
        pl.BlockSpec((1, rows, cols), lambda i: (jnp.minimum(i, 1), 0, 0)),
        pl.BlockSpec((1, rows, cols), lambda i: (jnp.maximum(i - 2, 0), 0, 0)),
    ]


def ffn_forward(w, attended, inputs, keep, part=0, parts=1):
    rows, model = inputs.shape
    rows //= parts
    width = w["up"][0].shape[2]
    all_of = lambda *shape: pl.BlockSpec(shape, lambda i: (0,) * len(shape))
    by_step = pl.BlockSpec((rows, width), lambda i: (0, i))
    shape = lambda cols, kind: jax.ShapeDtypeStruct((rows, cols), kind)
    out_specs = [all_of(rows, model)]
    out_shape = [shape(model, f32 if keep else bf16)]
    if keep:
        out_specs += [all_of(rows, model), by_step, by_step]
        out_specs += [all_of(rows, model), all_of(rows, 1)] * 2
        out_shape += [shape(model, bf16), shape(4 * width, bf16), shape(4 * width, bf16)]
        out_shape += [shape(model, f32), shape(1, f32)] * 2
    flops = 2 * rows * model * (model + 8 * width)
    return pl.pallas_call(
        functools.partial(ffn_forward_kernel, keep),
        grid=(4,),
        in_specs=[
            pl.BlockSpec((rows, model), lambda i: (part, 0)),
            pl.BlockSpec((rows, model), lambda i: (part, 0)),
            all_of(model, model),
            *near_far(model, width),
            *near_far(width, model),
            pl.BlockSpec((1, 1, width), lambda i: (i, 0, 0)),
            all_of(2, model),
            all_of(4, model),
        ],
        out_specs=out_specs,
        out_shape=out_shape,
        scratch_shapes=[pltpu.VMEM((rows, model), bf16), pltpu.VMEM((rows, model), f32)],
        compiler_params=pltpu.CompilerParams(vmem_limit_bytes=48 * MIB),
        cost_estimate=cost(15),
        name="ffn_forward",
    )(
        attended,
        inputs,
        w["out"],
        *w["up"],
        *w["down"],
        w["up_bias"],
        w["gains"],
        w["shifts"],
    )


def top_back_kernel(gy_ref, n_two_ref, s_two_ref, gain_ref, after_ref, second_ref, sums_ref):
    gy = gy_ref[...].astype(f32)
    after = norm_back(gy, gain_ref[1:2, :], n_two_ref[...], s_two_ref[...])
    low = after.astype(bf16)
    after_ref[...] = after
    second_ref[...] = low
    sums_ref[0:1, :] = jnp.sum(gy * n_two_ref[...], 0, keepdims=True)
    sums_ref[1:2, :] = jnp.sum(low.astype(f32), 0, keepdims=True)
    sums_ref[2:3, :] = jnp.sum(gy, 0, keepdims=True)
    sums_ref[3:8, :] = jnp.zeros((5, sums_ref.shape[1]), f32)


def top_back(w, saved, grad_y):
    rows, model = grad_y.shape
    return pl.pallas_call(
        top_back_kernel,
        out_shape=[
            jax.ShapeDtypeStruct((rows, model), f32),
            jax.ShapeDtypeStruct((rows, model), bf16),
            jax.ShapeDtypeStruct((8, model), f32),
        ],
        compiler_params=pltpu.CompilerParams(vmem_limit_bytes=20 * MIB),
        cost_estimate=cost(2),
        name="top_back",
    )(grad_y, saved["n_two"], saved["s_two"], w["gains"])


def ffn_backward_kernel(deps, *refs):
    (
        after_ref,
        second_ref,
        slope_ref,
        n_one_ref,
        s_one_ref,
        out_ref,
        up_ref,
        up_far_ref,
        down_ref,
        down_far_ref,
        gain_ref,
    ) = refs[:11]
    hidden_ref, before_ref, branch_ref, att_ref, sums_ref, hidden_sums_ref, total = refs[11 + deps :]
    i = pl.program_id(0)

    def add_up(value):
        return jnp.sum(value, 0, keepdims=True)

    @pl.when(i == 0)
    def _():
        total[...] = after_ref[...]

    near = i < 2
    width = up_ref.shape[2]
    step = 256
    add = None
    for first in range(0, width, step):
        cols = slice(first, first + step)
        up = jnp.where(near, up_ref[0, :, cols], up_far_ref[0, :, cols])
        down = jnp.where(near, down_ref[0, cols, :], down_far_ref[0, cols, :])
        active = dotf(second_ref[...], down, NT)
        hidden = (active * slope_ref[:, cols].astype(f32)).astype(bf16)
        hidden_ref[:, cols] = hidden
        hidden_sums_ref[0, :, cols] = add_up(hidden.astype(f32))
        part = dotf(hidden, up, NT)
        add = part if add is None else add + part
    total[...] += add

    @pl.when(i == pl.num_programs(0) - 1)
    def _():
        normed = total[...]
        before = norm_back(normed, gain_ref[0:1, :], n_one_ref[...], s_one_ref[...])
        low = before.astype(bf16)
        before_ref[...] = before
        branch_ref[...] = low
        att_ref[...] = dotf(low, out_ref[...], NT).astype(bf16)
        sums_ref[0:1, :] = add_up(normed * n_one_ref[...])
        sums_ref[1:2, :] = add_up(low.astype(f32))
        sums_ref[2:3, :] = add_up(normed)
        sums_ref[3:8, :] = jnp.zeros((5, sums_ref.shape[1]), f32)


def ffn_backward(w, saved, after, second, deps=()):
    rows, model = after.shape
    width = w["up"][0].shape[2]
    all_of = lambda *shape: pl.BlockSpec(shape, lambda i: (0,) * len(shape))
    by_step = pl.BlockSpec((rows, width), lambda i: (0, i))
    by_block = pl.BlockSpec((1, 1, width), lambda i: (i, 0, 0))
    shape = lambda cols, kind: jax.ShapeDtypeStruct((rows, cols), kind)
    whole_rows = all_of(rows, model)
    return pl.pallas_call(
        functools.partial(ffn_backward_kernel, len(deps)),
        grid=(4,),
        in_specs=[
            whole_rows,
            whole_rows,
            by_step,
            whole_rows,
            all_of(rows, 1),
            all_of(model, model),
            *near_far(model, width),
            *near_far(width, model),
            all_of(2, model),
            *[pl.BlockSpec(memory_space=pl.ANY)] * len(deps),
        ],
        out_specs=[by_step, whole_rows, whole_rows, whole_rows, all_of(8, model), by_block],
        out_shape=[
            shape(4 * width, bf16),
            shape(model, f32),
            shape(model, bf16),
            shape(model, bf16),
            jax.ShapeDtypeStruct((8, model), f32),
            jax.ShapeDtypeStruct((4, 1, width), f32),
        ],
        scratch_shapes=[pltpu.VMEM((rows, model), f32)],
        compiler_params=pltpu.CompilerParams(vmem_limit_bytes=48 * MIB),
        cost_estimate=cost(15),
        name="ffn_backward",
    )(
        after,
        second,
        saved["slope"],
        saved["n_one"],
        saved["s_one"],
        w["out"],
        *w["up"],
        *w["down"],
        w["gains"],
        *deps,
    )


def weight_grad_kernel(l_ref, lo_ref, r_ref, ro_ref, o_ref):
    total = dotf(l_ref[...], r_ref[...], TN) + dotf(lo_ref[...], ro_ref[...], TN)
    o_ref[...] = total.astype(o_ref.dtype)


def weight_grad(left, left_far, right, right_far, kind, left_cols, right_cols):
    rows = left.shape[0]
    lf, ln, lw = left_cols
    rf, rn, rw = right_cols
    return pl.pallas_call(
        weight_grad_kernel,
        grid=(rn, ln),
        in_specs=[
            pl.BlockSpec((rows, lw), lambda j, i: (0, lf + i)),
            pl.BlockSpec((rows, lw), lambda j, i: (0, lf + i)),
            pl.BlockSpec((rows, rw), lambda j, i: (0, rf + j)),
            pl.BlockSpec((rows, rw), lambda j, i: (0, rf + j)),
        ],
        out_specs=pl.BlockSpec((lw, rw), lambda j, i: (i, j)),
        out_shape=jax.ShapeDtypeStruct((ln * lw, rn * rw), kind),
        compiler_params=pltpu.CompilerParams(vmem_limit_bytes=40 * MIB),
        cost_estimate=cost(4),
        name="weight_grad",
    )(left, left_far, right, right_far)


def split_grad_kernel(l_ref, lo_ref, r_ref, ro_ref, kept_ref, sent_ref):
    total = dotf(l_ref[...], r_ref[...], TN) + dotf(lo_ref[...], ro_ref[...], TN)
    half = total.shape[0] // 2
    kept_ref[...] = total[:half]
    sent_ref[...] = total[half:].astype(bf16)


def split_grad(left, left_far, right, right_far, width):
    rows, model = right.shape
    count = left_far.shape[1] // width
    left_block = pl.BlockSpec((rows, width), lambda i: (0, i))
    right_block = pl.BlockSpec((rows, model), lambda i: (0, 0))
    made = pl.BlockSpec((width // 2, model), lambda i: (i, 0))
    shape = (count * width // 2, model)
    return pl.pallas_call(
        split_grad_kernel,
        grid=(count,),
        in_specs=[left_block, left_block, right_block, right_block],
        out_specs=[made, made],
        out_shape=[jax.ShapeDtypeStruct(shape, f32), jax.ShapeDtypeStruct(shape, bf16)],
        compiler_params=pltpu.CompilerParams(vmem_limit_bytes=40 * MIB),
        cost_estimate=cost(4),
        name="split_grad",
    )(left, left_far, right, right_far)


def input_back_kernel(
    q_ref,
    k_ref,
    k_came_ref,
    v_ref,
    v_came_ref,
    before_ref,
    w_ref,
    near_ref,
    far_ref,
    grad_ref,
    low_ref,
    sums_ref,
    mixed,
    total,
):
    i = pl.program_id(0)
    which = i // 2

    @pl.when(i == 0)
    def _():
        total[...] = before_ref[...]

    @pl.when(which == 0)
    def _():
        mixed[...] = q_ref[...]

    @pl.when(which == 1)
    def _():
        mixed[...] = (k_ref[...] + k_came_ref[...].astype(f32)).astype(bf16)

    @pl.when(which == 2)
    def _():
        mixed[...] = (v_ref[...] + v_came_ref[...].astype(f32)).astype(bf16)

    @pl.when(i % 2 == 0)
    def _():
        near_ref[...] = mixed[...]

    @pl.when(i % 2 == 1)
    def _():
        far_ref[...] = mixed[...]

    sums_ref[0] = jnp.sum(mixed[...].astype(f32), 0, keepdims=True)
    total[...] += dotf(mixed[...], w_ref[...])

    @pl.when(i == 5)
    def _():
        grad_ref[...] = total[...]
        low_ref[...] = total[...].astype(bf16)


def input_back(grads, came, before, qkv, part=0, parts=1):
    q, k, v = grads
    k_came, v_came = came
    rows, model = q.shape
    rows //= parts
    half = model // 2

    def at(first, turn=False):
        def index(i):
            step = jnp.clip(i - first, 0, 1)
            return part, (1 - step if turn else step)

        return pl.BlockSpec((rows, half), index)

    split = pl.BlockSpec((rows, half), lambda i: (0, i // 2))
    full = pl.BlockSpec((rows, model), lambda i: (0, 0))
    return pl.pallas_call(
        input_back_kernel,
        grid=(6,),
        in_specs=[
            at(0),
            at(2),
            at(2, True),
            at(4),
            at(4, True),
            pl.BlockSpec((rows, model), lambda i: (part, 0)),
            pl.BlockSpec((half, model), lambda i: (i, 0)),
        ],
        out_specs=[split, split, full, full, pl.BlockSpec((1, 1, half), lambda i: (i, 0, 0))],
        out_shape=[
            jax.ShapeDtypeStruct((rows, 3 * half), bf16),
            jax.ShapeDtypeStruct((rows, 3 * half), bf16),
            jax.ShapeDtypeStruct((rows, model), f32),
            jax.ShapeDtypeStruct((rows, model), bf16),
            jax.ShapeDtypeStruct((6, 1, half), f32),
        ],
        scratch_shapes=[pltpu.VMEM((rows, half), bf16), pltpu.VMEM((rows, model), f32)],
        compiler_params=pltpu.CompilerParams(vmem_limit_bytes=40 * MIB),
        cost_estimate=cost(6),
        name="input_back",
    )(q, k, k_came, v, v_came, before, qkv)


def body(
    hidden,
    cotangent,
    pair_lengths,
    query_lengths,
    buckets,
    qkv_weight,
    qv_bias,
    out_weight,
    up_weight,
    ffn_bias,
    down_weight,
    norm_gains,
    vectors,
    bias_table,
):
    leading = lax.axis_index("section") == 0
    place = lax.axis_index("tensor")
    y, core = place // 2, place % 2
    plane = lax.axis_index("dp")
    planes = lax.axis_size("dp")
    odd = plane % 2
    local, model = hidden.shape[1], hidden.shape[2]
    total = 4 * local
    cols = qkv_weight.shape[3]
    width = up_weight.shape[2]
    heads = bias_table.shape[1]
    kinds = bias_table.shape[2] // 2
    near, far = slice(0, 2 * cols), slice(2 * cols, 4 * cols)

    def swap_z(value):
        return lax.ppermute(value, "dp", [(i, i ^ 1) for i in range(planes)])

    def mine(array):
        return lax.dynamic_index_in_dim(array, y, 0, keepdims=False)

    def theirs(array):
        return lax.dynamic_index_in_dim(array, 1 - y, 0, keepdims=False)

    def in_order(first, own, came, axis=0):
        return jnp.concatenate(
            [jnp.where(first, own, came), jnp.where(first, came, own)], axis
        )

    def own_half(block, axis=0):
        half = block.shape[axis] // 2
        return lax.dynamic_slice_in_dim(block, half * odd, half, axis)

    def edge_blocks(value):
        return value.reshape(2, local, model)

    def stage(work):
        shapes = jax.eval_shape(work)
        return lax.cond(
            pair_lengths[0] > 0,
            work,
            lambda: jax.tree.map(lambda leaf: jnp.zeros(leaf.shape, leaf.dtype), shapes),
        )

    qkv_own = qkv_weight[0].transpose(1, 2, 0)
    out_own, up_own, down_own = out_weight[0], up_weight[0], down_weight[0]
    x_sent, qkv_sent = theirs(hidden), own_half(qkv_own, 1)
    small = jnp.concatenate([qv_bias[0].reshape(-1), ffn_bias[0], bias_table[0].reshape(-1)])

    def first_stage():
        return (
            swap_y(x_sent),
            swap_y(small),
            swap_y(qkv_sent),
            own_half(out_own),
            own_half(up_own),
            own_half(down_own),
        )

    x_came, small_y, qkv_y, out_sent, up_sent, down_sent = stage(first_stage)
    onehot = (buckets[:, None] == jnp.arange(kinds, dtype=jnp.int32)[None, :]).astype(f32)
    onehot = jnp.pad(onehot, ((1, 0), (0, 0)))
    onehot = lax.dynamic_slice_in_dim(onehot, 256 * core, SPAN, 0)

    def second_stage():
        two = jnp.stack([small, small_y])
        four = jnp.concatenate([two, swap_c(two)])
        table = four[:, 2 * cols + width :].reshape(8 * heads, kinds)
        window = lax.dot_general(table, onehot, NT, precision=lax.Precision.HIGHEST)
        window = window.reshape(2 * heads, 2, 2, SPAN)
        return swap_y(out_sent), swap_y(up_sent), swap_z(qkv_y), four, window

    out_y, up_y, qkv_z, small, window = stage(second_stage)
    qv_all = small[:, : 2 * cols].reshape(4, 2, cols)
    q_bias = qv_all[:, 0].reshape(-1)
    kv_bias = jnp.concatenate([jnp.zeros((model,), f32), qv_all[:, 1].reshape(-1)])
    info = jnp.stack([mine(query_lengths), core, mine(pair_lengths)]).astype(jnp.int32)
    w = dict(
        up_bias=small[:, 2 * cols : 2 * cols + width].reshape(4, 1, width),
        gains=norm_gains[0],
        shifts=vectors[0],
    )

    def project(inputs, qkv):
        mixed = dotf(inputs, qkv, NT)
        kv = (mixed[:, model:] + kv_bias).astype(bf16)
        return (mixed[:, :model] + q_bias).astype(bf16), kv

    def third_stage():
        x0 = in_order(y == 0, mine(hidden), x_came)
        qkv = jnp.concatenate([qkv_own, in_order(odd == 0, qkv_y, qkv_z, 1)], 1)
        qkv = jnp.concatenate([qkv, swap_c(qkv)], 1).reshape(3 * model, model)
        q, kv = project(x0, qkv)
        kv_other = swap_c(kv)
        attended, _ = attend_forward(info, q, kv, kv_other, window)
        return x0, qkv, attended, swap_z(out_y), swap_z(up_y), swap_y(down_sent)

    x0, qkv, attended, out_z, up_z, down_y = stage(third_stage)

    def fourth_stage():
        out = jnp.concatenate([out_own, in_order(odd == 0, out_y, out_z)], 0)
        up = jnp.stack([up_own, in_order(odd == 0, up_y, up_z)])
        return jnp.concatenate([out, swap_c(out)], 0), up, swap_c(up), swap_z(down_y)

    w["out"], up, up_far, down_z = stage(fourth_stage)
    w["up"] = up, up_far

    def fifth_stage():
        down = jnp.stack([down_own, in_order(odd == 0, down_y, down_z)])
        return down, swap_c(down)

    w["down"] = stage(fifth_stage)

    def to_next(value):
        return lax.ppermute(value, "section", [(0, 1)])

    def to_last(value):
        return lax.ppermute(value, "section", [(1, 0)])

    middle = ffn_forward(w, attended, x0, False, 0, 2)[0]
    came_a, middle = stage(
        lambda: (to_next(middle), ffn_forward(w, attended, x0, False, 1, 2)[0])
    )
    x_a = jnp.where(leading, x0[:local], came_a)
    came_b, (q_a, kv_a) = stage(lambda: (to_next(middle), project(x_a, qkv)))

    def seventh_stage():
        x_b = jnp.where(leading, x0[local:], came_b)
        q_b, kv_b = project(x_b, qkv)
        kv = jnp.concatenate([kv_a, kv_b], 0)
        kv_other = swap_c(kv)
        x1, q = jnp.concatenate([x_a, x_b], 0), jnp.concatenate([q_a, q_b], 0)
        return x1, q, kv, kv_other

    x1, q, kv, kv_other = stage(seventh_stage)
    top_sent = theirs(cotangent)

    def eighth_stage():
        attended, lse = attend_forward(info, q, kv, kv_other, window)
        return swap_y(top_sent), swap_c(x1), attended, lse

    top_came, inputs_far, attended, lse = stage(eighth_stage)
    grad_top = in_order(y == 0, mine(cotangent), top_came)
    result, normed_low, active, slope, n_one, s_one, n_two, s_two = ffn_forward(
        w, attended, x1, True
    )
    saved = dict(slope=slope, n_one=n_one, s_one=s_one, n_two=n_two, s_two=s_two)

    def dense_back(after, second):
        names = ("hidden", "before", "branch", "attended", "low_sums", "hidden_sums")
        return dict(zip(names, ffn_backward(w, saved, after, second)))

    def attention_back(grads, table, first, count):
        return attend_backward(
            info, q, kv, kv_other, grads["attended"], lse, window, table, first, count
        )

    after, second, top_sums = top_back(w, saved, grad_top)

    def ninth_stage():
        return (
            swap_c(normed_low),
            swap_c(active[:, 2 * width :]),
            swap_c(attended[:, far]),
            dense_back(after, second),
        )

    normed_far, active_far, attended_far, grads = stage(ninth_stage)
    *qkv_grads, k_far, v_far = attention_back(grads, False, 0, 6)
    came = stage(lambda: (swap_c(k_far), swap_c(v_far)))

    def back(part, parts):
        return input_back(qkv_grads, came, grads["before"], qkv, part, parts)

    grad_a = back(0, 2)[3]
    came_a, grad_b = stage(lambda: (to_last(grad_a), back(1, 2)[3]))
    came_b = stage(lambda: to_last(grad_b))
    grad_y = jnp.where(leading, jnp.concatenate([came_a, came_b], 0), grad_top)

    thirds = width // 3

    def down_grad(kind, first):
        return weight_grad(
            active, active_far, second, second_far, kind, (first, 3, thirds), (0, 1, model)
        )

    def up_grad(kind, first):
        return weight_grad(
            normed_low, normed_far, hidden, hidden_far, kind, (0, 3, thirds), (first, 1, width)
        )

    def hops(value):
        if planes != 4:
            return lax.psum(value, "dp")
        value = value + lax.ppermute(value, "dp", [(0, 1), (3, 2)])
        value = value + lax.ppermute(value, "dp", [(1, 2), (2, 1)])
        back = lax.ppermute(value, "dp", [(1, 0), (2, 3)])
        return jnp.where((plane == 1) | (plane == 2), value, back)

    after, second, top_sums = top_back(w, saved, grad_y)
    second_far, grads = stage(lambda: (swap_c(second), dense_back(after, second)))
    hidden, branch = grads["hidden"], grads["branch"]

    def stage_2():
        return swap_c(hidden[:, 2 * width :]), swap_c(branch), down_grad(bf16, 3)

    hidden_far, branch_far, down_sent = stage(stage_2)
    up_sent = up_grad(bf16, 1)
    out_kept, out_sent = split_grad(attended, attended_far, branch, branch_far, 2 * cols)

    def stage_3():
        return (
            swap_y(down_sent),
            swap_y(up_sent),
            swap_y(out_sent),
            attention_back(grads, True, 0, 6),
            down_grad(f32, 0),
            up_grad(f32, 0),
        )

    *came, found, down_kept, up_kept = stage(stage_3)
    *qkv_grads, k_far, v_far, held = found
    kept = (down_kept, up_kept, out_kept)
    later = [(own + other.astype(f32)).astype(bf16) for own, other in zip(kept, came)]

    def stage_4():
        summed = lax.psum(later, "dp")
        near, far, grad_input, grad_low, qv_sums = input_back(
            qkv_grads, (swap_c(k_far), swap_c(v_far)), grads["before"], qkv
        )
        rest_kept, rest_sent = split_grad(near, swap_c(far), x1, inputs_far, 2 * cols)
        edge_low = edge_blocks(jnp.where(leading, grad_low, result.astype(bf16)))
        edge_came = swap_y(theirs(edge_low))
        parts = []
        for which in range(3):
            rows = slice(which * cols, which * cols + cols)
            rest = rest_kept[rows] + swap_y(rest_sent[rows]).astype(f32)
            parts.append(hops(rest.astype(bf16)))
        sums = token_sums(qv_sums)
        sums = sums[:2] + swap_c(sums[2:])
        sums = sums[0] + swap_y(sums[1])
        if planes == 4:
            sums = sums + swap_z(sums)
            sums = sums + lax.ppermute(sums, "dp", [(0, 2), (2, 0), (1, 3), (3, 1)])
        else:
            sums = lax.psum(sums, "dp")
        return summed, parts, sums, grad_input, edge_came

    share = model // 4

    def token_sums(qv_sums):
        wide = jnp.pad(held.reshape(4 * heads, 2, 8, SPAN), ((0, 0), (0, 0), (0, 0), (0, 8)))
        sums = sum(wide[:, :, s, s : s + SPAN] for s in range(8))
        sums = jnp.stack([sums[:, 0] - sums[:, 1], sums[:, 1]], 1).reshape(8 * heads, SPAN)
        grad_table = jnp.dot(sums, onehot, precision=lax.Precision.HIGHEST)
        grad_table = grad_table.reshape(4, heads * 2 * kinds)
        q_sums, _, v_sums = qv_sums.reshape(3, 4, cols)
        grad_ffn = grads["hidden_sums"].reshape(4, width)
        low_sums = grads["low_sums"]
        rows = [low_sums[0], top_sums[0], low_sums[1], low_sums[2], top_sums[1], top_sums[2]]
        by_share = jnp.stack(rows).reshape(6, 4, share)
        by_share = by_share.transpose(1, 0, 2).reshape(4, 6 * share)
        by_share = jnp.stack(
            [lax.dynamic_index_in_dim(by_share, place ^ flip, 0, False) for flip in (0, 2, 1, 3)]
        )
        return jnp.concatenate([grad_table, q_sums, v_sums, grad_ffn, by_share], 1)

    summed, parts, sums, grad_input, edge_came = stage(stage_4)
    grad_down, grad_up, grad_out = [value.astype(f32) for value in summed]
    grad_qkv = jnp.stack(parts).astype(f32)
    edge_own = mine(edge_blocks(jnp.where(leading, grad_input, result)))
    edge_came = edge_came.astype(f32)
    edges = jnp.stack([jnp.where(y == 0, edge_own, edge_came), jnp.where(y == 0, edge_came, edge_own)])
    grad_qkv = grad_qkv.reshape(1, 3, cols, model).transpose(0, 3, 1, 2)
    at = heads * 2 * kinds
    table_out = sums[:at].reshape(heads, 2 * kinds)
    qv_out = sums[at : at + 2 * cols].reshape(2, cols)
    ffn_out = sums[at + 2 * cols : at + 2 * cols + width]
    vec_out = sums[at + 2 * cols + width :].reshape(6, share)
    return (
        edges[None],
        grad_qkv,
        qv_out[None],
        grad_out[None],
        grad_up[None],
        ffn_out[None],
        grad_down[None],
        vec_out[:2][None],
        vec_out[2:][None],
        table_out[None],
    )


def solution(mesh):
    return jax.shard_map(
        body,
        mesh=mesh,
        in_specs=(
            P("dp", "tensor", None),
            P("dp", "tensor", None),
            P("dp"),
            P("dp"),
            P(),
            P("section", None, None, "tensor"),
            P("section", None, "tensor"),
            P("section", "tensor", None),
            P("section", None, "tensor"),
            P("section", "tensor"),
            P("section", "tensor", None),
            P("section", None, None),
            P("section", None, None),
            P("section", "tensor", None),
        ),
        out_specs=(
            P("section", "dp", "tensor", None),
            P("section", None, None, "tensor"),
            P("section", None, "tensor"),
            P("section", "tensor", None),
            P("section", None, "tensor"),
            P("section", "tensor"),
            P("section", "tensor", None),
            P("section", None, "tensor"),
            P("section", None, "tensor"),
            P("section", "tensor", None),
        ),
        check_vma=False,
    )
```

```python
import functools

import jax
import jax.numpy as jnp
from jax import lax
from jax.experimental import pallas as pl
from jax.experimental.pallas import tpu as pltpu
from jax.sharding import PartitionSpec as P


f32 = jnp.float32
bf16 = jnp.bfloat16
EPS = 1e-05
HEAD = 64
NEG = -1e30
SWAP_Y = [(0, 2), (2, 0), (1, 3), (3, 1)]
SWAP_C = [(0, 1), (1, 0), (2, 3), (3, 2)]
NT = (((1,), (1,)), ((), ()))
TN = (((0,), (0,)), ((), ()))
NN = (((1,), (0,)), ((), ()))
KEY_BASE = (0, 512, 256, 768)
TILE_BASE = (0, 128, 512, 640)
STRIP = 1664
SPAN = STRIP + 128
MIB = 2**20


def cost(us, flops=0):
    return pl.CostEstimate(flops=flops, bytes_accessed=int(us * 3.4e6), transcendentals=0)


def dotf(a, b, dims=NN):
    return lax.dot_general(a, b, dims, preferred_element_type=f32)


def swap_y(value):
    return lax.ppermute(value, "tensor", SWAP_Y)


def swap_c(value):
    return lax.ppermute(value, "tensor", SWAP_C)


def make_strip(window_ref, h, kind, strip_ref):
    blocks = STRIP // 128
    lane = lax.broadcasted_iota(jnp.int32, (8, 128), 1)
    row = lax.broadcasted_iota(jnp.int32, (8, 128), 0)

    def rolled(first):
        seg = window_ref[0, h, kind : kind + 1, first : first + 128]
        seg = pltpu.roll(jnp.broadcast_to(seg, (8, 128)), 0, 1, stride=1, stride_axis=0)
        return [pltpu.roll(seg, 8 * q, 1) if q else seg for q in range(16)]

    high = rolled(128 * blocks)
    for a in range(blocks):
        low = rolled(128 * (blocks - 1 - a))
        for q in range(16):
            rows = slice(128 * a + 8 * q, 128 * a + 8 * q + 8)
            strip_ref[h, kind, rows, :] = jnp.where(lane >= row + 8 * q, high[q], low[q])
        high = low


def sum_strip(strip_ref, h, kind, held_ref):
    blocks = STRIP // 128
    lane = lax.broadcasted_iota(jnp.int32, (8, 128), 1)
    carry = jnp.zeros((8, 128), f32)
    for a in reversed(range(blocks)):
        low, high = jnp.zeros((8, 128), f32), jnp.zeros((8, 128), f32)
        for q in range(16):
            part = strip_ref[h, kind, 128 * a + 8 * q : 128 * a + 8 * q + 8, :]
            if q:
                part = pltpu.roll(part, 128 - 8 * q, 1)
            stays = lane < 128 - 8 * q
            high += jnp.where(stays, part, 0.0)
            low += jnp.where(stays, 0.0, part)
        first = 128 * (blocks - 1 - a)
        held_ref[0, h, kind, :, first : first + 128] = low + carry
        carry = high
    held_ref[0, h, kind, :, 128 * blocks : 128 * blocks + 128] = carry


def lane_mask(rows, which):
    lane = lax.broadcasted_iota(jnp.int32, (rows, 128), 1)
    return (lane < HEAD) if which == 0 else (lane >= HEAD)


def cross_mask(qlen, core, tile, kb):
    key_low = KEY_BASE[kb] == 0
    row_low = tile < 2
    if not key_low and not row_low:
        return None
    shape = (256, 128)
    if row_low:
        first = 256 * core + 128 * tile
        row_side = first + lax.broadcasted_iota(jnp.int32, shape, 1) < qlen
    if key_low:
        key_side = lax.broadcasted_iota(jnp.int32, shape, 0) < qlen
    if row_low and key_low:
        return row_side != key_side
    return row_side if row_low else key_side


def strip_rows(tile, kb):
    first = KEY_BASE[kb] - TILE_BASE[tile] + 640
    return slice(first, first + 256)


def score_block(info_ref, keys, query, strip_ref, h, ib, kb):
    qlen, core, plen = info_ref[0], info_ref[1], info_ref[2]
    raw = dotf(keys, query, NT)
    parts = []
    for u in (0, 1):
        tile = 2 * ib + u
        rows = strip_rows(tile, kb)
        bias = strip_ref[h, 0, rows, :]
        cross = cross_mask(qlen, core, tile, kb)
        if cross is not None:
            bias = jnp.where(cross, strip_ref[h, 1, rows, :], bias)
        parts.append(raw[:, 128 * u : 128 * u + 128] + bias)
    scores = jnp.concatenate(parts, 1)
    if kb != 0:
        live = KEY_BASE[kb] + lax.broadcasted_iota(jnp.int32, (256, 256), 0) < plen
        scores = jnp.where(live, scores, NEG)
    return scores


def whole(core, own, other):
    return jnp.concatenate([jnp.where(core == 0, own, other), jnp.where(core == 0, other, own)], 0)


def forward_kernel(
    info_ref, q_ref, k_ref, v_ref, ko_ref, vo_ref, win_ref, o_ref, lse_ref, strip_ref
):
    core = info_ref[1]
    for h in range(2):
        for kind in range(2):
            make_strip(win_ref, h, kind, strip_ref)
    keys = whole(core, k_ref[...], ko_ref[...])
    values = whole(core, v_ref[...], vo_ref[...])
    one = jnp.ones_like(values)
    turned = [jnp.where(lane_mask(1024, h), values, one).T for h in range(2)]
    for ib in range(2):
        rows = slice(256 * ib, 256 * ib + 256)
        query = q_ref[rows, :] * jnp.asarray(0.125, bf16)
        outs = []
        for h in range(2):
            one = jnp.where(lane_mask(256, h), query, jnp.zeros_like(query))
            blocks = [
                score_block(
                    info_ref, keys[256 * kb : 256 * kb + 256], one, strip_ref, h, ib, kb
                )
                for kb in range(4)
            ]
            top = functools.reduce(
                jnp.maximum, [jnp.max(s, 0, keepdims=True) for s in blocks]
            )
            mixed = None
            for kb in range(4):
                probs = jnp.exp(blocks[kb] - top).astype(bf16)
                part = dotf(turned[h][:, 256 * kb : 256 * kb + 256], probs)
                mixed = part if mixed is None else mixed + part
            total = mixed[HEAD * (1 - h) : HEAD * (1 - h) + 1, :]
            lse_ref[0, h : h + 1, rows] = top + jnp.log(total)
            outs.append(mixed[HEAD * h : HEAD * h + HEAD, :] / total)
        o_ref[rows, :] = jnp.concatenate(outs, 0).T.astype(bf16)


def kv_blocks(groups, first=0):
    half = groups // 2
    return [
        pl.BlockSpec((512, 128), lambda i, s: (0, i + first)),
        pl.BlockSpec((512, 128), lambda i, s: (0, i + first + groups)),
        pl.BlockSpec((512, 128), lambda i, s: (0, (i + first + half) % groups)),
        pl.BlockSpec((512, 128), lambda i, s: (0, (i + first + half) % groups + groups)),
    ]


def attend_forward(info, q, kv, kv_other, window):
    groups = q.shape[1] // 128
    block = pl.BlockSpec((512, 128), lambda i, s: (0, i))
    return pl.pallas_call(
        forward_kernel,
        grid_spec=pltpu.PrefetchScalarGridSpec(
            num_scalar_prefetch=1,
            grid=(groups,),
            in_specs=[
                block,
                *kv_blocks(groups),
                pl.BlockSpec((1, 2, 2, SPAN), lambda i, s: (i, 0, 0, 0)),
            ],
            out_specs=[block, pl.BlockSpec((1, 2, 512), lambda i, s: (i, 0, 0))],
            scratch_shapes=[pltpu.VMEM((2, 2, STRIP, 128), f32)],
        ),
        out_shape=[
            jax.ShapeDtypeStruct((512, 128 * groups), bf16),
            jax.ShapeDtypeStruct((groups, 2, 512), f32),
        ],
        compiler_params=pltpu.CompilerParams(vmem_limit_bytes=24 * MIB),
        cost_estimate=cost(17),
        name="attend_forward",
    )(info, q, kv, kv, kv_other, kv_other, window)


def backward_kernel(with_table, *refs):
    info_ref, q_ref, k_ref, v_ref, ko_ref, vo_ref, do_ref, lse_ref, win_ref = refs[:9]
    dq_ref, dk_ref, dv_ref, dko_ref, dvo_ref, *rest = refs[9:]
    qlen, core = info_ref[0], info_ref[1]
    strip_ref = rest[-1]
    for h in range(2):
        for kind in range(2):
            make_strip(win_ref, h, kind, strip_ref)
    if with_table:
        held_ref, strip_grad_ref = rest[:2]
        strip_grad_ref[...] = jnp.zeros_like(strip_grad_ref)
    keys = whole(core, k_ref[...], ko_ref[...])
    values = whole(core, v_ref[...], vo_ref[...])
    keys_turned = keys.T
    key_grads = [jnp.zeros((256, 128), f32) for _ in range(4)]
    value_grads = [jnp.zeros((256, 128), f32) for _ in range(4)]
    for ib in range(2):
        rows = slice(256 * ib, 256 * ib + 256)
        query = q_ref[rows, :] * jnp.asarray(0.125, bf16)
        grad = do_ref[rows, :]
        query_grads = []
        for h in range(2):
            mask = lane_mask(256, h)
            one = jnp.where(mask, query, jnp.zeros_like(query))
            grad_one = jnp.where(mask, grad, jnp.zeros_like(grad))
            log_total = lse_ref[0, h : h + 1, rows]
            probs, terms = [], []
            row_term = 0.0
            for kb in range(4):
                kr = slice(256 * kb, 256 * kb + 256)
                scores = score_block(info_ref, keys[kr], one, strip_ref, h, ib, kb)
                part = jnp.exp(scores - log_total)
                term = part * dotf(values[kr], grad_one, NT)
                row_term = row_term + jnp.sum(term, 0, keepdims=True)
                value_grads[kb] = value_grads[kb] + dotf(part.astype(bf16), grad_one)
                probs.append(part)
                terms.append(term)
            flat = None
            for kb in range(4):
                kr = slice(256 * kb, 256 * kb + 256)
                grad_scores = (terms[kb] - probs[kb] * row_term).astype(bf16)
                key_grads[kb] = key_grads[kb] + dotf(grad_scores, one)
                part = dotf(keys_turned[:, kr], grad_scores)
                flat = part if flat is None else flat + part
                if with_table:
                    for u in (0, 1):
                        tile = 2 * ib + u
                        where = strip_rows(tile, kb)
                        part = grad_scores[:, 128 * u : 128 * u + 128].astype(f32)
                        strip_grad_ref[h, 0, where, :] += part
                        cross = cross_mask(qlen, core, tile, kb)
                        if cross is not None:
                            strip_grad_ref[h, 1, where, :] += jnp.where(cross, part, 0.0)
            query_grads.append(flat[HEAD * h : HEAD * h + HEAD, :])
        dq_ref[rows, :] = (jnp.concatenate(query_grads, 0).T * 0.125).astype(bf16)
    for grads, own_ref, other_ref in (
        (key_grads, dk_ref, dko_ref),
        (value_grads, dv_ref, dvo_ref),
    ):
        first = jnp.concatenate(grads[:2], 0)
        second = jnp.concatenate(grads[2:], 0)
        own_ref[...] = jnp.where(core == 0, first, second)
        other_ref[...] = jnp.where(core == 0, second, first).astype(bf16)
    if with_table:
        for h in range(2):
            for kind in range(2):
                sum_strip(strip_grad_ref, h, kind, held_ref)


def attend_backward(info, q, kv, kv_other, grad, lse, window, with_table, first, count):
    groups = q.shape[1] // 128
    block = pl.BlockSpec((512, 128), lambda i, s: (0, i + first))
    rows = lambda kind: jax.ShapeDtypeStruct((512, 128 * count), kind)
    out_specs = [pl.BlockSpec((512, 128), lambda i, s: (0, i))] * 5
    out_shape = [rows(bf16), rows(f32), rows(f32), rows(bf16), rows(bf16)]
    scratch = [pltpu.VMEM((2, 2, STRIP, 128), f32)]
    if with_table:
        out_specs.append(pl.BlockSpec((1, 2, 2, 8, SPAN), lambda i, s: (i, 0, 0, 0, 0)))
        out_shape.append(jax.ShapeDtypeStruct((count, 2, 2, 8, SPAN), f32))
        scratch = scratch * 2
    return pl.pallas_call(
        functools.partial(backward_kernel, with_table),
        grid_spec=pltpu.PrefetchScalarGridSpec(
            num_scalar_prefetch=1,
            grid=(count,),
            in_specs=[
                block,
                *kv_blocks(groups, first),
                block,
                pl.BlockSpec((1, 2, 512), lambda i, s: (i + first, 0, 0)),
                pl.BlockSpec((1, 2, 2, SPAN), lambda i, s: (i + first, 0, 0, 0)),
            ],
            out_specs=out_specs,
            scratch_shapes=scratch,
        ),
        out_shape=out_shape,
        compiler_params=pltpu.CompilerParams(vmem_limit_bytes=36 * MIB),
        cost_estimate=cost(30),
        name="attend_backward",
    )(info, q, kv, kv, kv_other, kv_other, grad, lse, window)


def norm_parts(values):
    centre = jnp.mean(values, -1, keepdims=True)
    centred = values - centre
    scale = lax.rsqrt(jnp.mean(centred * centred, -1, keepdims=True) + EPS)
    return centred * scale, scale


def norm_back(grad, gain, normal, scale):
    scaled = grad * gain
    return scale * (
        scaled
        - jnp.mean(scaled, -1, keepdims=True)
        - normal * jnp.mean(scaled * normal, -1, keepdims=True)
    )


def normal_cdf(units):
    size = jnp.abs(units)
    t = 1.0 / (1.0 + (0.3275911 * 0.5**0.5) * size)
    bell = jnp.exp(-0.5 * units * units)
    poly = 0.5 * 1.061405429
    for coef in (-1.453152027, 1.421413741, -0.284496736, 0.254829592):
        poly = poly * t + 0.5 * coef
    tail = poly * t * bell
    return jnp.where(units >= 0, 1.0 - tail, tail), bell


def ffn_forward_kernel(
    keep,
    att_ref,
    x_ref,
    out_ref,
    up_ref,
    up_far_ref,
    down_ref,
    down_far_ref,
    bias_ref,
    gain_ref,
    shift_ref,
    result_ref,
    *rest,
):
    if keep:
        (
            low_ref,
            active_ref,
            slope_ref,
            n_one_ref,
            s_one_ref,
            n_two_ref,
            s_two_ref,
            normed_low,
            total,
        ) = rest
    else:
        normed_low, total = rest
    i = pl.program_id(0)

    @pl.when(i == 0)
    def _():
        before = x_ref[...].astype(f32) + (dotf(att_ref[...], out_ref[...]) + shift_ref[0:1, :])
        normal, scale = norm_parts(before)
        normed = normal * gain_ref[0:1, :] + shift_ref[1:2, :]
        normed_low[...] = normed.astype(bf16)
        total[...] = normed + shift_ref[2:3, :]
        if keep:
            n_one_ref[...] = normal
            s_one_ref[...] = scale
            low_ref[...] = normed_low[...]

    near = i < 2
    width = up_ref.shape[2]
    step = 256
    add = None
    for first in range(0, width, step):
        cols = slice(first, first + step)
        up = jnp.where(near, up_ref[0, :, cols], up_far_ref[0, :, cols])
        down = jnp.where(near, down_ref[0, cols, :], down_far_ref[0, cols, :])
        units = dotf(normed_low[...], up) + bias_ref[0, :, cols]
        side, bell = normal_cdf(units)
        active = (units * side).astype(bf16)
        if keep:
            active_ref[:, cols] = active
            slope_ref[:, cols] = (side + units * bell * 0.3989422804014327).astype(bf16)
        part = dotf(active, down)
        add = part if add is None else add + part
    total[...] += add

    @pl.when(i == pl.num_programs(0) - 1)
    def _():
        normal, scale = norm_parts(total[...])
        result = normal * gain_ref[1:2, :] + shift_ref[3:4, :]
        result_ref[...] = result.astype(result_ref.dtype)
        if keep:
            n_two_ref[...] = normal
            s_two_ref[...] = scale


def near_far(rows, cols):
    return [
        pl.BlockSpec((1, rows, cols), lambda i: (jnp.minimum(i, 1), 0, 0)),
        pl.BlockSpec((1, rows, cols), lambda i: (jnp.maximum(i - 2, 0), 0, 0)),
    ]


def ffn_forward(w, attended, inputs, keep, part=0, parts=1):
    rows, model = inputs.shape
    rows //= parts
    width = w["up"][0].shape[2]
    all_of = lambda *shape: pl.BlockSpec(shape, lambda i: (0,) * len(shape))
    by_step = pl.BlockSpec((rows, width), lambda i: (0, i))
    shape = lambda cols, kind: jax.ShapeDtypeStruct((rows, cols), kind)
    out_specs = [all_of(rows, model)]
    out_shape = [shape(model, f32 if keep else bf16)]
    if keep:
        out_specs += [all_of(rows, model), by_step, by_step]
        out_specs += [all_of(rows, model), all_of(rows, 1)] * 2
        out_shape += [shape(model, bf16), shape(4 * width, bf16), shape(4 * width, bf16)]
        out_shape += [shape(model, f32), shape(1, f32)] * 2
    flops = 2 * rows * model * (model + 8 * width)
    return pl.pallas_call(
        functools.partial(ffn_forward_kernel, keep),
        grid=(4,),
        in_specs=[
            pl.BlockSpec((rows, model), lambda i: (part, 0)),
            pl.BlockSpec((rows, model), lambda i: (part, 0)),
            all_of(model, model),
            *near_far(model, width),
            *near_far(width, model),
            pl.BlockSpec((1, 1, width), lambda i: (i, 0, 0)),
            all_of(2, model),
            all_of(4, model),
        ],
        out_specs=out_specs,
        out_shape=out_shape,
        scratch_shapes=[pltpu.VMEM((rows, model), bf16), pltpu.VMEM((rows, model), f32)],
        compiler_params=pltpu.CompilerParams(vmem_limit_bytes=32 * MIB),
        cost_estimate=cost(15),
        name="ffn_forward",
    )(
        attended,
        inputs,
        w["out"],
        *w["up"],
        *w["down"],
        w["up_bias"],
        w["gains"],
        w["shifts"],
    )


def top_back_kernel(gy_ref, n_two_ref, s_two_ref, gain_ref, after_ref, second_ref, sums_ref):
    gy = gy_ref[...].astype(f32)
    after = norm_back(gy, gain_ref[1:2, :], n_two_ref[...], s_two_ref[...])
    low = after.astype(bf16)
    after_ref[...] = after
    second_ref[...] = low
    sums_ref[0:1, :] = jnp.sum(gy * n_two_ref[...], 0, keepdims=True)
    sums_ref[1:2, :] = jnp.sum(low.astype(f32), 0, keepdims=True)
    sums_ref[2:3, :] = jnp.sum(gy, 0, keepdims=True)
    sums_ref[3:8, :] = jnp.zeros((5, sums_ref.shape[1]), f32)


def top_back(w, saved, grad_y):
    rows, model = grad_y.shape
    return pl.pallas_call(
        top_back_kernel,
        out_shape=[
            jax.ShapeDtypeStruct((rows, model), f32),
            jax.ShapeDtypeStruct((rows, model), bf16),
            jax.ShapeDtypeStruct((8, model), f32),
        ],
        compiler_params=pltpu.CompilerParams(vmem_limit_bytes=16 * MIB),
        cost_estimate=cost(2),
        name="top_back",
    )(grad_y, saved["n_two"], saved["s_two"], w["gains"])


def ffn_backward_kernel(deps, *refs):
    (
        after_ref,
        second_ref,
        slope_ref,
        n_one_ref,
        s_one_ref,
        out_ref,
        up_ref,
        up_far_ref,
        down_ref,
        down_far_ref,
        gain_ref,
    ) = refs[:11]
    hidden_ref, before_ref, branch_ref, att_ref, sums_ref, hidden_sums_ref, total = refs[11 + deps :]
    i = pl.program_id(0)

    def add_up(value):
        return jnp.sum(value, 0, keepdims=True)

    @pl.when(i == 0)
    def _():
        total[...] = after_ref[...]

    near = i < 2
    width = up_ref.shape[2]
    step = 256
    add = None
    for first in range(0, width, step):
        cols = slice(first, first + step)
        up = jnp.where(near, up_ref[0, :, cols], up_far_ref[0, :, cols])
        down = jnp.where(near, down_ref[0, cols, :], down_far_ref[0, cols, :])
        active = dotf(second_ref[...], down, NT)
        hidden = (active * slope_ref[:, cols].astype(f32)).astype(bf16)
        hidden_ref[:, cols] = hidden
        hidden_sums_ref[0, :, cols] = add_up(hidden.astype(f32))
        part = dotf(hidden, up, NT)
        add = part if add is None else add + part
    total[...] += add

    @pl.when(i == pl.num_programs(0) - 1)
    def _():
        normed = total[...]
        before = norm_back(normed, gain_ref[0:1, :], n_one_ref[...], s_one_ref[...])
        low = before.astype(bf16)
        before_ref[...] = before
        branch_ref[...] = low
        att_ref[...] = dotf(low, out_ref[...], NT).astype(bf16)
        sums_ref[0:1, :] = add_up(normed * n_one_ref[...])
        sums_ref[1:2, :] = add_up(low.astype(f32))
        sums_ref[2:3, :] = add_up(normed)
        sums_ref[3:8, :] = jnp.zeros((5, sums_ref.shape[1]), f32)


def ffn_backward(w, saved, after, second, deps=()):
    rows, model = after.shape
    width = w["up"][0].shape[2]
    all_of = lambda *shape: pl.BlockSpec(shape, lambda i: (0,) * len(shape))
    by_step = pl.BlockSpec((rows, width), lambda i: (0, i))
    by_block = pl.BlockSpec((1, 1, width), lambda i: (i, 0, 0))
    shape = lambda cols, kind: jax.ShapeDtypeStruct((rows, cols), kind)
    whole_rows = all_of(rows, model)
    return pl.pallas_call(
        functools.partial(ffn_backward_kernel, len(deps)),
        grid=(4,),
        in_specs=[
            whole_rows,
            whole_rows,
            by_step,
            whole_rows,
            all_of(rows, 1),
            all_of(model, model),
            *near_far(model, width),
            *near_far(width, model),
            all_of(2, model),
            *[pl.BlockSpec(memory_space=pl.ANY)] * len(deps),
        ],
        out_specs=[by_step, whole_rows, whole_rows, whole_rows, all_of(8, model), by_block],
        out_shape=[
            shape(4 * width, bf16),
            shape(model, f32),
            shape(model, bf16),
            shape(model, bf16),
            jax.ShapeDtypeStruct((8, model), f32),
            jax.ShapeDtypeStruct((4, 1, width), f32),
        ],
        scratch_shapes=[pltpu.VMEM((rows, model), f32)],
        compiler_params=pltpu.CompilerParams(vmem_limit_bytes=32 * MIB),
        cost_estimate=cost(15),
        name="ffn_backward",
    )(
        after,
        second,
        saved["slope"],
        saved["n_one"],
        saved["s_one"],
        w["out"],
        *w["up"],
        *w["down"],
        w["gains"],
        *deps,
    )


def weight_grad_kernel(l_ref, lo_ref, r_ref, ro_ref, o_ref):
    total = dotf(l_ref[...], r_ref[...], TN) + dotf(lo_ref[...], ro_ref[...], TN)
    o_ref[...] = total.astype(o_ref.dtype)


def weight_grad(left, left_far, right, right_far, kind, left_cols, right_cols):
    rows = left.shape[0]
    lf, ln, lw = left_cols
    rf, rn, rw = right_cols
    return pl.pallas_call(
        weight_grad_kernel,
        grid=(rn, ln),
        in_specs=[
            pl.BlockSpec((rows, lw), lambda j, i: (0, lf + i)),
            pl.BlockSpec((rows, lw), lambda j, i: (0, lf + i)),
            pl.BlockSpec((rows, rw), lambda j, i: (0, rf + j)),
            pl.BlockSpec((rows, rw), lambda j, i: (0, rf + j)),
        ],
        out_specs=pl.BlockSpec((lw, rw), lambda j, i: (i, j)),
        out_shape=jax.ShapeDtypeStruct((ln * lw, rn * rw), kind),
        compiler_params=pltpu.CompilerParams(vmem_limit_bytes=20 * MIB),
        cost_estimate=cost(4),
        name="weight_grad",
    )(left, left_far, right, right_far)


def split_grad_kernel(l_ref, lo_ref, r_ref, ro_ref, kept_ref, sent_ref):
    total = dotf(l_ref[...], r_ref[...], TN) + dotf(lo_ref[...], ro_ref[...], TN)
    half = total.shape[0] // 2
    kept_ref[...] = total[:half]
    sent_ref[...] = total[half:].astype(bf16)


def split_grad(left, left_far, right, right_far, width):
    rows, model = right.shape
    count = left_far.shape[1] // width
    left_block = pl.BlockSpec((rows, width), lambda i: (0, i))
    right_block = pl.BlockSpec((rows, model), lambda i: (0, 0))
    made = pl.BlockSpec((width // 2, model), lambda i: (i, 0))
    shape = (count * width // 2, model)
    return pl.pallas_call(
        split_grad_kernel,
        grid=(count,),
        in_specs=[left_block, left_block, right_block, right_block],
        out_specs=[made, made],
        out_shape=[jax.ShapeDtypeStruct(shape, f32), jax.ShapeDtypeStruct(shape, bf16)],
        compiler_params=pltpu.CompilerParams(vmem_limit_bytes=20 * MIB),
        cost_estimate=cost(4),
        name="split_grad",
    )(left, left_far, right, right_far)


IN_VMEM = pl.BlockSpec(memory_space=pltpu.VMEM)


def project_kernel(x_ref, near_ref, far_ref, bias_ref, q_ref, kv_ref):
    inputs = x_ref[...]
    half = near_ref.shape[1]
    for which in range(3):
        for side, ref in enumerate((near_ref, far_ref)):
            made = dotf(inputs, ref[which], NT) + bias_ref[2 * which + side]
            first = half * side + 2 * half * max(which - 1, 0)
            out_ref = kv_ref if which else q_ref
            out_ref[:, first : first + half] = made.astype(bf16)


def project(inputs, near, far, bias):
    rows, model = inputs.shape
    return pl.pallas_call(
        project_kernel,
        in_specs=[IN_VMEM] * 4,
        out_specs=[IN_VMEM] * 2,
        out_shape=[
            jax.ShapeDtypeStruct((rows, model), bf16),
            jax.ShapeDtypeStruct((rows, 2 * model), bf16),
        ],
        compiler_params=pltpu.CompilerParams(vmem_limit_bytes=16 * MIB),
        cost_estimate=cost(4),
        name="project",
    )(inputs, near, far, bias)


def input_back_kernel(*refs):
    q_ref, k_ref, k_came_ref, v_ref, v_came_ref, before_ref, *weights = refs[:8]
    near_ref, far_ref, grad_ref, low_ref, sums_ref = refs[8:]
    half = near_ref.shape[1] // 3
    total = before_ref[...]
    for which in range(3):
        for side in range(2):
            cols = slice(half * side, half * side + half)
            other = slice(half * (1 - side), half * (1 - side) + half)
            if which == 0:
                mixed = q_ref[:, cols]
            else:
                own, came = (k_ref, k_came_ref) if which == 1 else (v_ref, v_came_ref)
                mixed = (own[:, cols] + came[:, other].astype(f32)).astype(bf16)
            (far_ref if side else near_ref)[:, half * which : half * which + half] = mixed
            sums_ref[2 * which + side] = jnp.sum(mixed.astype(f32), 0, keepdims=True)
            total = total + dotf(mixed, weights[side][which])
    grad_ref[...] = total
    low_ref[...] = total.astype(bf16)


def input_back(q, k, k_came, v, v_came, before, near, far):
    rows, model = before.shape
    half = model // 2
    return pl.pallas_call(
        input_back_kernel,
        in_specs=[IN_VMEM] * 8,
        out_specs=[IN_VMEM] * 5,
        out_shape=[
            jax.ShapeDtypeStruct((rows, 3 * half), bf16),
            jax.ShapeDtypeStruct((rows, 3 * half), bf16),
            jax.ShapeDtypeStruct((rows, model), f32),
            jax.ShapeDtypeStruct((rows, model), bf16),
            jax.ShapeDtypeStruct((6, 1, half), f32),
        ],
        compiler_params=pltpu.CompilerParams(vmem_limit_bytes=24 * MIB),
        cost_estimate=cost(6),
        name="input_back",
    )(q, k, k_came, v, v_came, before, near, far)


def body(
    hidden,
    cotangent,
    pair_lengths,
    query_lengths,
    buckets,
    qkv_weight,
    qv_bias,
    out_weight,
    up_weight,
    ffn_bias,
    down_weight,
    norm_gains,
    vectors,
    bias_table,
):
    leading = lax.axis_index("section") == 0
    place = lax.axis_index("tensor")
    y, core = place // 2, place % 2
    plane = lax.axis_index("dp")
    planes = lax.axis_size("dp")
    odd = plane % 2
    local, model = hidden.shape[1], hidden.shape[2]
    total = 4 * local
    cols = qkv_weight.shape[3]
    width = up_weight.shape[2]
    heads = bias_table.shape[1]
    kinds = bias_table.shape[2] // 2
    near, far = slice(0, 2 * cols), slice(2 * cols, 4 * cols)

    def swap_z(value):
        return lax.ppermute(value, "dp", [(i, i ^ 1) for i in range(planes)])

    def mine(array):
        return lax.dynamic_index_in_dim(array, y, 0, keepdims=False)

    def theirs(array):
        return lax.dynamic_index_in_dim(array, 1 - y, 0, keepdims=False)

    def in_order(first, own, came, axis=0):
        return jnp.concatenate(
            [jnp.where(first, own, came), jnp.where(first, came, own)], axis
        )

    def own_half(block, axis=0):
        half = block.shape[axis] // 2
        return lax.dynamic_slice_in_dim(block, half * odd, half, axis)

    def edge_blocks(value):
        return value.reshape(2, local, model)

    def stage(work):
        shapes = jax.eval_shape(work)
        return lax.cond(
            pair_lengths[0] > 0,
            work,
            lambda: jax.tree.map(lambda leaf: jnp.zeros(leaf.shape, leaf.dtype), shapes),
        )

    qkv_own = qkv_weight[0].transpose(1, 2, 0)
    out_own, up_own, down_own = out_weight[0], up_weight[0], down_weight[0]
    small = jnp.concatenate([qv_bias[0].reshape(-1), ffn_bias[0], bias_table[0].reshape(-1)])

    def send_small():
        return swap_y(small), theirs(hidden), own_half(qkv_own, 1)

    small_y, x_sent, qkv_sent = stage(send_small)

    def gather_small():
        two = jnp.stack([small, small_y])
        four = jnp.concatenate([two, swap_c(two)])
        table = four[:, 2 * cols + width :].reshape(8 * heads, kinds)
        turned = lax.dynamic_slice_in_dim(jnp.pad(buckets, (1, 0)), 256 * core, SPAN, 0)
        onehot = (turned[:, None] == jnp.arange(kinds, dtype=jnp.int32)[None, :]).astype(f32)
        window = lax.dot_general(table, onehot, NT, precision=lax.Precision.HIGHEST)
        qv_all = four[:, : 2 * cols].reshape(4, 2, cols)
        q_bias, v_bias = qv_all[:, 0].reshape(-1), qv_all[:, 1].reshape(-1)
        bias = jnp.concatenate([q_bias, jnp.zeros((model,), f32), v_bias])
        info = jnp.stack([mine(query_lengths), core, mine(pair_lengths)]).astype(jnp.int32)
        return (
            window.reshape(2 * heads, 2, 2, SPAN),
            onehot,
            bias.reshape(6, 1, 2 * cols),
            four[:, 2 * cols : 2 * cols + width].reshape(4, 1, width),
            info,
            own_half(out_own),
            own_half(up_own),
            own_half(down_own),
        )

    x_came, qkv_y, found = stage(lambda: (swap_y(x_sent), swap_y(qkv_sent), stage(gather_small)))
    window, onehot, bias, up_bias, info, out_sent, up_sent, down_sent = found
    w = dict(up_bias=up_bias, gains=norm_gains[0], shifts=vectors[0])

    def second_stage():
        x0 = in_order(y == 0, mine(hidden), x_came)
        return swap_z(qkv_y), swap_y(out_sent), swap_y(up_sent), x0

    qkv_z, out_y, up_y, x0 = stage(second_stage)

    def gather_qkv():
        near = jnp.concatenate([qkv_own, in_order(odd == 0, qkv_y, qkv_z, 1)], 1)
        far = swap_c(near)
        q, kv = project(x0, near, far, bias)
        return (near, far), q, kv, swap_c(kv)

    def third_stage():
        return stage(gather_qkv), swap_y(down_sent), swap_z(out_y), swap_z(up_y)

    (qkv, q, kv, kv_other), down_y, out_z, up_z = stage(third_stage)
    out = jnp.concatenate([out_own, in_order(odd == 0, out_y, out_z)], 0)
    up = jnp.stack([up_own, in_order(odd == 0, up_y, up_z)])

    def fourth_stage():
        found = stage(lambda: attend_forward(info, q, kv, kv_other, window)[0])
        return swap_z(down_y), swap_c(out), swap_c(up), found

    down_z, out_far, up_far, attended = stage(fourth_stage)
    down = jnp.stack([down_own, in_order(odd == 0, down_y, down_z)])
    w["down"] = down, stage(lambda: swap_c(down))
    w["out"] = jnp.concatenate([out, out_far], 0)
    w["up"] = up, up_far

    def to_next(value):
        return lax.ppermute(value, "section", [(0, 1)])

    def to_last(value):
        return lax.ppermute(value, "section", [(1, 0)])

    middle = ffn_forward(w, attended, x0, False, 0, 2)[0]
    came_a, middle = stage(
        lambda: (to_next(middle), ffn_forward(w, attended, x0, False, 1, 2)[0])
    )
    came_b = stage(lambda: to_next(middle))

    def project_again():
        x1 = jnp.where(leading, x0, jnp.concatenate([came_a, came_b], 0))
        q, kv = project(x1, *qkv, bias)
        return x1, q, kv, swap_c(kv)

    x1, q, kv, kv_other = stage(project_again)
    top_sent = theirs(cotangent)

    def eighth_stage():
        attended, lse = attend_forward(info, q, kv, kv_other, window)
        return swap_y(top_sent), swap_c(x1), attended, lse

    top_came, inputs_far, attended, lse = stage(eighth_stage)
    grad_top = in_order(y == 0, mine(cotangent), top_came)
    result, normed_low, active, slope, n_one, s_one, n_two, s_two = ffn_forward(
        w, attended, x1, True
    )
    saved = dict(slope=slope, n_one=n_one, s_one=s_one, n_two=n_two, s_two=s_two)

    def dense_back(after, second):
        names = ("hidden", "before", "branch", "attended", "low_sums", "hidden_sums")
        return dict(zip(names, ffn_backward(w, saved, after, second)))

    def attention_back(grads, table, first, count):
        return attend_backward(
            info, q, kv, kv_other, grads["attended"], lse, window, table, first, count
        )

    after, second, top_sums = top_back(w, saved, grad_top)

    def ninth_stage():
        return (
            swap_c(normed_low),
            swap_c(active[:, 2 * width :]),
            swap_c(attended[:, far]),
            dense_back(after, second),
        )

    normed_far, active_far, attended_far, grads = stage(ninth_stage)
    grad_q, grad_k, grad_v, k_far, v_far = attention_back(grads, False, 0, 6)

    def to_middle():
        k_came, v_came = swap_c(k_far), swap_c(v_far)
        found = input_back(grad_q, grad_k, k_came, grad_v, v_came, grads["before"], *qkv)
        return to_last(found[3])

    grad_y = jnp.where(leading, stage(to_middle), grad_top)

    thirds = width // 3

    def down_grad(kind, first):
        return weight_grad(
            active, active_far, second, second_far, kind, (first, 3, thirds), (0, 1, model)
        )

    after, second, top_sums = top_back(w, saved, grad_y)
    second_far = stage(lambda: swap_c(second))
    down_sent = down_grad(bf16, 3)

    def through_dense():
        return dense_back(after, second), down_grad(f32, 0)

    down_came, (grads, down_kept) = stage(lambda: (swap_y(down_sent), stage(through_dense)))
    hidden, branch = grads["hidden"], grads["branch"]
    low_sum = lambda own, came: (own + came.astype(f32)).astype(bf16)
    down = low_sum(down_kept, down_came)

    def exchange_dense():
        return swap_c(hidden[:, 2 * width :]), swap_c(branch)

    def send_dense(hidden_far, branch_far):
        args = normed_low, normed_far, hidden, hidden_far
        sent = weight_grad(*args, bf16, (0, 3, thirds), (1, 1, width))
        return sent, split_grad(attended, attended_far, branch, branch_far, 2 * cols)

    def through_attention(hidden_far):
        args = normed_low, normed_far, hidden, hidden_far
        kept = weight_grad(*args, f32, (0, 3, thirds), (0, 1, width))
        return attention_back(grads, True, 0, 6), kept

    def through_input(q_grad, k_grad, v_grad, k_far, v_far):
        came = swap_c(k_far), swap_c(v_far)
        near, far, grad_input, grad_low, qv_sums = input_back(
            q_grad, k_grad, came[0], v_grad, came[1], grads["before"], *qkv
        )
        rest_kept, rest_sent = split_grad(near, swap_c(far), x1, inputs_far, 2 * cols)
        return rest_kept, rest_sent, grad_input, grad_low, qv_sums

    def after_down():
        hidden_far, branch_far = stage(exchange_dense)
        up_sent, (out_kept, out_sent) = stage(lambda: send_dense(hidden_far, branch_far))
        up_came, out_came, (found, up_kept) = stage(
            lambda: (
                swap_y(up_sent),
                swap_y(out_sent),
                stage(lambda: through_attention(hidden_far)),
            )
        )
        return found, low_sum(up_kept, up_came), low_sum(out_kept, out_came)

    def after_up():
        rest_kept, rest_sent, *found = stage(lambda: through_input(*attention_found))
        return low_sum(rest_kept, stage(lambda: swap_y(rest_sent))), found

    def through_sums(held, qv_sums, grad_low):
        edge_low = edge_blocks(jnp.where(leading, grad_low, result.astype(bf16)))
        edge_came = swap_y(theirs(edge_low))
        sums = token_sums(held, qv_sums)
        sums = sums[:2] + swap_c(sums[2:])
        sums = sums[0] + swap_y(sums[1])
        if planes == 4:
            sums = sums + swap_z(sums)
            sums = sums + lax.ppermute(sums, "dp", [(0, 2), (2, 0), (1, 3), (3, 1)])
        else:
            sums = lax.psum(sums, "dp")
        return sums, edge_came

    share = model // 4

    def token_sums(held, qv_sums):
        wide = jnp.pad(held.reshape(4 * heads, 2, 8, SPAN), ((0, 0), (0, 0), (0, 0), (0, 8)))
        sums = sum(wide[:, :, s, s : s + SPAN] for s in range(8))
        sums = jnp.stack([sums[:, 0] - sums[:, 1], sums[:, 1]], 1).reshape(8 * heads, SPAN)
        grad_table = jnp.dot(sums, onehot, precision=lax.Precision.HIGHEST)
        grad_table = grad_table.reshape(4, heads * 2 * kinds)
        q_sums, _, v_sums = qv_sums.reshape(3, 4, cols)
        grad_ffn = grads["hidden_sums"].reshape(4, width)
        low_sums = grads["low_sums"]
        rows = [low_sums[0], top_sums[0], low_sums[1], low_sums[2], top_sums[1], top_sums[2]]
        by_share = jnp.stack(rows).reshape(6, 4, share)
        by_share = by_share.transpose(1, 0, 2).reshape(4, 6 * share)
        by_share = jnp.stack(
            [lax.dynamic_index_in_dim(by_share, place ^ flip, 0, False) for flip in (0, 2, 1, 3)]
        )
        return jnp.concatenate([grad_table, q_sums, v_sums, grad_ffn, by_share], 1)

    grad_down, (found, *later) = stage(lambda: (lax.psum(down, "dp"), stage(after_down)))
    *attention_found, held = found
    summed, (rest, found) = stage(lambda: (lax.psum(later, "dp"), stage(after_up)))
    grad_input, grad_low, qv_sums = found
    grad_qkv, (sums, edge_came) = stage(
        lambda: (lax.psum(rest, "dp"), stage(lambda: through_sums(held, qv_sums, grad_low)))
    )
    grad_down, grad_qkv = grad_down.astype(f32), grad_qkv.astype(f32)
    grad_up, grad_out = [value.astype(f32) for value in summed]
    edge_own = mine(edge_blocks(jnp.where(leading, grad_input, result)))
    edge_came = edge_came.astype(f32)
    edges = jnp.stack([jnp.where(y == 0, edge_own, edge_came), jnp.where(y == 0, edge_came, edge_own)])
    grad_qkv = grad_qkv.reshape(1, 3, cols, model).transpose(0, 3, 1, 2)
    at = heads * 2 * kinds
    table_out = sums[:at].reshape(heads, 2 * kinds)
    qv_out = sums[at : at + 2 * cols].reshape(2, cols)
    ffn_out = sums[at + 2 * cols : at + 2 * cols + width]
    vec_out = sums[at + 2 * cols + width :].reshape(6, share)
    return (
        edges[None],
        grad_qkv,
        qv_out[None],
        grad_out[None],
        grad_up[None],
        ffn_out[None],
        grad_down[None],
        vec_out[:2][None],
        vec_out[2:][None],
        table_out[None],
    )


def solution(mesh):
    return jax.shard_map(
        body,
        mesh=mesh,
        in_specs=(
            P("dp", "tensor", None),
            P("dp", "tensor", None),
            P("dp"),
            P("dp"),
            P(),
            P("section", None, None, "tensor"),
            P("section", None, "tensor"),
            P("section", "tensor", None),
            P("section", None, "tensor"),
            P("section", "tensor"),
            P("section", "tensor", None),
            P("section", None, None),
            P("section", None, None),
            P("section", "tensor", None),
        ),
        out_specs=(
            P("section", "dp", "tensor", None),
            P("section", None, None, "tensor"),
            P("section", None, "tensor"),
            P("section", "tensor", None),
            P("section", None, "tensor"),
            P("section", "tensor"),
            P("section", "tensor", None),
            P("section", None, "tensor"),
            P("section", None, "tensor"),
            P("section", "tensor", None),
        ),
        check_vma=False,
    )
```

```python
import functools

import jax
import jax.numpy as jnp
from jax import lax
from jax.experimental import pallas as pl
from jax.experimental.pallas import tpu as pltpu
from jax.sharding import PartitionSpec as P


f32 = jnp.float32
bf16 = jnp.bfloat16
EPS = 1e-05
HEAD = 64
NEG = -1e30
SWAP_Y = [(0, 2), (2, 0), (1, 3), (3, 1)]
SWAP_C = [(0, 1), (1, 0), (2, 3), (3, 2)]
NT = (((1,), (1,)), ((), ()))
TN = (((0,), (0,)), ((), ()))
NN = (((1,), (0,)), ((), ()))
KEY_BASE = (0, 512, 256, 768)
TILE_BASE = (0, 128, 512, 640)
STRIP = 1664
SPAN = STRIP + 128
PIECE = 32
MIB = 2**20


def cost(us, flops=0):
    return pl.CostEstimate(flops=flops, bytes_accessed=int(us * 3.4e6), transcendentals=0)


def dotf(a, b, dims=NN):
    return lax.dot_general(a, b, dims, preferred_element_type=f32)


def swap_y(value):
    return lax.ppermute(value, "tensor", SWAP_Y)


def swap_c(value):
    return lax.ppermute(value, "tensor", SWAP_C)


def make_strip(window_ref, h, kind, strip_ref):
    blocks = STRIP // 128
    lane = lax.broadcasted_iota(jnp.int32, (8, 128), 1)
    row = lax.broadcasted_iota(jnp.int32, (8, 128), 0)

    def rolled(first):
        seg = window_ref[0, h, kind : kind + 1, first : first + 128]
        seg = pltpu.roll(jnp.broadcast_to(seg, (8, 128)), 0, 1, stride=1, stride_axis=0)
        return [pltpu.roll(seg, 8 * q, 1) if q else seg for q in range(16)]

    high = rolled(128 * blocks)
    for a in range(blocks):
        low = rolled(128 * (blocks - 1 - a))
        for q in range(16):
            rows = slice(128 * a + 8 * q, 128 * a + 8 * q + 8)
            strip_ref[h, kind, rows, :] = jnp.where(lane >= row + 8 * q, high[q], low[q])
        high = low


def sum_strip(strip_ref, h, kind, held_ref):
    blocks = STRIP // 128
    lane = lax.broadcasted_iota(jnp.int32, (8, 128), 1)
    carry = jnp.zeros((8, 128), f32)
    for a in reversed(range(blocks)):
        low, high = jnp.zeros((8, 128), f32), jnp.zeros((8, 128), f32)
        for q in range(16):
            part = strip_ref[h, kind, 128 * a + 8 * q : 128 * a + 8 * q + 8, :]
            if q:
                part = pltpu.roll(part, 128 - 8 * q, 1)
            stays = lane < 128 - 8 * q
            high += jnp.where(stays, part, 0.0)
            low += jnp.where(stays, 0.0, part)
        first = 128 * (blocks - 1 - a)
        held_ref[0, h, kind, :, first : first + 128] = low + carry
        carry = high
    held_ref[0, h, kind, :, 128 * blocks : 128 * blocks + 128] = carry


def lane_mask(rows, which):
    lane = lax.broadcasted_iota(jnp.int32, (rows, 128), 1)
    return (lane < HEAD) if which == 0 else (lane >= HEAD)


def cross_mask(info_ref, tile, first):
    key_low = first < 256
    row_low = tile < 2
    if not key_low and not row_low:
        return None
    qlen, core = info_ref[0], info_ref[1]
    shape = (PIECE, 128)
    if row_low:
        row = 256 * core + 128 * tile + lax.broadcasted_iota(jnp.int32, shape, 1)
        row_side = row < qlen
    if key_low:
        key_side = first + lax.broadcasted_iota(jnp.int32, shape, 0) < qlen
    if row_low and key_low:
        return row_side != key_side
    return row_side if row_low else key_side


def pieces(kb):
    for at in range(0, 256, PIECE):
        yield KEY_BASE[kb] + at, slice(256 * kb + at, 256 * kb + at + PIECE), slice(at, at + PIECE)


def strip_rows(tile, first):
    start = first - TILE_BASE[tile] + 640
    return slice(start, start + PIECE)


def piece_scores(info_ref, raw, strip_ref, h, ib, first):
    parts = []
    for u in (0, 1):
        tile = 2 * ib + u
        rows = strip_rows(tile, first)
        bias = strip_ref[h, 0, rows, :]
        cross = cross_mask(info_ref, tile, first)
        if cross is not None:
            bias = jnp.where(cross, strip_ref[h, 1, rows, :], bias)
        parts.append(raw[:, 128 * u : 128 * u + 128] + bias)
    scores = jnp.concatenate(parts, 1)
    if first >= 256:
        live = first + lax.broadcasted_iota(jnp.int32, (PIECE, 256), 0) < info_ref[2]
        scores = jnp.where(live, scores, NEG)
    return scores


def by_eight(value):
    return value.reshape(PIECE // 8, 8, 256)


def whole(core, own, other):
    return jnp.concatenate([jnp.where(core == 0, own, other), jnp.where(core == 0, other, own)], 0)


def forward_kernel(
    info_ref,
    q_ref,
    k_ref,
    v_ref,
    ko_ref,
    vo_ref,
    win_ref,
    o_ref,
    lse_ref,
    strip_ref,
    score_ref,
    prob_ref,
):
    core = info_ref[1]
    for h in range(2):
        for kind in range(2):
            make_strip(win_ref, h, kind, strip_ref)
    keys = whole(core, k_ref[...], ko_ref[...])
    values = whole(core, v_ref[...], vo_ref[...])
    one = jnp.ones_like(values)
    turned = [jnp.where(lane_mask(1024, h), values, one).T for h in range(2)]
    for ib in range(2):
        rows = slice(256 * ib, 256 * ib + 256)
        query = q_ref[rows, :] * jnp.asarray(0.125, bf16)
        outs = []
        for h in range(2):
            one = jnp.where(lane_mask(256, h), query, jnp.zeros_like(query))
            top = None
            for kb in range(4):
                raw = dotf(keys[256 * kb : 256 * kb + 256], one, NT)
                for first, at, within in pieces(kb):
                    scores = piece_scores(info_ref, raw[within], strip_ref, h, ib, first)
                    score_ref[h, at, :] = scores
                    most = jnp.max(by_eight(scores), 0)
                    top = most if top is None else jnp.maximum(top, most)
            top = jnp.max(top, 0, keepdims=True)
            for kb in range(4):
                for _, at, _ in pieces(kb):
                    prob_ref[h, at, :] = jnp.exp(score_ref[h, at, :] - top).astype(bf16)
            mixed = dotf(turned[h], prob_ref[h])
            total = mixed[HEAD * (1 - h) : HEAD * (1 - h) + 1, :]
            lse_ref[0, h : h + 1, rows] = top + jnp.log(total)
            outs.append(mixed[HEAD * h : HEAD * h + HEAD, :] / total)
        o_ref[rows, :] = jnp.concatenate(outs, 0).T.astype(bf16)


def kv_blocks(groups, first=0):
    half = groups // 2
    return [
        pl.BlockSpec((512, 128), lambda i, s: (0, i + first)),
        pl.BlockSpec((512, 128), lambda i, s: (0, i + first + groups)),
        pl.BlockSpec((512, 128), lambda i, s: (0, (i + first + half) % groups)),
        pl.BlockSpec((512, 128), lambda i, s: (0, (i + first + half) % groups + groups)),
    ]


def attend_forward(info, q, kv, kv_other, window):
    groups = q.shape[1] // 128
    block = pl.BlockSpec((512, 128), lambda i, s: (0, i))
    return pl.pallas_call(
        forward_kernel,
        grid_spec=pltpu.PrefetchScalarGridSpec(
            num_scalar_prefetch=1,
            grid=(groups,),
            in_specs=[
                block,
                *kv_blocks(groups),
                pl.BlockSpec((1, 2, 2, SPAN), lambda i, s: (i, 0, 0, 0)),
            ],
            out_specs=[block, pl.BlockSpec((1, 2, 512), lambda i, s: (i, 0, 0))],
            scratch_shapes=[
                pltpu.VMEM((2, 2, STRIP, 128), f32),
                pltpu.VMEM((2, 1024, 256), f32),
                pltpu.VMEM((2, 1024, 256), bf16),
            ],
        ),
        out_shape=[
            jax.ShapeDtypeStruct((512, 128 * groups), bf16),
            jax.ShapeDtypeStruct((groups, 2, 512), f32),
        ],
        compiler_params=pltpu.CompilerParams(vmem_limit_bytes=24 * MIB),
        cost_estimate=cost(17),
        name="attend_forward",
    )(info, q, kv, kv, kv_other, kv_other, window)


def backward_kernel(with_table, *refs):
    info_ref, q_ref, k_ref, v_ref, ko_ref, vo_ref, do_ref, lse_ref, win_ref = refs[:9]
    dq_ref, dk_ref, dv_ref, dko_ref, dvo_ref, *rest = refs[9:]
    core = info_ref[1]
    *rest, strip_ref, wide_ref, term_ref, prob_ref, grad_ref = rest
    for h in range(2):
        for kind in range(2):
            make_strip(win_ref, h, kind, strip_ref)
    if with_table:
        held_ref, strip_grad_ref = rest
        strip_grad_ref[...] = jnp.zeros_like(strip_grad_ref)
    keys = whole(core, k_ref[...], ko_ref[...])
    values = whole(core, v_ref[...], vo_ref[...])
    keys_turned = keys.T
    key_grad = value_grad = 0.0
    for ib in range(2):
        rows = slice(256 * ib, 256 * ib + 256)
        query = q_ref[rows, :] * jnp.asarray(0.125, bf16)
        grad = do_ref[rows, :]
        query_grads = []
        for h in range(2):
            mask = lane_mask(256, h)
            one = jnp.where(mask, query, jnp.zeros_like(query))
            grad_one = jnp.where(mask, grad, jnp.zeros_like(grad))
            log_total = lse_ref[0, h : h + 1, rows]
            row_term = 0.0
            for kb in range(4):
                kr = slice(256 * kb, 256 * kb + 256)
                raw = dotf(keys[kr], one, NT)
                grad_probs = dotf(values[kr], grad_one, NT)
                for first, at, within in pieces(kb):
                    scores = piece_scores(info_ref, raw[within], strip_ref, h, ib, first)
                    probs = jnp.exp(scores - log_total)
                    term = probs * grad_probs[within]
                    wide_ref[h, at, :] = probs
                    term_ref[h, at, :] = term
                    prob_ref[h, at, :] = probs.astype(bf16)
                    row_term = row_term + jnp.sum(by_eight(term), 0)
            row_term = jnp.sum(row_term, 0, keepdims=True)
            for kb in range(4):
                for first, at, _ in pieces(kb):
                    low = (term_ref[h, at, :] - wide_ref[h, at, :] * row_term).astype(bf16)
                    grad_ref[h, at, :] = low
                    if with_table:
                        for u in (0, 1):
                            tile = 2 * ib + u
                            where = strip_rows(tile, first)
                            part = low[:, 128 * u : 128 * u + 128].astype(f32)
                            strip_grad_ref[h, 0, where, :] += part
                            cross = cross_mask(info_ref, tile, first)
                            if cross is not None:
                                strip_grad_ref[h, 1, where, :] += jnp.where(cross, part, 0.0)
            value_grad = value_grad + dotf(prob_ref[h], grad_one)
            key_grad = key_grad + dotf(grad_ref[h], one)
            flat = dotf(keys_turned, grad_ref[h])
            query_grads.append(flat[HEAD * h : HEAD * h + HEAD, :])
        dq_ref[rows, :] = (jnp.concatenate(query_grads, 0).T * 0.125).astype(bf16)
    for grads, own_ref, other_ref in (
        (key_grad, dk_ref, dko_ref),
        (value_grad, dv_ref, dvo_ref),
    ):
        first, second = grads[:512], grads[512:]
        own_ref[...] = jnp.where(core == 0, first, second)
        other_ref[...] = jnp.where(core == 0, second, first).astype(bf16)
    if with_table:
        for h in range(2):
            for kind in range(2):
                sum_strip(strip_grad_ref, h, kind, held_ref)


def attend_backward(info, q, kv, kv_other, grad, lse, window, with_table, first, count):
    groups = q.shape[1] // 128
    block = pl.BlockSpec((512, 128), lambda i, s: (0, i + first))
    rows = lambda kind: jax.ShapeDtypeStruct((512, 128 * count), kind)
    out_specs = [pl.BlockSpec((512, 128), lambda i, s: (0, i))] * 5
    out_shape = [rows(bf16), rows(f32), rows(f32), rows(bf16), rows(bf16)]
    scratch = [pltpu.VMEM((2, 2, STRIP, 128), f32)]
    if with_table:
        out_specs.append(pl.BlockSpec((1, 2, 2, 8, SPAN), lambda i, s: (i, 0, 0, 0, 0)))
        out_shape.append(jax.ShapeDtypeStruct((count, 2, 2, 8, SPAN), f32))
        scratch = scratch * 2
    scratch += [pltpu.VMEM((2, 1024, 256), f32)] * 2 + [pltpu.VMEM((2, 1024, 256), bf16)] * 2
    return pl.pallas_call(
        functools.partial(backward_kernel, with_table),
        grid_spec=pltpu.PrefetchScalarGridSpec(
            num_scalar_prefetch=1,
            grid=(count,),
            in_specs=[
                block,
                *kv_blocks(groups, first),
                block,
                pl.BlockSpec((1, 2, 512), lambda i, s: (i + first, 0, 0)),
                pl.BlockSpec((1, 2, 2, SPAN), lambda i, s: (i + first, 0, 0, 0)),
            ],
            out_specs=out_specs,
            scratch_shapes=scratch,
        ),
        out_shape=out_shape,
        compiler_params=pltpu.CompilerParams(vmem_limit_bytes=36 * MIB),
        cost_estimate=cost(30),
        name="attend_backward",
    )(info, q, kv, kv, kv_other, kv_other, grad, lse, window)


def norm_parts(values):
    centre = jnp.mean(values, -1, keepdims=True)
    centred = values - centre
    scale = lax.rsqrt(jnp.mean(centred * centred, -1, keepdims=True) + EPS)
    return centred * scale, scale


def norm_back(grad, gain, normal, scale):
    scaled = grad * gain
    return scale * (
        scaled
        - jnp.mean(scaled, -1, keepdims=True)
        - normal * jnp.mean(scaled * normal, -1, keepdims=True)
    )


def normal_cdf(units):
    size = jnp.abs(units)
    t = 1.0 / (1.0 + (0.3275911 * 0.5**0.5) * size)
    bell = jnp.exp(-0.5 * units * units)
    poly = 0.5 * 1.061405429
    for coef in (-1.453152027, 1.421413741, -0.284496736, 0.254829592):
        poly = poly * t + 0.5 * coef
    tail = poly * t * bell
    return jnp.where(units >= 0, 1.0 - tail, tail), bell


def ffn_forward_kernel(
    keep,
    att_ref,
    x_ref,
    out_ref,
    up_ref,
    up_far_ref,
    down_ref,
    down_far_ref,
    bias_ref,
    gain_ref,
    shift_ref,
    result_ref,
    *rest,
):
    if keep:
        (
            low_ref,
            active_ref,
            slope_ref,
            n_one_ref,
            s_one_ref,
            n_two_ref,
            s_two_ref,
            normed_low,
            total,
        ) = rest
    else:
        normed_low, total = rest
    i = pl.program_id(0)

    @pl.when(i == 0)
    def _():
        before = x_ref[...].astype(f32) + (dotf(att_ref[...], out_ref[...]) + shift_ref[0:1, :])
        normal, scale = norm_parts(before)
        normed = normal * gain_ref[0:1, :] + shift_ref[1:2, :]
        normed_low[...] = normed.astype(bf16)
        total[...] = normed + shift_ref[2:3, :]
        if keep:
            n_one_ref[...] = normal
            s_one_ref[...] = scale
            low_ref[...] = normed_low[...]

    near = i < 2
    width = up_ref.shape[2]
    step = 256
    add = None
    for first in range(0, width, step):
        cols = slice(first, first + step)
        up = jnp.where(near, up_ref[0, :, cols], up_far_ref[0, :, cols])
        down = jnp.where(near, down_ref[0, cols, :], down_far_ref[0, cols, :])
        units = dotf(normed_low[...], up) + bias_ref[0, :, cols]
        side, bell = normal_cdf(units)
        active = (units * side).astype(bf16)
        if keep:
            active_ref[:, cols] = active
            slope_ref[:, cols] = (side + units * bell * 0.3989422804014327).astype(bf16)
        part = dotf(active, down)
        add = part if add is None else add + part
    total[...] += add

    @pl.when(i == pl.num_programs(0) - 1)
    def _():
        normal, scale = norm_parts(total[...])
        result = normal * gain_ref[1:2, :] + shift_ref[3:4, :]
        result_ref[...] = result.astype(result_ref.dtype)
        if keep:
            n_two_ref[...] = normal
            s_two_ref[...] = scale


def near_far(rows, cols):
    return [
        pl.BlockSpec((1, rows, cols), lambda i: (jnp.minimum(i, 1), 0, 0)),
        pl.BlockSpec((1, rows, cols), lambda i: (jnp.maximum(i - 2, 0), 0, 0)),
    ]


def ffn_forward(w, attended, inputs, keep, part=0, parts=1):
    rows, model = inputs.shape
    rows //= parts
    width = w["up"][0].shape[2]
    all_of = lambda *shape: pl.BlockSpec(shape, lambda i: (0,) * len(shape))
    by_step = pl.BlockSpec((rows, width), lambda i: (0, i))
    shape = lambda cols, kind: jax.ShapeDtypeStruct((rows, cols), kind)
    out_specs = [all_of(rows, model)]
    out_shape = [shape(model, f32 if keep else bf16)]
    if keep:
        out_specs += [all_of(rows, model), by_step, by_step]
        out_specs += [all_of(rows, model), all_of(rows, 1)] * 2
        out_shape += [shape(model, bf16), shape(4 * width, bf16), shape(4 * width, bf16)]
        out_shape += [shape(model, f32), shape(1, f32)] * 2
    flops = 2 * rows * model * (model + 8 * width)
    return pl.pallas_call(
        functools.partial(ffn_forward_kernel, keep),
        grid=(4,),
        in_specs=[
            pl.BlockSpec((rows, model), lambda i: (part, 0)),
            pl.BlockSpec((rows, model), lambda i: (part, 0)),
            all_of(model, model),
            *near_far(model, width),
            *near_far(width, model),
            pl.BlockSpec((1, 1, width), lambda i: (i, 0, 0)),
            all_of(2, model),
            all_of(4, model),
        ],
        out_specs=out_specs,
        out_shape=out_shape,
        scratch_shapes=[pltpu.VMEM((rows, model), bf16), pltpu.VMEM((rows, model), f32)],
        compiler_params=pltpu.CompilerParams(vmem_limit_bytes=32 * MIB),
        cost_estimate=cost(15),
        name="ffn_forward",
    )(
        attended,
        inputs,
        w["out"],
        *w["up"],
        *w["down"],
        w["up_bias"],
        w["gains"],
        w["shifts"],
    )


def top_back_kernel(gy_ref, n_two_ref, s_two_ref, gain_ref, after_ref, second_ref, sums_ref):
    gy = gy_ref[...].astype(f32)
    after = norm_back(gy, gain_ref[1:2, :], n_two_ref[...], s_two_ref[...])
    low = after.astype(bf16)
    after_ref[...] = after
    second_ref[...] = low
    sums_ref[0:1, :] = jnp.sum(gy * n_two_ref[...], 0, keepdims=True)
    sums_ref[1:2, :] = jnp.sum(low.astype(f32), 0, keepdims=True)
    sums_ref[2:3, :] = jnp.sum(gy, 0, keepdims=True)
    sums_ref[3:8, :] = jnp.zeros((5, sums_ref.shape[1]), f32)


def top_back(w, saved, grad_y):
    rows, model = grad_y.shape
    return pl.pallas_call(
        top_back_kernel,
        out_shape=[
            jax.ShapeDtypeStruct((rows, model), f32),
            jax.ShapeDtypeStruct((rows, model), bf16),
            jax.ShapeDtypeStruct((8, model), f32),
        ],
        compiler_params=pltpu.CompilerParams(vmem_limit_bytes=16 * MIB),
        cost_estimate=cost(2),
        name="top_back",
    )(grad_y, saved["n_two"], saved["s_two"], w["gains"])


def ffn_backward_kernel(deps, *refs):
    (
        after_ref,
        second_ref,
        slope_ref,
        n_one_ref,
        s_one_ref,
        out_ref,
        up_ref,
        up_far_ref,
        down_ref,
        down_far_ref,
        gain_ref,
    ) = refs[:11]
    hidden_ref, before_ref, branch_ref, att_ref, sums_ref, hidden_sums_ref, total = refs[11 + deps :]
    i = pl.program_id(0)

    def add_up(value):
        return jnp.sum(value, 0, keepdims=True)

    @pl.when(i == 0)
    def _():
        total[...] = after_ref[...]

    near = i < 2
    width = up_ref.shape[2]
    step = 256
    add = None
    for first in range(0, width, step):
        cols = slice(first, first + step)
        up = jnp.where(near, up_ref[0, :, cols], up_far_ref[0, :, cols])
        down = jnp.where(near, down_ref[0, cols, :], down_far_ref[0, cols, :])
        active = dotf(second_ref[...], down, NT)
        hidden = (active * slope_ref[:, cols].astype(f32)).astype(bf16)
        hidden_ref[:, cols] = hidden
        hidden_sums_ref[0, :, cols] = add_up(hidden.astype(f32))
        part = dotf(hidden, up, NT)
        add = part if add is None else add + part
    total[...] += add

    @pl.when(i == pl.num_programs(0) - 1)
    def _():
        normed = total[...]
        before = norm_back(normed, gain_ref[0:1, :], n_one_ref[...], s_one_ref[...])
        low = before.astype(bf16)
        before_ref[...] = before
        branch_ref[...] = low
        att_ref[...] = dotf(low, out_ref[...], NT).astype(bf16)
        sums_ref[0:1, :] = add_up(normed * n_one_ref[...])
        sums_ref[1:2, :] = add_up(low.astype(f32))
        sums_ref[2:3, :] = add_up(normed)
        sums_ref[3:8, :] = jnp.zeros((5, sums_ref.shape[1]), f32)


def ffn_backward(w, saved, after, second, deps=()):
    rows, model = after.shape
    width = w["up"][0].shape[2]
    all_of = lambda *shape: pl.BlockSpec(shape, lambda i: (0,) * len(shape))
    by_step = pl.BlockSpec((rows, width), lambda i: (0, i))
    by_block = pl.BlockSpec((1, 1, width), lambda i: (i, 0, 0))
    shape = lambda cols, kind: jax.ShapeDtypeStruct((rows, cols), kind)
    whole_rows = all_of(rows, model)
    return pl.pallas_call(
        functools.partial(ffn_backward_kernel, len(deps)),
        grid=(4,),
        in_specs=[
            whole_rows,
            whole_rows,
            by_step,
            whole_rows,
            all_of(rows, 1),
            all_of(model, model),
            *near_far(model, width),
            *near_far(width, model),
            all_of(2, model),
            *[pl.BlockSpec(memory_space=pl.ANY)] * len(deps),
        ],
        out_specs=[by_step, whole_rows, whole_rows, whole_rows, all_of(8, model), by_block],
        out_shape=[
            shape(4 * width, bf16),
            shape(model, f32),
            shape(model, bf16),
            shape(model, bf16),
            jax.ShapeDtypeStruct((8, model), f32),
            jax.ShapeDtypeStruct((4, 1, width), f32),
        ],
        scratch_shapes=[pltpu.VMEM((rows, model), f32)],
        compiler_params=pltpu.CompilerParams(vmem_limit_bytes=32 * MIB),
        cost_estimate=cost(15),
        name="ffn_backward",
    )(
        after,
        second,
        saved["slope"],
        saved["n_one"],
        saved["s_one"],
        w["out"],
        *w["up"],
        *w["down"],
        w["gains"],
        *deps,
    )


def weight_grad_kernel(l_ref, lo_ref, r_ref, ro_ref, o_ref):
    total = dotf(l_ref[...], r_ref[...], TN) + dotf(lo_ref[...], ro_ref[...], TN)
    o_ref[...] = total.astype(o_ref.dtype)


def weight_grad(left, left_far, right, right_far, kind, left_cols, right_cols):
    rows = left.shape[0]
    lf, ln, lw = left_cols
    rf, rn, rw = right_cols
    return pl.pallas_call(
        weight_grad_kernel,
        grid=(rn, ln),
        in_specs=[
            pl.BlockSpec((rows, lw), lambda j, i: (0, lf + i)),
            pl.BlockSpec((rows, lw), lambda j, i: (0, lf + i)),
            pl.BlockSpec((rows, rw), lambda j, i: (0, rf + j)),
            pl.BlockSpec((rows, rw), lambda j, i: (0, rf + j)),
        ],
        out_specs=pl.BlockSpec((lw, rw), lambda j, i: (i, j)),
        out_shape=jax.ShapeDtypeStruct((ln * lw, rn * rw), kind),
        compiler_params=pltpu.CompilerParams(vmem_limit_bytes=20 * MIB),
        cost_estimate=cost(4),
        name="weight_grad",
    )(left, left_far, right, right_far)


def split_grad_kernel(l_ref, lo_ref, r_ref, ro_ref, kept_ref, sent_ref):
    total = dotf(l_ref[...], r_ref[...], TN) + dotf(lo_ref[...], ro_ref[...], TN)
    half = total.shape[0] // 2
    kept_ref[...] = total[:half].astype(bf16)
    sent_ref[...] = total[half:].astype(bf16)


def split_grad(left, left_far, right, right_far, width):
    rows, model = right.shape
    count = left_far.shape[1] // width
    left_block = pl.BlockSpec((rows, width), lambda i: (0, i))
    right_block = pl.BlockSpec((rows, model), lambda i: (0, 0))
    made = pl.BlockSpec((width // 2, model), lambda i: (i, 0))
    shape = (count * width // 2, model)
    return pl.pallas_call(
        split_grad_kernel,
        grid=(count,),
        in_specs=[left_block, left_block, right_block, right_block],
        out_specs=[made, made],
        out_shape=[jax.ShapeDtypeStruct(shape, bf16)] * 2,
        compiler_params=pltpu.CompilerParams(vmem_limit_bytes=20 * MIB),
        cost_estimate=cost(4),
        name="split_grad",
    )(left, left_far, right, right_far)


IN_VMEM = pl.BlockSpec(memory_space=pltpu.VMEM)


def project_kernel(x_ref, near_ref, far_ref, bias_ref, q_ref, kv_ref):
    inputs = x_ref[...]
    half = near_ref.shape[1]
    for which in range(3):
        for side, ref in enumerate((near_ref, far_ref)):
            made = dotf(inputs, ref[which], NT) + bias_ref[2 * which + side]
            first = half * side + 2 * half * max(which - 1, 0)
            out_ref = kv_ref if which else q_ref
            out_ref[:, first : first + half] = made.astype(bf16)


def project(inputs, near, far, bias):
    rows, model = inputs.shape
    return pl.pallas_call(
        project_kernel,
        in_specs=[IN_VMEM] * 4,
        out_specs=[IN_VMEM] * 2,
        out_shape=[
            jax.ShapeDtypeStruct((rows, model), bf16),
            jax.ShapeDtypeStruct((rows, 2 * model), bf16),
        ],
        compiler_params=pltpu.CompilerParams(vmem_limit_bytes=16 * MIB),
        cost_estimate=cost(4),
        name="project",
    )(inputs, near, far, bias)


def input_back_kernel(*refs):
    q_ref, k_ref, k_came_ref, v_ref, v_came_ref, before_ref, *weights = refs[:8]
    near_ref, far_ref, grad_ref, low_ref, sums_ref = refs[8:]
    half = near_ref.shape[1] // 3
    total = before_ref[...]
    for which in range(3):
        for side in range(2):
            cols = slice(half * side, half * side + half)
            other = slice(half * (1 - side), half * (1 - side) + half)
            if which == 0:
                mixed = q_ref[:, cols]
            else:
                own, came = (k_ref, k_came_ref) if which == 1 else (v_ref, v_came_ref)
                mixed = (own[:, cols] + came[:, other].astype(f32)).astype(bf16)
            (far_ref if side else near_ref)[:, half * which : half * which + half] = mixed
            sums_ref[2 * which + side] = jnp.sum(mixed.astype(f32), 0, keepdims=True)
            total = total + dotf(mixed, weights[side][which])
    grad_ref[...] = total
    low_ref[...] = total.astype(bf16)


def input_back(q, k, k_came, v, v_came, before, near, far):
    rows, model = before.shape
    half = model // 2
    return pl.pallas_call(
        input_back_kernel,
        in_specs=[IN_VMEM] * 8,
        out_specs=[IN_VMEM] * 5,
        out_shape=[
            jax.ShapeDtypeStruct((rows, 3 * half), bf16),
            jax.ShapeDtypeStruct((rows, 3 * half), bf16),
            jax.ShapeDtypeStruct((rows, model), f32),
            jax.ShapeDtypeStruct((rows, model), bf16),
            jax.ShapeDtypeStruct((6, 1, half), f32),
        ],
        compiler_params=pltpu.CompilerParams(vmem_limit_bytes=24 * MIB),
        cost_estimate=cost(6),
        name="input_back",
    )(q, k, k_came, v, v_came, before, near, far)


def body(
    hidden,
    cotangent,
    pair_lengths,
    query_lengths,
    buckets,
    qkv_weight,
    qv_bias,
    out_weight,
    up_weight,
    ffn_bias,
    down_weight,
    norm_gains,
    vectors,
    bias_table,
):
    leading = lax.axis_index("section") == 0
    place = lax.axis_index("tensor")
    y, core = place // 2, place % 2
    plane = lax.axis_index("dp")
    planes = lax.axis_size("dp")
    odd = plane % 2
    local, model = hidden.shape[1], hidden.shape[2]
    total = 4 * local
    cols = qkv_weight.shape[3]
    width = up_weight.shape[2]
    heads = bias_table.shape[1]
    kinds = bias_table.shape[2] // 2
    near, far = slice(0, 2 * cols), slice(2 * cols, 4 * cols)

    def swap_z(value):
        return lax.ppermute(value, "dp", [(i, i ^ 1) for i in range(planes)])

    def mine(array):
        return lax.dynamic_index_in_dim(array, y, 0, keepdims=False)

    def theirs(array):
        return lax.dynamic_index_in_dim(array, 1 - y, 0, keepdims=False)

    def in_order(first, own, came, axis=0):
        return jnp.concatenate(
            [jnp.where(first, own, came), jnp.where(first, came, own)], axis
        )

    def own_half(block, axis=0):
        half = block.shape[axis] // 2
        return lax.dynamic_slice_in_dim(block, half * odd, half, axis)

    def edge_blocks(value):
        return value.reshape(2, local, model)

    def stage(work):
        shapes = jax.eval_shape(work)
        return lax.cond(
            pair_lengths[0] > 0,
            work,
            lambda: jax.tree.map(lambda leaf: jnp.zeros(leaf.shape, leaf.dtype), shapes),
        )

    qkv_own = qkv_weight[0].transpose(1, 2, 0)
    out_own, up_own, down_own = out_weight[0], up_weight[0], down_weight[0]
    small = jnp.concatenate([qv_bias[0].reshape(-1), ffn_bias[0], bias_table[0].reshape(-1)])

    x_sent, qkv_sent = theirs(hidden), own_half(qkv_own, 1)

    def first_stage():
        halves = own_half(out_own), own_half(up_own), own_half(down_own)
        return swap_y(small), swap_y(x_sent), swap_y(qkv_sent), halves

    small_y, x_came, qkv_y, (out_sent, up_sent, down_sent) = stage(first_stage)

    def gather_small():
        two = jnp.stack([small, small_y])
        four = jnp.concatenate([two, swap_c(two)])
        table = four[:, 2 * cols + width :].reshape(8 * heads, kinds)
        turned = lax.dynamic_slice_in_dim(jnp.pad(buckets, (1, 0)), 256 * core, SPAN, 0)
        onehot = (turned[:, None] == jnp.arange(kinds, dtype=jnp.int32)[None, :]).astype(f32)
        window = lax.dot_general(table, onehot, NT, precision=lax.Precision.HIGHEST)
        qv_all = four[:, : 2 * cols].reshape(4, 2, cols)
        q_bias, v_bias = qv_all[:, 0].reshape(-1), qv_all[:, 1].reshape(-1)
        bias = jnp.concatenate([q_bias, jnp.zeros((model,), f32), v_bias])
        info = jnp.stack([mine(query_lengths), core, mine(pair_lengths)]).astype(jnp.int32)
        return (
            window.reshape(2 * heads, 2, 2, SPAN),
            onehot,
            bias.reshape(6, 1, 2 * cols),
            four[:, 2 * cols : 2 * cols + width].reshape(4, 1, width),
            info,
            in_order(y == 0, mine(hidden), x_came),
        )

    def second_stage():
        return swap_z(qkv_y), swap_y(out_sent), swap_y(up_sent), stage(gather_small)

    qkv_z, out_y, up_y, found = stage(second_stage)
    window, onehot, bias, up_bias, info, x0 = found
    w = dict(up_bias=up_bias, gains=norm_gains[0], shifts=vectors[0])

    def gather_qkv():
        near = jnp.concatenate([qkv_own, in_order(odd == 0, qkv_y, qkv_z, 1)], 1)
        far = swap_c(near)
        q, kv = project(x0, near, far, bias)
        return (near, far), q, kv, swap_c(kv)

    def third_stage():
        return stage(gather_qkv), swap_y(down_sent), swap_z(out_y), swap_z(up_y)

    (qkv, q, kv, kv_other), down_y, out_z, up_z = stage(third_stage)
    out = jnp.concatenate([out_own, in_order(odd == 0, out_y, out_z)], 0)
    up = jnp.stack([up_own, in_order(odd == 0, up_y, up_z)])

    def fourth_stage():
        found = stage(lambda: attend_forward(info, q, kv, kv_other, window)[0])
        return swap_z(down_y), swap_c(out), swap_c(up), found

    down_z, out_far, up_far, attended = stage(fourth_stage)
    down = jnp.stack([down_own, in_order(odd == 0, down_y, down_z)])
    w["down"] = down, stage(lambda: swap_c(down))
    w["out"] = jnp.concatenate([out, out_far], 0)
    w["up"] = up, up_far

    def to_next(value):
        return lax.ppermute(value, "section", [(0, 1)])

    def to_last(value):
        return lax.ppermute(value, "section", [(1, 0)])

    middle = ffn_forward(w, attended, x0, False, 0, 2)[0]
    came_a, middle = stage(
        lambda: (to_next(middle), ffn_forward(w, attended, x0, False, 1, 2)[0])
    )
    came_b = stage(lambda: to_next(middle))

    def project_again():
        x1 = jnp.where(leading, x0, jnp.concatenate([came_a, came_b], 0))
        q, kv = project(x1, *qkv, bias)
        return x1, q, kv, swap_c(kv)

    x1, q, kv, kv_other = stage(project_again)
    top_sent = theirs(cotangent)

    def eighth_stage():
        attended, lse = attend_forward(info, q, kv, kv_other, window)
        return swap_y(top_sent), swap_c(x1), attended, lse

    top_came, inputs_far, attended, lse = stage(eighth_stage)
    grad_top = in_order(y == 0, mine(cotangent), top_came)
    result, normed_low, active, slope, n_one, s_one, n_two, s_two = ffn_forward(
        w, attended, x1, True
    )
    saved = dict(slope=slope, n_one=n_one, s_one=s_one, n_two=n_two, s_two=s_two)

    def dense_back(after, second):
        names = ("hidden", "before", "branch", "attended", "low_sums", "hidden_sums")
        return dict(zip(names, ffn_backward(w, saved, after, second)))

    def attention_back(grads, table, first, count):
        return attend_backward(
            info, q, kv, kv_other, grads["attended"], lse, window, table, first, count
        )

    after, second, top_sums = top_back(w, saved, grad_top)

    def ninth_stage():
        return (
            swap_c(normed_low),
            swap_c(active[:, 2 * width :]),
            swap_c(attended[:, far]),
            dense_back(after, second),
        )

    normed_far, active_far, attended_far, grads = stage(ninth_stage)
    grad_q, grad_k, grad_v, k_far, v_far = attention_back(grads, False, 0, 6)

    def to_middle():
        k_came, v_came = swap_c(k_far), swap_c(v_far)
        found = input_back(grad_q, grad_k, k_came, grad_v, v_came, grads["before"], *qkv)
        return to_last(found[3])

    grad_y = jnp.where(leading, stage(to_middle), grad_top)

    thirds = width // 3

    def down_grad(kind, first):
        return weight_grad(
            active, active_far, second, second_far, kind, (first, 3, thirds), (0, 1, model)
        )

    after, second, top_sums = top_back(w, saved, grad_y)
    second_far = stage(lambda: swap_c(second))
    down_sent = down_grad(bf16, 3)

    def through_dense():
        return dense_back(after, second), down_grad(bf16, 0)

    down_came, (grads, down_kept) = stage(lambda: (swap_y(down_sent), stage(through_dense)))
    hidden, branch = grads["hidden"], grads["branch"]
    down = down_kept + down_came

    def exchange_dense():
        return swap_c(hidden[:, 2 * width :]), swap_c(branch)

    def send_dense(hidden_far, branch_far):
        args = normed_low, normed_far, hidden, hidden_far
        sent = weight_grad(*args, bf16, (0, 3, thirds), (1, 1, width))
        return sent, split_grad(attended, attended_far, branch, branch_far, 2 * cols)

    def through_attention(hidden_far):
        args = normed_low, normed_far, hidden, hidden_far
        kept = weight_grad(*args, bf16, (0, 3, thirds), (0, 1, width))
        return attention_back(grads, True, 0, 6), kept

    def through_input(q_grad, k_grad, v_grad, k_far, v_far):
        came = swap_c(k_far), swap_c(v_far)
        near, far, grad_input, grad_low, qv_sums = input_back(
            q_grad, k_grad, came[0], v_grad, came[1], grads["before"], *qkv
        )
        rest_kept, rest_sent = split_grad(near, swap_c(far), x1, inputs_far, 2 * cols)
        return rest_kept, rest_sent, grad_input, grad_low, qv_sums

    def after_down():
        hidden_far, branch_far = stage(exchange_dense)
        up_sent, (out_kept, out_sent) = stage(lambda: send_dense(hidden_far, branch_far))
        up_came, out_came, (found, up_kept) = stage(
            lambda: (
                swap_y(up_sent),
                swap_y(out_sent),
                stage(lambda: through_attention(hidden_far)),
            )
        )
        return found, up_kept + up_came, out_kept + out_came

    def over_planes(value, beside):
        if planes != 4:
            return lax.psum(value, "dp").astype(f32), stage(beside)
        rows = value.shape[0] // 2
        first, second = value[:rows], value[rows:]
        held, sent = jnp.where(odd == 0, first, second), jnp.where(odd == 0, second, first)
        came, found = stage(lambda: (swap_z(sent), stage(beside)))
        held = held + came
        far_planes = [(0, 2), (2, 0), (1, 3), (3, 1)]
        held = held + stage(lambda: lax.ppermute(held, "dp", far_planes))
        return in_order(odd == 0, held, stage(lambda: swap_z(held))).astype(f32), found

    def after_up():
        rest_kept, rest_sent, grad_input, grad_low, qv_sums = stage(
            lambda: through_input(*attention_found)
        )
        def own_sums():
            sums = token_sums(held, qv_sums)
            sums = sums[:2] + swap_c(sums[2:])
            if planes == 4:
                sums = sums + swap_z(sums)
                sums = sums + lax.ppermute(sums, "dp", [(0, 2), (2, 0), (1, 3), (3, 1)])
            else:
                sums = lax.psum(sums, "dp")
            return sums, grad_down.astype(f32)[None]

        rest_came, (sums, down_out) = stage(
            lambda: (swap_y(rest_sent), stage(own_sums))
        )
        rest = rest_kept + rest_came
        grad_qkv, found = over_planes(
            rest, lambda: through_sums(sums, grad_input, grad_low)
        )
        return down_out, grad_qkv.reshape(1, 3, cols, model), found

    def through_sums(sums, grad_input, grad_low):
        edge_low = edge_blocks(jnp.where(leading, grad_low, result.astype(bf16)))
        edge_own = mine(edge_blocks(jnp.where(leading, grad_input, result)))
        edge_came = swap_y(theirs(edge_low)).astype(f32)
        edges = [jnp.where(y == 0, edge_own, edge_came), jnp.where(y == 0, edge_came, edge_own)]
        sums = sums[0] + swap_y(sums[1])
        at = heads * 2 * kinds
        vec_out = sums[at + 2 * cols + width :].reshape(1, 6, share)
        return (
            jnp.stack(edges)[None],
            sums[at : at + 2 * cols].reshape(1, 2, cols),
            sums[at + 2 * cols : at + 2 * cols + width].reshape(1, width),
            vec_out[:, :2],
            vec_out[:, 2:],
            sums[:at].reshape(1, heads, 2 * kinds),
        )

    share = model // 4

    def token_sums(held, qv_sums):
        wide = jnp.pad(held.reshape(4 * heads, 2, 8, SPAN), ((0, 0), (0, 0), (0, 0), (0, 8)))
        sums = sum(wide[:, :, s, s : s + SPAN] for s in range(8))
        sums = jnp.stack([sums[:, 0] - sums[:, 1], sums[:, 1]], 1).reshape(8 * heads, SPAN)
        grad_table = jnp.dot(sums, onehot, precision=lax.Precision.HIGHEST)
        grad_table = grad_table.reshape(4, heads * 2 * kinds)
        q_sums, _, v_sums = qv_sums.reshape(3, 4, cols)
        grad_ffn = grads["hidden_sums"].reshape(4, width)
        low_sums = grads["low_sums"]
        rows = [low_sums[0], top_sums[0], low_sums[1], low_sums[2], top_sums[1], top_sums[2]]
        by_share = jnp.stack(rows).reshape(6, 4, share)
        by_share = by_share.transpose(1, 0, 2).reshape(4, 6 * share)
        by_share = jnp.stack(
            [lax.dynamic_index_in_dim(by_share, place ^ flip, 0, False) for flip in (0, 2, 1, 3)]
        )
        return jnp.concatenate([grad_table, q_sums, v_sums, grad_ffn, by_share], 1)

    grad_down, (found, *later) = stage(lambda: (lax.psum(down, "dp"), stage(after_down)))
    *attention_found, held = found
    (up_out, out_out), (down_out, qkv_out, found) = stage(
        lambda: (lax.psum(later, "dp"), stage(after_up))
    )
    edges, qv_out, ffn_out, gain_out, vec_out, table_out = found
    return (
        edges,
        qkv_out.transpose(0, 3, 1, 2),
        qv_out,
        out_out.astype(f32)[None],
        up_out.astype(f32)[None],
        ffn_out,
        down_out,
        gain_out,
        vec_out,
        table_out,
    )


def solution(mesh):
    return jax.shard_map(
        body,
        mesh=mesh,
        in_specs=(
            P("dp", "tensor", None),
            P("dp", "tensor", None),
            P("dp"),
            P("dp"),
            P(),
            P("section", None, None, "tensor"),
            P("section", None, "tensor"),
            P("section", "tensor", None),
            P("section", None, "tensor"),
            P("section", "tensor"),
            P("section", "tensor", None),
            P("section", None, None),
            P("section", None, None),
            P("section", "tensor", None),
        ),
        out_specs=(
            P("section", "dp", "tensor", None),
            P("section", None, None, "tensor"),
            P("section", None, "tensor"),
            P("section", "tensor", None),
            P("section", None, "tensor"),
            P("section", "tensor"),
            P("section", "tensor", None),
            P("section", None, "tensor"),
            P("section", None, "tensor"),
            P("section", "tensor", None),
        ),
        check_vma=False,
    )
```

```python
import functools

import jax
import jax.numpy as jnp
from jax import lax
from jax.experimental import pallas as pl
from jax.experimental.pallas import tpu as pltpu
from jax.sharding import PartitionSpec as P


f32 = jnp.float32
bf16 = jnp.bfloat16
EPS = 1e-05
HEAD = 64
NEG = -1e30
SWAP_Y = [(0, 2), (2, 0), (1, 3), (3, 1)]
SWAP_C = [(0, 1), (1, 0), (2, 3), (3, 2)]
NT = (((1,), (1,)), ((), ()))
TN = (((0,), (0,)), ((), ()))
NN = (((1,), (0,)), ((), ()))
KEY_BASE = (0, 512, 256, 768)
TILE_BASE = (0, 128, 512, 640)
STRIP = 1664
SPAN = STRIP + 128
PIECE = 32
MIB = 2**20
IN_VMEM = pl.BlockSpec(memory_space=pltpu.VMEM)


def cost(us, flops=0):
    return pl.CostEstimate(flops=flops, bytes_accessed=int(us * 3.4e6), transcendentals=0)


def dotf(a, b, dims=NN):
    return lax.dot_general(a, b, dims, preferred_element_type=f32)


def swap_y(value):
    return lax.ppermute(value, "tensor", SWAP_Y)


def swap_c(value):
    return lax.ppermute(value, "tensor", SWAP_C)


def make_strip(window_ref, h, kind, strip_ref):
    blocks = STRIP // 128
    lane = lax.broadcasted_iota(jnp.int32, (8, 128), 1)
    row = lax.broadcasted_iota(jnp.int32, (8, 128), 0)

    def rolled(first):
        seg = window_ref[0, h, kind : kind + 1, first : first + 128]
        seg = pltpu.roll(jnp.broadcast_to(seg, (8, 128)), 0, 1, stride=1, stride_axis=0)
        return [pltpu.roll(seg, 8 * q, 1) if q else seg for q in range(16)]

    high = rolled(128 * blocks)
    for a in range(blocks):
        low = rolled(128 * (blocks - 1 - a))
        for q in range(16):
            rows = slice(128 * a + 8 * q, 128 * a + 8 * q + 8)
            strip_ref[h, kind, rows, :] = jnp.where(lane >= row + 8 * q, high[q], low[q])
        high = low


def sum_strip(strip_ref, h, kind, held_ref):
    blocks = STRIP // 128
    lane = lax.broadcasted_iota(jnp.int32, (8, 128), 1)
    carry = jnp.zeros((8, 128), f32)
    for a in reversed(range(blocks)):
        low, high = jnp.zeros((8, 128), f32), jnp.zeros((8, 128), f32)
        for q in range(16):
            part = strip_ref[h, kind, 128 * a + 8 * q : 128 * a + 8 * q + 8, :]
            if q:
                part = pltpu.roll(part, 128 - 8 * q, 1)
            stays = lane < 128 - 8 * q
            high += jnp.where(stays, part, 0.0)
            low += jnp.where(stays, 0.0, part)
        first = 128 * (blocks - 1 - a)
        held_ref[0, h, kind, :, first : first + 128] = low + carry
        carry = high
    held_ref[0, h, kind, :, 128 * blocks : 128 * blocks + 128] = carry


def lane_mask(rows, which):
    lane = lax.broadcasted_iota(jnp.int32, (rows, 128), 1)
    return (lane < HEAD) if which == 0 else (lane >= HEAD)


def cross_mask(info_ref, tile, first):
    key_low = first < 256
    row_low = tile < 2
    if not key_low and not row_low:
        return None
    qlen, core = info_ref[0], info_ref[1]
    shape = (PIECE, 128)
    if row_low:
        row = 256 * core + 128 * tile + lax.broadcasted_iota(jnp.int32, shape, 1)
        row_side = row < qlen
    if key_low:
        key_side = first + lax.broadcasted_iota(jnp.int32, shape, 0) < qlen
    if row_low and key_low:
        return row_side != key_side
    return row_side if row_low else key_side


def pieces(kb):
    for at in range(0, 256, PIECE):
        yield KEY_BASE[kb] + at, slice(256 * kb + at, 256 * kb + at + PIECE), slice(at, at + PIECE)


def strip_rows(tile, first):
    start = first - TILE_BASE[tile] + 640
    return slice(start, start + PIECE)


def piece_scores(info_ref, raw, strip_ref, h, ib, first):
    parts = []
    for u in (0, 1):
        tile = 2 * ib + u
        rows = strip_rows(tile, first)
        bias = strip_ref[h, 0, rows, :]
        cross = cross_mask(info_ref, tile, first)
        if cross is not None:
            bias = jnp.where(cross, strip_ref[h, 1, rows, :], bias)
        parts.append(raw[:, 128 * u : 128 * u + 128] + bias)
    scores = jnp.concatenate(parts, 1)
    if first >= 256:
        live = first + lax.broadcasted_iota(jnp.int32, (PIECE, 256), 0) < info_ref[2]
        scores = jnp.where(live, scores, NEG)
    return scores


def by_eight(value):
    return value.reshape(PIECE // 8, 8, 256)


def whole(core, own, other):
    return jnp.concatenate([jnp.where(core == 0, own, other), jnp.where(core == 0, other, own)], 0)


def forward_kernel(
    info_ref,
    q_ref,
    k_ref,
    v_ref,
    ko_ref,
    vo_ref,
    win_ref,
    o_ref,
    lse_ref,
    strip_ref,
    score_ref,
    prob_ref,
):
    core = info_ref[1]
    for h in range(2):
        for kind in range(2):
            make_strip(win_ref, h, kind, strip_ref)
    keys = whole(core, k_ref[...], ko_ref[...])
    values = whole(core, v_ref[...], vo_ref[...])
    one = jnp.ones_like(values)
    turned = [jnp.where(lane_mask(1024, h), values, one).T for h in range(2)]
    for ib in range(2):
        rows = slice(256 * ib, 256 * ib + 256)
        query = q_ref[rows, :] * jnp.asarray(0.125, bf16)
        outs = []
        for h in range(2):
            one = jnp.where(lane_mask(256, h), query, jnp.zeros_like(query))
            top = None
            for kb in range(4):
                raw = dotf(keys[256 * kb : 256 * kb + 256], one, NT)
                for first, at, within in pieces(kb):
                    scores = piece_scores(info_ref, raw[within], strip_ref, h, ib, first)
                    score_ref[h, at, :] = scores
                    most = jnp.max(by_eight(scores), 0)
                    top = most if top is None else jnp.maximum(top, most)
            top = jnp.max(top, 0, keepdims=True)
            for kb in range(4):
                for _, at, _ in pieces(kb):
                    prob_ref[h, at, :] = jnp.exp(score_ref[h, at, :] - top).astype(bf16)
            mixed = dotf(turned[h], prob_ref[h])
            total = mixed[HEAD * (1 - h) : HEAD * (1 - h) + 1, :]
            lse_ref[0, h : h + 1, rows] = top + jnp.log(total)
            outs.append(mixed[HEAD * h : HEAD * h + HEAD, :] / total)
        o_ref[rows, :] = jnp.concatenate(outs, 0).T.astype(bf16)


def kv_blocks(groups, first=0):
    half = groups // 2
    return [
        pl.BlockSpec((512, 128), lambda i, s: (0, i + first)),
        pl.BlockSpec((512, 128), lambda i, s: (0, i + first + groups)),
        pl.BlockSpec((512, 128), lambda i, s: (0, (i + first + half) % groups)),
        pl.BlockSpec((512, 128), lambda i, s: (0, (i + first + half) % groups + groups)),
    ]


def attend_forward(info, q, kv, kv_other, window):
    groups = q.shape[1] // 128
    block = pl.BlockSpec((512, 128), lambda i, s: (0, i))
    return pl.pallas_call(
        forward_kernel,
        grid_spec=pltpu.PrefetchScalarGridSpec(
            num_scalar_prefetch=1,
            grid=(groups,),
            in_specs=[
                block,
                *kv_blocks(groups),
                pl.BlockSpec((1, 2, 2, SPAN), lambda i, s: (i, 0, 0, 0)),
            ],
            out_specs=[block, pl.BlockSpec((1, 2, 512), lambda i, s: (i, 0, 0))],
            scratch_shapes=[
                pltpu.VMEM((2, 2, STRIP, 128), f32),
                pltpu.VMEM((2, 1024, 256), f32),
                pltpu.VMEM((2, 1024, 256), bf16),
            ],
        ),
        out_shape=[
            jax.ShapeDtypeStruct((512, 128 * groups), bf16),
            jax.ShapeDtypeStruct((groups, 2, 512), f32),
        ],
        compiler_params=pltpu.CompilerParams(vmem_limit_bytes=24 * MIB),
        cost_estimate=cost(17),
        name="attend_forward",
    )(info, q, kv, kv, kv_other, kv_other, window)


def backward_kernel(with_table, *refs):
    info_ref, q_ref, k_ref, v_ref, ko_ref, vo_ref, do_ref, lse_ref, win_ref = refs[:9]
    dq_ref, dk_ref, dv_ref, dko_ref, dvo_ref, *rest = refs[9:]
    core = info_ref[1]
    *rest, strip_ref, wide_ref, term_ref, prob_ref, grad_ref = rest
    for h in range(2):
        for kind in range(2):
            make_strip(win_ref, h, kind, strip_ref)
    if with_table:
        held_ref, strip_grad_ref = rest
        strip_grad_ref[...] = jnp.zeros_like(strip_grad_ref)
    keys = whole(core, k_ref[...], ko_ref[...])
    values = whole(core, v_ref[...], vo_ref[...])
    keys_turned = keys.T
    key_grad = value_grad = 0.0
    for ib in range(2):
        rows = slice(256 * ib, 256 * ib + 256)
        query = q_ref[rows, :] * jnp.asarray(0.125, bf16)
        grad = do_ref[rows, :]
        query_grads = []
        for h in range(2):
            mask = lane_mask(256, h)
            one = jnp.where(mask, query, jnp.zeros_like(query))
            grad_one = jnp.where(mask, grad, jnp.zeros_like(grad))
            log_total = lse_ref[0, h : h + 1, rows]
            row_term = 0.0
            for kb in range(4):
                kr = slice(256 * kb, 256 * kb + 256)
                raw = dotf(keys[kr], one, NT)
                grad_probs = dotf(values[kr], grad_one, NT)
                for first, at, within in pieces(kb):
                    scores = piece_scores(info_ref, raw[within], strip_ref, h, ib, first)
                    probs = jnp.exp(scores - log_total)
                    term = probs * grad_probs[within]
                    wide_ref[h, at, :] = probs
                    term_ref[h, at, :] = term
                    prob_ref[h, at, :] = probs.astype(bf16)
                    row_term = row_term + jnp.sum(by_eight(term), 0)
            row_term = jnp.sum(row_term, 0, keepdims=True)
            for kb in range(4):
                for first, at, _ in pieces(kb):
                    low = (term_ref[h, at, :] - wide_ref[h, at, :] * row_term).astype(bf16)
                    grad_ref[h, at, :] = low
                    if with_table:
                        for u in (0, 1):
                            tile = 2 * ib + u
                            where = strip_rows(tile, first)
                            part = low[:, 128 * u : 128 * u + 128].astype(f32)
                            strip_grad_ref[h, 0, where, :] += part
                            cross = cross_mask(info_ref, tile, first)
                            if cross is not None:
                                strip_grad_ref[h, 1, where, :] += jnp.where(cross, part, 0.0)
            value_grad = value_grad + dotf(prob_ref[h], grad_one)
            key_grad = key_grad + dotf(grad_ref[h], one)
            flat = dotf(keys_turned, grad_ref[h])
            query_grads.append(flat[HEAD * h : HEAD * h + HEAD, :])
        dq_ref[rows, :] = (jnp.concatenate(query_grads, 0).T * 0.125).astype(bf16)
    for grads, own_ref, other_ref in (
        (key_grad, dk_ref, dko_ref),
        (value_grad, dv_ref, dvo_ref),
    ):
        first, second = grads[:512], grads[512:]
        own_ref[...] = jnp.where(core == 0, first, second)
        other_ref[...] = jnp.where(core == 0, second, first).astype(bf16)
    if with_table:
        for h in range(2):
            for kind in range(2):
                sum_strip(strip_grad_ref, h, kind, held_ref)


def attend_backward(info, q, kv, kv_other, grad, lse, window, with_table, first, count):
    groups = q.shape[1] // 128
    block = pl.BlockSpec((512, 128), lambda i, s: (0, i + first))
    rows = lambda kind: jax.ShapeDtypeStruct((512, 128 * count), kind)
    out_specs = [pl.BlockSpec((512, 128), lambda i, s: (0, i))] * 5
    out_shape = [rows(bf16), rows(f32), rows(f32), rows(bf16), rows(bf16)]
    scratch = [pltpu.VMEM((2, 2, STRIP, 128), f32)]
    if with_table:
        out_specs.append(pl.BlockSpec((1, 2, 2, 8, SPAN), lambda i, s: (i, 0, 0, 0, 0)))
        out_shape.append(jax.ShapeDtypeStruct((count, 2, 2, 8, SPAN), f32))
        scratch = scratch * 2
    scratch += [pltpu.VMEM((2, 1024, 256), f32)] * 2 + [pltpu.VMEM((2, 1024, 256), bf16)] * 2
    return pl.pallas_call(
        functools.partial(backward_kernel, with_table),
        grid_spec=pltpu.PrefetchScalarGridSpec(
            num_scalar_prefetch=1,
            grid=(count,),
            in_specs=[
                block,
                *kv_blocks(groups, first),
                block,
                pl.BlockSpec((1, 2, 512), lambda i, s: (i + first, 0, 0)),
                pl.BlockSpec((1, 2, 2, SPAN), lambda i, s: (i + first, 0, 0, 0)),
            ],
            out_specs=out_specs,
            scratch_shapes=scratch,
        ),
        out_shape=out_shape,
        compiler_params=pltpu.CompilerParams(vmem_limit_bytes=36 * MIB),
        cost_estimate=cost(30),
        name="attend_backward",
    )(info, q, kv, kv, kv_other, kv_other, grad, lse, window)


def norm_parts(values):
    centre = jnp.mean(values, -1, keepdims=True)
    centred = values - centre
    scale = lax.rsqrt(jnp.mean(centred * centred, -1, keepdims=True) + EPS)
    return centred * scale, scale


def norm_back(grad, gain, normal, scale):
    scaled = grad * gain
    return scale * (
        scaled
        - jnp.mean(scaled, -1, keepdims=True)
        - normal * jnp.mean(scaled * normal, -1, keepdims=True)
    )


def normal_cdf(units):
    size = jnp.abs(units)
    t = 1.0 / (1.0 + (0.3275911 * 0.5**0.5) * size)
    bell = jnp.exp(-0.5 * units * units)
    poly = 0.5 * 1.061405429
    for coef in (-1.453152027, 1.421413741, -0.284496736, 0.254829592):
        poly = poly * t + 0.5 * coef
    tail = poly * t * bell
    return jnp.where(units >= 0, 1.0 - tail, tail), bell


def ffn_forward_kernel(
    keep,
    att_ref,
    x_ref,
    out_ref,
    up_ref,
    up_far_ref,
    down_ref,
    down_far_ref,
    bias_ref,
    gain_ref,
    shift_ref,
    result_ref,
    *rest,
):
    if keep:
        (
            low_ref,
            active_ref,
            slope_ref,
            n_one_ref,
            s_one_ref,
            n_two_ref,
            s_two_ref,
            normed_low,
            total,
        ) = rest
    else:
        normed_low, total = rest
    i = pl.program_id(0)

    @pl.when(i == 0)
    def _():
        before = x_ref[...].astype(f32) + (dotf(att_ref[...], out_ref[...]) + shift_ref[0:1, :])
        normal, scale = norm_parts(before)
        normed = normal * gain_ref[0:1, :] + shift_ref[1:2, :]
        normed_low[...] = normed.astype(bf16)
        total[...] = normed + shift_ref[2:3, :]
        if keep:
            n_one_ref[...] = normal
            s_one_ref[...] = scale
            low_ref[...] = normed_low[...]

    near = i < 2
    width = up_ref.shape[2]
    step = 256
    add = None
    for first in range(0, width, step):
        cols = slice(first, first + step)
        up = jnp.where(near, up_ref[0, :, cols], up_far_ref[0, :, cols])
        down = jnp.where(near, down_ref[0, cols, :], down_far_ref[0, cols, :])
        units = dotf(normed_low[...], up) + bias_ref[0, :, cols]
        side, bell = normal_cdf(units)
        active = (units * side).astype(bf16)
        if keep:
            active_ref[:, cols] = active
            slope_ref[:, cols] = (side + units * bell * 0.3989422804014327).astype(bf16)
        part = dotf(active, down)
        add = part if add is None else add + part
    total[...] += add

    @pl.when(i == pl.num_programs(0) - 1)
    def _():
        normal, scale = norm_parts(total[...])
        result = normal * gain_ref[1:2, :] + shift_ref[3:4, :]
        result_ref[...] = result.astype(result_ref.dtype)
        if keep:
            n_two_ref[...] = normal
            s_two_ref[...] = scale


def near_far(rows, cols):
    return [
        pl.BlockSpec((1, rows, cols), lambda i: (jnp.minimum(i, 1), 0, 0)),
        pl.BlockSpec((1, rows, cols), lambda i: (jnp.maximum(i - 2, 0), 0, 0)),
    ]


def ffn_forward(w, attended, inputs, keep, part=0, parts=1):
    rows, model = inputs.shape
    rows //= parts
    width = w["up"][0].shape[2]
    all_of = lambda *shape: pl.BlockSpec(shape, lambda i: (0,) * len(shape))
    by_step = pl.BlockSpec((rows, width), lambda i: (0, i))
    shape = lambda cols, kind: jax.ShapeDtypeStruct((rows, cols), kind)
    out_specs = [all_of(rows, model)]
    out_shape = [shape(model, f32 if keep else bf16)]
    if keep:
        out_specs += [all_of(rows, model), by_step, by_step]
        out_specs += [all_of(rows, model), all_of(rows, 1)] * 2
        out_shape += [shape(model, bf16), shape(4 * width, bf16), shape(4 * width, bf16)]
        out_shape += [shape(model, f32), shape(1, f32)] * 2
    flops = 2 * rows * model * (model + 8 * width)
    return pl.pallas_call(
        functools.partial(ffn_forward_kernel, keep),
        grid=(4,),
        in_specs=[
            pl.BlockSpec((rows, model), lambda i: (part, 0)),
            pl.BlockSpec((rows, model), lambda i: (part, 0)),
            all_of(model, model),
            *near_far(model, width),
            *near_far(width, model),
            pl.BlockSpec((1, 1, width), lambda i: (i, 0, 0)),
            all_of(2, model),
            all_of(4, model),
        ],
        out_specs=out_specs,
        out_shape=out_shape,
        scratch_shapes=[pltpu.VMEM((rows, model), bf16), pltpu.VMEM((rows, model), f32)],
        compiler_params=pltpu.CompilerParams(vmem_limit_bytes=32 * MIB),
        cost_estimate=cost(15),
        name="ffn_forward",
    )(
        attended,
        inputs,
        w["out"],
        *w["up"],
        *w["down"],
        w["up_bias"],
        w["gains"],
        w["shifts"],
    )


def top_back_kernel(
    first_ref, came_ref, gy_ref, n_two_ref, s_two_ref, gain_ref, after_ref, second_ref, sums_ref
):
    gy = jnp.where(first_ref[0] == 1, came_ref[...], gy_ref[...]).astype(f32)
    after = norm_back(gy, gain_ref[1:2, :], n_two_ref[...], s_two_ref[...])
    low = after.astype(bf16)
    after_ref[...] = after
    second_ref[...] = low
    sums_ref[0:1, :] = jnp.sum(gy * n_two_ref[...], 0, keepdims=True)
    sums_ref[1:2, :] = jnp.sum(low.astype(f32), 0, keepdims=True)
    sums_ref[2:3, :] = jnp.sum(gy, 0, keepdims=True)
    sums_ref[3:8, :] = jnp.zeros((5, sums_ref.shape[1]), f32)


def top_back(w, saved, first_layer, came, grad_y):
    rows, model = grad_y.shape
    return pl.pallas_call(
        top_back_kernel,
        in_specs=[pl.BlockSpec(memory_space=pltpu.SMEM), *[IN_VMEM] * 5],
        out_specs=[IN_VMEM] * 3,
        out_shape=[
            jax.ShapeDtypeStruct((rows, model), f32),
            jax.ShapeDtypeStruct((rows, model), bf16),
            jax.ShapeDtypeStruct((8, model), f32),
        ],
        compiler_params=pltpu.CompilerParams(vmem_limit_bytes=16 * MIB),
        cost_estimate=cost(2),
        name="top_back",
    )(first_layer, came, grad_y, saved["n_two"], saved["s_two"], w["gains"])


def ffn_backward_kernel(deps, *refs):
    (
        after_ref,
        second_ref,
        slope_ref,
        n_one_ref,
        s_one_ref,
        out_ref,
        up_ref,
        up_far_ref,
        down_ref,
        down_far_ref,
        gain_ref,
    ) = refs[:11]
    hidden_ref, before_ref, branch_ref, att_ref, sums_ref, hidden_sums_ref, total = refs[11 + deps :]
    i = pl.program_id(0)

    def add_up(value):
        return jnp.sum(value, 0, keepdims=True)

    @pl.when(i == 0)
    def _():
        total[...] = after_ref[...]

    near = i < 2
    width = up_ref.shape[2]
    step = 256
    add = None
    for first in range(0, width, step):
        cols = slice(first, first + step)
        up = jnp.where(near, up_ref[0, :, cols], up_far_ref[0, :, cols])
        down = jnp.where(near, down_ref[0, cols, :], down_far_ref[0, cols, :])
        active = dotf(second_ref[...], down, NT)
        hidden = (active * slope_ref[:, cols].astype(f32)).astype(bf16)
        hidden_ref[:, cols] = hidden
        hidden_sums_ref[0, :, cols] = add_up(hidden.astype(f32))
        part = dotf(hidden, up, NT)
        add = part if add is None else add + part
    total[...] += add

    @pl.when(i == pl.num_programs(0) - 1)
    def _():
        normed = total[...]
        before = norm_back(normed, gain_ref[0:1, :], n_one_ref[...], s_one_ref[...])
        low = before.astype(bf16)
        before_ref[...] = before
        branch_ref[...] = low
        att_ref[...] = dotf(low, out_ref[...], NT).astype(bf16)
        sums_ref[0:1, :] = add_up(normed * n_one_ref[...])
        sums_ref[1:2, :] = add_up(low.astype(f32))
        sums_ref[2:3, :] = add_up(normed)
        sums_ref[3:8, :] = jnp.zeros((5, sums_ref.shape[1]), f32)


def ffn_backward(w, saved, after, second, deps=()):
    rows, model = after.shape
    width = w["up"][0].shape[2]
    all_of = lambda *shape: pl.BlockSpec(shape, lambda i: (0,) * len(shape))
    by_step = pl.BlockSpec((rows, width), lambda i: (0, i))
    by_block = pl.BlockSpec((1, 1, width), lambda i: (i, 0, 0))
    shape = lambda cols, kind: jax.ShapeDtypeStruct((rows, cols), kind)
    whole_rows = all_of(rows, model)
    return pl.pallas_call(
        functools.partial(ffn_backward_kernel, len(deps)),
        grid=(4,),
        in_specs=[
            whole_rows,
            whole_rows,
            by_step,
            whole_rows,
            all_of(rows, 1),
            all_of(model, model),
            *near_far(model, width),
            *near_far(width, model),
            all_of(2, model),
            *[pl.BlockSpec(memory_space=pl.ANY)] * len(deps),
        ],
        out_specs=[by_step, whole_rows, whole_rows, whole_rows, all_of(8, model), by_block],
        out_shape=[
            shape(4 * width, bf16),
            shape(model, f32),
            shape(model, bf16),
            shape(model, bf16),
            jax.ShapeDtypeStruct((8, model), f32),
            jax.ShapeDtypeStruct((4, 1, width), f32),
        ],
        scratch_shapes=[pltpu.VMEM((rows, model), f32)],
        compiler_params=pltpu.CompilerParams(vmem_limit_bytes=32 * MIB),
        cost_estimate=cost(15),
        name="ffn_backward",
    )(
        after,
        second,
        saved["slope"],
        saved["n_one"],
        saved["s_one"],
        w["out"],
        *w["up"],
        *w["down"],
        w["gains"],
        *deps,
    )


def weight_grad_kernel(l_ref, lo_ref, r_ref, ro_ref, o_ref):
    total = dotf(l_ref[...], r_ref[...], TN) + dotf(lo_ref[...], ro_ref[...], TN)
    o_ref[...] = total.astype(o_ref.dtype)


def weight_grad(left, left_far, right, right_far, kind, left_cols, right_cols):
    rows = left.shape[0]
    lf, ln, lw = left_cols
    rf, rn, rw = right_cols
    return pl.pallas_call(
        weight_grad_kernel,
        grid=(rn, ln),
        in_specs=[
            pl.BlockSpec((rows, lw), lambda j, i: (0, lf + i)),
            pl.BlockSpec((rows, lw), lambda j, i: (0, lf + i)),
            pl.BlockSpec((rows, rw), lambda j, i: (0, rf + j)),
            pl.BlockSpec((rows, rw), lambda j, i: (0, rf + j)),
        ],
        out_specs=pl.BlockSpec((lw, rw), lambda j, i: (i, j)),
        out_shape=jax.ShapeDtypeStruct((ln * lw, rn * rw), kind),
        compiler_params=pltpu.CompilerParams(vmem_limit_bytes=20 * MIB),
        cost_estimate=cost(4),
        name="weight_grad",
    )(left, left_far, right, right_far)


def split_grad_kernel(l_ref, lo_ref, r_ref, ro_ref, kept_ref, sent_ref):
    total = dotf(l_ref[...], r_ref[...], TN) + dotf(lo_ref[...], ro_ref[...], TN)
    half = total.shape[0] // 2
    kept_ref[...] = total[:half].astype(bf16)
    sent_ref[...] = total[half:].astype(bf16)


def split_grad(left, left_far, right, right_far, width):
    rows, model = right.shape
    count = left_far.shape[1] // width
    left_block = pl.BlockSpec((rows, width), lambda i: (0, i))
    right_block = pl.BlockSpec((rows, model), lambda i: (0, 0))
    made = pl.BlockSpec((width // 2, model), lambda i: (i, 0))
    shape = (count * width // 2, model)
    return pl.pallas_call(
        split_grad_kernel,
        grid=(count,),
        in_specs=[left_block, left_block, right_block, right_block],
        out_specs=[made, made],
        out_shape=[jax.ShapeDtypeStruct(shape, bf16)] * 2,
        compiler_params=pltpu.CompilerParams(vmem_limit_bytes=20 * MIB),
        cost_estimate=cost(4),
        name="split_grad",
    )(left, left_far, right, right_far)


def project_kernel(x_ref, near_ref, far_ref, bias_ref, *refs):
    inputs = x_ref[...]
    *refs, q_ref, kv_ref = refs
    if refs:
        keep_ref, a_ref, b_ref, x1_ref = refs
        inputs = jnp.where(keep_ref[0] == 1, inputs, jnp.concatenate([a_ref[...], b_ref[...]], 0))
        x1_ref[...] = inputs
    half = near_ref.shape[1]
    for which in range(3):
        weight = jnp.concatenate([near_ref[which], far_ref[which]], 0)
        bias = jnp.concatenate([bias_ref[2 * which], bias_ref[2 * which + 1]], 1)
        made = (dotf(inputs, weight, NT) + bias).astype(bf16)
        if which == 0:
            q_ref[...] = made
        else:
            kv_ref[:, 2 * half * (which - 1) : 2 * half * which] = made


def project(inputs, near, far, bias, *instead):
    rows, model = inputs.shape
    shapes = [(rows, model)] * (2 if instead else 1) + [(rows, 2 * model)]
    extra = [pl.BlockSpec(memory_space=pltpu.SMEM), IN_VMEM, IN_VMEM] if instead else []
    return pl.pallas_call(
        project_kernel,
        in_specs=[IN_VMEM] * 4 + extra,
        out_specs=[IN_VMEM] * len(shapes),
        out_shape=[jax.ShapeDtypeStruct(shape, bf16) for shape in shapes],
        compiler_params=pltpu.CompilerParams(vmem_limit_bytes=20 * MIB),
        cost_estimate=cost(4),
        name="project",
    )(inputs, near, far, bias, *instead)


def input_back_kernel(*refs):
    q_ref, k_ref, k_came_ref, v_ref, v_came_ref, before_ref, *weights = refs[:8]
    near_ref, far_ref, grad_ref, low_ref, sums_ref = refs[8:]
    half = near_ref.shape[1] // 3
    total = before_ref[...]
    for which in range(3):
        if which == 0:
            mixed = q_ref[...]
        else:
            own, came = (k_ref, k_came_ref) if which == 1 else (v_ref, v_came_ref)
            other = jnp.concatenate([came[:, half:], came[:, :half]], 1)
            mixed = (own[...] + other.astype(f32)).astype(bf16)
        near_ref[:, half * which : half * which + half] = mixed[:, :half]
        far_ref[:, half * which : half * which + half] = mixed[:, half:]
        sums = jnp.sum(mixed.astype(f32), 0, keepdims=True)
        sums_ref[2 * which] = sums[:, :half]
        sums_ref[2 * which + 1] = sums[:, half:]
        weight = jnp.concatenate([weights[0][which], weights[1][which]], 0)
        total = total + dotf(mixed, weight)
    grad_ref[...] = total
    low_ref[...] = total.astype(bf16)


def input_back(q, k, k_came, v, v_came, before, near, far):
    rows, model = before.shape
    half = model // 2
    return pl.pallas_call(
        input_back_kernel,
        in_specs=[IN_VMEM] * 8,
        out_specs=[IN_VMEM] * 5,
        out_shape=[
            jax.ShapeDtypeStruct((rows, 3 * half), bf16),
            jax.ShapeDtypeStruct((rows, 3 * half), bf16),
            jax.ShapeDtypeStruct((rows, model), f32),
            jax.ShapeDtypeStruct((rows, model), bf16),
            jax.ShapeDtypeStruct((6, 1, half), f32),
        ],
        compiler_params=pltpu.CompilerParams(vmem_limit_bytes=24 * MIB),
        cost_estimate=cost(6),
        name="input_back",
    )(q, k, k_came, v, v_came, before, near, far)


def body(
    hidden,
    cotangent,
    pair_lengths,
    query_lengths,
    buckets,
    qkv_weight,
    qv_bias,
    out_weight,
    up_weight,
    ffn_bias,
    down_weight,
    norm_gains,
    vectors,
    bias_table,
):
    leading = lax.axis_index("section") == 0
    place = lax.axis_index("tensor")
    y, core = place // 2, place % 2
    plane = lax.axis_index("dp")
    planes = lax.axis_size("dp")
    odd = plane % 2
    local, model = hidden.shape[1], hidden.shape[2]
    total = 4 * local
    cols = qkv_weight.shape[3]
    width = up_weight.shape[2]
    heads = bias_table.shape[1]
    kinds = bias_table.shape[2] // 2
    near, far = slice(0, 2 * cols), slice(2 * cols, 4 * cols)

    def swap_z(value):
        return lax.ppermute(value, "dp", [(i, i ^ 1) for i in range(planes)])

    def mine(array):
        return lax.dynamic_index_in_dim(array, y, 0, keepdims=False)

    def theirs(array):
        return lax.dynamic_index_in_dim(array, 1 - y, 0, keepdims=False)

    def in_order(first, own, came, axis=0):
        return jnp.concatenate(
            [jnp.where(first, own, came), jnp.where(first, came, own)], axis
        )

    def own_half(block, axis=0):
        half = block.shape[axis] // 2
        return lax.dynamic_slice_in_dim(block, half * odd, half, axis)

    def edge_blocks(value):
        return value.reshape(2, local, model)

    def stage(work):
        shapes = jax.eval_shape(work)
        return lax.cond(
            pair_lengths[0] > 0,
            work,
            lambda: jax.tree.map(lambda leaf: jnp.zeros(leaf.shape, leaf.dtype), shapes),
        )

    qkv_own = qkv_weight[0].transpose(1, 2, 0)
    out_own, up_own, down_own = out_weight[0], up_weight[0], down_weight[0]
    small = jnp.concatenate([qv_bias[0].reshape(-1), ffn_bias[0], bias_table[0].reshape(-1)])

    x_sent, qkv_sent = theirs(hidden), own_half(qkv_own, 1)

    def first_stage():
        halves = own_half(out_own), own_half(up_own), own_half(down_own)
        return swap_y(small), swap_y(x_sent), swap_y(qkv_sent), halves

    small_y, x_came, qkv_y, (out_sent, up_sent, down_sent) = stage(first_stage)

    def gather_small():
        two = jnp.stack([small, small_y])
        four = jnp.concatenate([two, swap_c(two)])
        table = four[:, 2 * cols + width :].reshape(8 * heads, kinds)
        kind = jnp.pad(buckets, (1, 0))
        kind = lax.dynamic_slice_in_dim(kind, 256 * core, SPAN, 0)
        kind = jnp.stack([jnp.pad(kind, (s, 0), constant_values=-1)[:SPAN] for s in range(8)])
        kind = kind.reshape(1, 8 * SPAN)
        onehot = (kind == jnp.arange(kinds, dtype=jnp.int32)[:, None]).astype(bf16)
        window = jnp.dot(
            table, onehot[:, :SPAN].astype(f32), precision=lax.Precision.HIGHEST
        )
        qv_all = four[:, : 2 * cols].reshape(4, 2, cols)
        q_bias, v_bias = qv_all[:, 0].reshape(-1), qv_all[:, 1].reshape(-1)
        bias = jnp.concatenate([q_bias, jnp.zeros((model,), f32), v_bias])
        info = jnp.stack([mine(query_lengths), core, mine(pair_lengths)]).astype(jnp.int32)
        return (
            window.reshape(2 * heads, 2, 2, SPAN),
            onehot,
            bias.reshape(6, 1, 2 * cols),
            four[:, 2 * cols : 2 * cols + width].reshape(4, 1, width),
            info,
            in_order(y == 0, mine(hidden), x_came),
        )

    def second_stage():
        return swap_z(qkv_y), swap_y(out_sent), swap_y(up_sent), stage(gather_small)

    qkv_z, out_y, up_y, found = stage(second_stage)
    window, onehot, bias, up_bias, info, x0 = found
    w = dict(up_bias=up_bias, gains=norm_gains[0], shifts=vectors[0])

    def gather_qkv():
        near = jnp.concatenate([qkv_own, in_order(odd == 0, qkv_y, qkv_z, 1)], 1)
        far = swap_c(near)
        q, kv = project(x0, near, far, bias)
        return (near, far), q, kv, swap_c(kv)

    def third_stage():
        return stage(gather_qkv), swap_y(down_sent), swap_z(out_y), swap_z(up_y)

    (qkv, q, kv, kv_other), down_y, out_z, up_z = stage(third_stage)
    out = jnp.concatenate([out_own, in_order(odd == 0, out_y, out_z)], 0)
    up = jnp.stack([up_own, in_order(odd == 0, up_y, up_z)])

    def fourth_stage():
        found = stage(lambda: attend_forward(info, q, kv, kv_other, window)[0])
        return swap_z(down_y), swap_c(out), swap_c(up), found

    down_z, out_far, up_far, attended = stage(fourth_stage)
    down = jnp.stack([down_own, in_order(odd == 0, down_y, down_z)])
    w["down"] = down, stage(lambda: swap_c(down))
    w["out"] = jnp.concatenate([out, out_far], 0)
    w["up"] = up, up_far

    def to_next(value):
        return lax.ppermute(value, "section", [(0, 1)])

    def to_last(value):
        return lax.ppermute(value, "section", [(1, 0)])

    middle = ffn_forward(w, attended, x0, False, 0, 2)[0]
    came_a, middle = stage(
        lambda: (to_next(middle), ffn_forward(w, attended, x0, False, 1, 2)[0])
    )
    came_b = stage(lambda: to_next(middle))

    first_layer = leading.astype(jnp.int32).reshape(1)

    def project_again():
        x1, q, kv = project(x0, *qkv, bias, first_layer, came_a, came_b)
        return x1, q, kv, swap_c(kv)

    x1, q, kv, kv_other = stage(project_again)
    top_sent = theirs(cotangent)

    def eighth_stage():
        attended, lse = attend_forward(info, q, kv, kv_other, window)
        return swap_y(top_sent), swap_c(x1), attended, lse

    top_came, inputs_far, attended, lse = stage(eighth_stage)
    grad_top = in_order(y == 0, mine(cotangent), top_came)
    result, normed_low, active, slope, n_one, s_one, n_two, s_two = ffn_forward(
        w, attended, x1, True
    )
    saved = dict(slope=slope, n_one=n_one, s_one=s_one, n_two=n_two, s_two=s_two)

    def dense_back(after, second):
        names = ("hidden", "before", "branch", "attended", "low_sums", "hidden_sums")
        return dict(zip(names, ffn_backward(w, saved, after, second)))

    def attention_back(grads, table, first, count):
        return attend_backward(
            info, q, kv, kv_other, grads["attended"], lse, window, table, first, count
        )

    after, second, top_sums = top_back(w, saved, jnp.zeros((1,), jnp.int32), grad_top, grad_top)

    def ninth_stage():
        return (
            swap_c(normed_low),
            swap_c(active[:, 2 * width :]),
            swap_c(attended[:, far]),
            dense_back(after, second),
        )

    normed_far, active_far, attended_far, grads = stage(ninth_stage)
    grad_q, grad_k, grad_v, k_far, v_far = attention_back(grads, False, 0, 6)

    def to_middle():
        k_came, v_came = swap_c(k_far), swap_c(v_far)
        found = input_back(grad_q, grad_k, k_came, grad_v, v_came, grads["before"], *qkv)
        return to_last(found[3])

    grad_middle = stage(to_middle)

    thirds = width // 3

    def down_grad(kind, first):
        return weight_grad(
            active, active_far, second, second_far, kind, (first, 3, thirds), (0, 1, model)
        )

    after, second, top_sums = top_back(w, saved, first_layer, grad_middle, grad_top)
    second_far = stage(lambda: swap_c(second))
    down_sent = down_grad(bf16, 3)

    def through_dense():
        grads = dense_back(after, second)
        hidden, branch = grads["hidden"], grads["branch"]
        hidden_far, branch_far = swap_c(hidden[:, 2 * width :]), swap_c(branch)
        return grads, hidden_far, branch_far, down_grad(bf16, 0)

    def send_dense(grads, hidden_far, branch_far):
        args = normed_low, normed_far, grads["hidden"], hidden_far
        sent = weight_grad(*args, bf16, (0, 3, thirds), (1, 1, width))
        branch = grads["branch"]
        return sent, split_grad(attended, attended_far, branch, branch_far, 2 * cols)

    def dense_and_sends():
        grads, hidden_far, branch_far, down_kept = through_dense()
        return grads, hidden_far, down_kept, send_dense(grads, hidden_far, branch_far)

    down_came, (grads, hidden_far, down_kept, sends) = stage(
        lambda: (swap_y(down_sent), stage(dense_and_sends))
    )
    up_sent, (out_kept, out_sent) = sends
    down = down_kept + down_came

    def through_attention():
        args = normed_low, normed_far, grads["hidden"], hidden_far
        kept = weight_grad(*args, bf16, (0, 3, thirds), (0, 1, width))
        return attention_back(grads, True, 0, 6), kept

    def through_input(q_grad, k_grad, v_grad, k_far, v_far):
        came = swap_c(k_far), swap_c(v_far)
        near, far, grad_input, grad_low, qv_sums = input_back(
            q_grad, k_grad, came[0], v_grad, came[1], grads["before"], *qkv
        )
        rest_kept, rest_sent = split_grad(near, swap_c(far), x1, inputs_far, 2 * cols)
        return rest_kept, rest_sent, grad_input, grad_low, qv_sums

    def after_down():
        up_came, out_came, (found, up_kept) = stage(
            lambda: (swap_y(up_sent), swap_y(out_sent), stage(through_attention))
        )
        *found, held = found
        found = stage(lambda: through_input(*found))
        return found, held, up_kept + up_came, out_kept + out_came

    def over_planes(value, beside):
        if planes != 4:
            return lax.psum(value, "dp"), stage(beside)
        rows = value.shape[0] // 2
        first, second = value[:rows], value[rows:]
        held, sent = jnp.where(odd == 0, first, second), jnp.where(odd == 0, second, first)
        came, found = stage(lambda: (swap_z(sent), stage(beside)))
        held = held + came
        far_planes = [(0, 2), (2, 0), (1, 3), (3, 1)]
        return held + stage(lambda: lax.ppermute(held, "dp", far_planes)), found

    def after_up():
        rest_kept, rest_sent, grad_input, grad_low, qv_sums = input_found

        def own_sums():
            sums = token_sums(held, qv_sums)
            sums = sums[:2] + swap_c(sums[2:])
            if planes == 4:
                sums = sums + swap_z(sums)
                sums = sums + lax.ppermute(sums, "dp", [(0, 2), (2, 0), (1, 3), (3, 1)])
            else:
                sums = lax.psum(sums, "dp")
            return sums, grad_down.astype(f32)[None]

        rest_came, (sums, down_out) = stage(
            lambda: (swap_y(rest_sent), stage(own_sums))
        )
        rest = rest_kept + rest_came
        grad_qkv, found = over_planes(
            rest, lambda: through_sums(sums, grad_input, grad_low)
        )
        return down_out, grad_qkv, found

    def through_sums(sums, grad_input, grad_low):
        edge_low = edge_blocks(jnp.where(leading, grad_low, result.astype(bf16)))
        edge_own = mine(edge_blocks(jnp.where(leading, grad_input, result)))
        edge_came = swap_y(theirs(edge_low)).astype(f32)
        edges = [jnp.where(y == 0, edge_own, edge_came), jnp.where(y == 0, edge_came, edge_own)]
        sums = sums[0] + swap_y(sums[1])
        at = heads * 2 * kinds
        vec_out = sums[at + 2 * cols + width :].reshape(1, 6, share)
        return (
            jnp.stack(edges)[None],
            sums[at : at + 2 * cols].reshape(1, 2, cols),
            sums[at + 2 * cols : at + 2 * cols + width].reshape(1, width),
            vec_out[:, :2],
            vec_out[:, 2:],
            sums[:at].reshape(1, heads, 2 * kinds),
        )

    share = model // 4

    def token_sums(held, qv_sums):
        wide = held.reshape(4 * heads, 2, 8 * SPAN)
        wide = jnp.stack([wide[:, 0] - wide[:, 1], wide[:, 1]], 1).reshape(8 * heads, 8 * SPAN)
        high = wide.astype(bf16)
        low = (wide - high.astype(f32)).astype(bf16)
        grad_table = dotf(high, onehot, NT) + dotf(low, onehot, NT)
        grad_table = grad_table.reshape(4, heads * 2 * kinds)
        q_sums, _, v_sums = qv_sums.reshape(3, 4, cols)
        grad_ffn = grads["hidden_sums"].reshape(4, width)
        low_sums = grads["low_sums"]
        rows = [low_sums[0], top_sums[0], low_sums[1], low_sums[2], top_sums[1], top_sums[2]]
        by_share = jnp.stack(rows).reshape(6, 4, share)
        by_share = by_share.transpose(1, 0, 2).reshape(4, 6 * share)
        by_share = jnp.stack(
            [lax.dynamic_index_in_dim(by_share, place ^ flip, 0, False) for flip in (0, 2, 1, 3)]
        )
        return jnp.concatenate([grad_table, q_sums, v_sums, grad_ffn, by_share], 1)

    grad_down, (input_found, held, *later) = stage(
        lambda: (lax.psum(down, "dp"), stage(after_down))
    )
    summed, (down_out, grad_qkv, found) = stage(lambda: (lax.psum(later, "dp"), stage(after_up)))

    def last_stage():
        back = swap_z(grad_qkv) if planes == 4 else grad_qkv
        return back, *[value.astype(f32)[None] for value in summed]

    back, up_out, out_out = stage(last_stage)
    if planes == 4:
        grad_qkv = in_order(odd == 0, grad_qkv, back)
    qkv_out = grad_qkv.astype(f32).reshape(1, 3, cols, model)
    edges, qv_out, ffn_out, gain_out, vec_out, table_out = found
    return (
        edges,
        qkv_out.transpose(0, 3, 1, 2),
        qv_out,
        out_out,
        up_out,
        ffn_out,
        down_out,
        gain_out,
        vec_out,
        table_out,
    )


def solution(mesh):
    return jax.shard_map(
        body,
        mesh=mesh,
        in_specs=(
            P("dp", "tensor", None),
            P("dp", "tensor", None),
            P("dp"),
            P("dp"),
            P(),
            P("section", None, None, "tensor"),
            P("section", None, "tensor"),
            P("section", "tensor", None),
            P("section", None, "tensor"),
            P("section", "tensor"),
            P("section", "tensor", None),
            P("section", None, None),
            P("section", None, None),
            P("section", "tensor", None),
        ),
        out_specs=(
            P("section", "dp", "tensor", None),
            P("section", None, None, "tensor"),
            P("section", None, "tensor"),
            P("section", "tensor", None),
            P("section", None, "tensor"),
            P("section", "tensor"),
            P("section", "tensor", None),
            P("section", None, "tensor"),
            P("section", None, "tensor"),
            P("section", "tensor", None),
        ),
        check_vma=False,
    )
```

```python
import functools

import jax
import jax.numpy as jnp
from jax import lax
from jax.experimental import pallas as pl
from jax.experimental.pallas import tpu as pltpu
from jax.sharding import PartitionSpec as P


f32 = jnp.float32
bf16 = jnp.bfloat16
EPS = 1e-05
HEAD = 64
NEG = -1e30
SWAP_Y = [(0, 2), (2, 0), (1, 3), (3, 1)]
SWAP_C = [(0, 1), (1, 0), (2, 3), (3, 2)]
NT = (((1,), (1,)), ((), ()))
TN = (((0,), (0,)), ((), ()))
NN = (((1,), (0,)), ((), ()))
KEY_BASE = (0, 512, 256, 768)
TILE_BASE = (0, 128, 512, 640)
STRIP = 1664
SPAN = STRIP + 128
PIECE = 32
MIB = 2**20
IN_VMEM = pl.BlockSpec(memory_space=pltpu.VMEM)


def cost(us, flops=0):
    return pl.CostEstimate(flops=flops, bytes_accessed=int(us * 3.4e6), transcendentals=0)


def dotf(a, b, dims=NN):
    return lax.dot_general(a, b, dims, preferred_element_type=f32)


def swap_y(value):
    return lax.ppermute(value, "tensor", SWAP_Y)


def swap_c(value):
    return lax.ppermute(value, "tensor", SWAP_C)


def make_strip(window_ref, h, kind, strip_ref):
    blocks = STRIP // 128
    lane = lax.broadcasted_iota(jnp.int32, (8, 128), 1)
    row = lax.broadcasted_iota(jnp.int32, (8, 128), 0)

    def rolled(first):
        at = 2 * h + kind
        seg = window_ref[at : at + 1, first : first + 128]
        seg = pltpu.roll(jnp.broadcast_to(seg, (8, 128)), 0, 1, stride=1, stride_axis=0)
        return [pltpu.roll(seg, 8 * q, 1) if q else seg for q in range(16)]

    high = rolled(128 * blocks)
    for a in range(blocks):
        low = rolled(128 * (blocks - 1 - a))
        for q in range(16):
            rows = slice(128 * a + 8 * q, 128 * a + 8 * q + 8)
            strip_ref[h, kind, rows, :] = jnp.where(lane >= row + 8 * q, high[q], low[q])
        high = low


def sum_strip(strip_ref, h, kind, held_ref):
    blocks = STRIP // 128
    lane = lax.broadcasted_iota(jnp.int32, (8, 128), 1)
    carry = jnp.zeros((8, 128), f32)
    for a in reversed(range(blocks)):
        low, high = jnp.zeros((8, 128), f32), jnp.zeros((8, 128), f32)
        for q in range(16):
            part = strip_ref[h, kind, 128 * a + 8 * q : 128 * a + 8 * q + 8, :]
            if q:
                part = pltpu.roll(part, 128 - 8 * q, 1)
            stays = lane < 128 - 8 * q
            high += jnp.where(stays, part, 0.0)
            low += jnp.where(stays, 0.0, part)
        first = 128 * (blocks - 1 - a)
        held_ref[0, h, kind, :, first : first + 128] = low + carry
        carry = high
    held_ref[0, h, kind, :, 128 * blocks : 128 * blocks + 128] = carry


def lane_mask(rows, which):
    lane = lax.broadcasted_iota(jnp.int32, (rows, 128), 1)
    return (lane < HEAD) if which == 0 else (lane >= HEAD)


def cross_mask(info_ref, tile, first):
    key_low = first < 256
    row_low = tile < 2
    if not key_low and not row_low:
        return None
    qlen, core = info_ref[0], info_ref[1]
    shape = (PIECE, 128)
    if row_low:
        row = 256 * core + 128 * tile + lax.broadcasted_iota(jnp.int32, shape, 1)
        row_side = row < qlen
    if key_low:
        key_side = first + lax.broadcasted_iota(jnp.int32, shape, 0) < qlen
    if row_low and key_low:
        return row_side != key_side
    return row_side if row_low else key_side


def pieces(kb):
    for at in range(0, 256, PIECE):
        yield KEY_BASE[kb] + at, slice(256 * kb + at, 256 * kb + at + PIECE), slice(at, at + PIECE)


def strip_rows(tile, first):
    start = first - TILE_BASE[tile] + 640
    return slice(start, start + PIECE)


def piece_scores(info_ref, raw, strip_ref, h, ib, first):
    parts = []
    for u in (0, 1):
        tile = 2 * ib + u
        rows = strip_rows(tile, first)
        bias = strip_ref[h, 0, rows, :]
        cross = cross_mask(info_ref, tile, first)
        if cross is not None:
            bias = jnp.where(cross, strip_ref[h, 1, rows, :], bias)
        parts.append(raw[:, 128 * u : 128 * u + 128] + bias)
    scores = jnp.concatenate(parts, 1)
    if first >= 256:
        live = first + lax.broadcasted_iota(jnp.int32, (PIECE, 256), 0) < info_ref[2]
        scores = jnp.where(live, scores, NEG)
    return scores


def by_eight(value):
    return value.reshape(PIECE // 8, 8, 256)


def whole(core, own, other):
    return jnp.concatenate([jnp.where(core == 0, own, other), jnp.where(core == 0, other, own)], 0)


def forward_kernel(
    info_ref,
    q_ref,
    k_ref,
    v_ref,
    ko_ref,
    vo_ref,
    win_ref,
    o_ref,
    lse_ref,
    strip_ref,
    score_ref,
    prob_ref,
):
    core = info_ref[1]
    for h in range(2):
        for kind in range(2):
            make_strip(win_ref, h, kind, strip_ref)
    keys = whole(core, k_ref[...], ko_ref[...])
    values = whole(core, v_ref[...], vo_ref[...])
    one = jnp.ones_like(values)
    turned = [jnp.where(lane_mask(1024, h), values, one).T for h in range(2)]
    for ib in range(2):
        rows = slice(256 * ib, 256 * ib + 256)
        query = q_ref[rows, :] * jnp.asarray(0.125, bf16)
        outs = []
        for h in range(2):
            one = jnp.where(lane_mask(256, h), query, jnp.zeros_like(query))
            top = None
            for kb in range(4):
                raw = dotf(keys[256 * kb : 256 * kb + 256], one, NT)
                for first, at, within in pieces(kb):
                    scores = piece_scores(info_ref, raw[within], strip_ref, h, ib, first)
                    score_ref[h, at, :] = scores
                    most = jnp.max(by_eight(scores), 0)
                    top = most if top is None else jnp.maximum(top, most)
            top = jnp.max(top, 0, keepdims=True)
            for kb in range(4):
                for _, at, _ in pieces(kb):
                    prob_ref[h, at, :] = jnp.exp(score_ref[h, at, :] - top).astype(bf16)
            mixed = dotf(turned[h], prob_ref[h])
            total = mixed[HEAD * (1 - h) : HEAD * (1 - h) + 1, :]
            lse_ref[0, h : h + 1, rows] = top + jnp.log(total)
            outs.append(mixed[HEAD * h : HEAD * h + HEAD, :] / total)
        o_ref[rows, :] = jnp.concatenate(outs, 0).T.astype(bf16)


def kv_blocks(groups, first=0):
    half = groups // 2
    return [
        pl.BlockSpec((512, 128), lambda i, s: (0, i + first)),
        pl.BlockSpec((512, 128), lambda i, s: (0, i + first + groups)),
        pl.BlockSpec((512, 128), lambda i, s: (0, (i + first + half) % groups)),
        pl.BlockSpec((512, 128), lambda i, s: (0, (i + first + half) % groups + groups)),
    ]


def attend_forward(info, q, kv, kv_other, window):
    groups = q.shape[1] // 128
    block = pl.BlockSpec((512, 128), lambda i, s: (0, i))
    return pl.pallas_call(
        forward_kernel,
        grid_spec=pltpu.PrefetchScalarGridSpec(
            num_scalar_prefetch=1,
            grid=(groups,),
            in_specs=[
                block,
                *kv_blocks(groups),
                pl.BlockSpec((8, SPAN), lambda i, s: (i, 0)),
            ],
            out_specs=[block, pl.BlockSpec((1, 2, 512), lambda i, s: (i, 0, 0))],
            scratch_shapes=[
                pltpu.VMEM((2, 2, STRIP, 128), f32),
                pltpu.VMEM((2, 1024, 256), f32),
                pltpu.VMEM((2, 1024, 256), bf16),
            ],
        ),
        out_shape=[
            jax.ShapeDtypeStruct((512, 128 * groups), bf16),
            jax.ShapeDtypeStruct((groups, 2, 512), f32),
        ],
        compiler_params=pltpu.CompilerParams(vmem_limit_bytes=24 * MIB),
        cost_estimate=cost(17),
        name="attend_forward",
    )(info, q, kv, kv, kv_other, kv_other, window)


def backward_kernel(with_table, *refs):
    info_ref, q_ref, k_ref, v_ref, ko_ref, vo_ref, do_ref, lse_ref, win_ref = refs[:9]
    dq_ref, dk_ref, dv_ref, dko_ref, dvo_ref, *rest = refs[9:]
    core = info_ref[1]
    *rest, strip_ref, wide_ref, term_ref, prob_ref, grad_ref = rest
    for h in range(2):
        for kind in range(2):
            make_strip(win_ref, h, kind, strip_ref)
    if with_table:
        held_ref, strip_grad_ref = rest
        strip_grad_ref[...] = jnp.zeros_like(strip_grad_ref)
    keys = whole(core, k_ref[...], ko_ref[...])
    values = whole(core, v_ref[...], vo_ref[...])
    keys_turned = keys.T
    key_grad = value_grad = 0.0
    for ib in range(2):
        rows = slice(256 * ib, 256 * ib + 256)
        query = q_ref[rows, :] * jnp.asarray(0.125, bf16)
        grad = do_ref[rows, :]
        query_grads = []
        for h in range(2):
            mask = lane_mask(256, h)
            one = jnp.where(mask, query, jnp.zeros_like(query))
            grad_one = jnp.where(mask, grad, jnp.zeros_like(grad))
            log_total = lse_ref[0, h : h + 1, rows]
            row_term = 0.0
            for kb in range(4):
                kr = slice(256 * kb, 256 * kb + 256)
                raw = dotf(keys[kr], one, NT)
                grad_probs = dotf(values[kr], grad_one, NT)
                for first, at, within in pieces(kb):
                    scores = piece_scores(info_ref, raw[within], strip_ref, h, ib, first)
                    probs = jnp.exp(scores - log_total)
                    term = probs * grad_probs[within]
                    wide_ref[h, at, :] = probs
                    term_ref[h, at, :] = term
                    prob_ref[h, at, :] = probs.astype(bf16)
                    row_term = row_term + jnp.sum(by_eight(term), 0)
            row_term = jnp.sum(row_term, 0, keepdims=True)
            for kb in range(4):
                for first, at, _ in pieces(kb):
                    low = (term_ref[h, at, :] - wide_ref[h, at, :] * row_term).astype(bf16)
                    grad_ref[h, at, :] = low
                    if with_table:
                        for u in (0, 1):
                            tile = 2 * ib + u
                            where = strip_rows(tile, first)
                            part = low[:, 128 * u : 128 * u + 128].astype(f32)
                            strip_grad_ref[h, 0, where, :] += part
                            cross = cross_mask(info_ref, tile, first)
                            if cross is not None:
                                strip_grad_ref[h, 1, where, :] += jnp.where(cross, part, 0.0)
            value_grad = value_grad + dotf(prob_ref[h], grad_one)
            key_grad = key_grad + dotf(grad_ref[h], one)
            flat = dotf(keys_turned, grad_ref[h])
            query_grads.append(flat[HEAD * h : HEAD * h + HEAD, :])
        dq_ref[rows, :] = (jnp.concatenate(query_grads, 0).T * 0.125).astype(bf16)
    for grads, own_ref, other_ref in (
        (key_grad, dk_ref, dko_ref),
        (value_grad, dv_ref, dvo_ref),
    ):
        first, second = grads[:512], grads[512:]
        own_ref[...] = jnp.where(core == 0, first, second)
        other_ref[...] = jnp.where(core == 0, second, first).astype(bf16)
    if with_table:
        for h in range(2):
            for kind in range(2):
                sum_strip(strip_grad_ref, h, kind, held_ref)


def attend_backward(info, q, kv, kv_other, grad, lse, window, with_table, first, count):
    groups = q.shape[1] // 128
    block = pl.BlockSpec((512, 128), lambda i, s: (0, i + first))
    rows = lambda kind: jax.ShapeDtypeStruct((512, 128 * count), kind)
    out_specs = [pl.BlockSpec((512, 128), lambda i, s: (0, i))] * 5
    out_shape = [rows(bf16), rows(f32), rows(f32), rows(bf16), rows(bf16)]
    scratch = [pltpu.VMEM((2, 2, STRIP, 128), f32)]
    if with_table:
        out_specs.append(pl.BlockSpec((1, 2, 2, 8, SPAN), lambda i, s: (i, 0, 0, 0, 0)))
        out_shape.append(jax.ShapeDtypeStruct((count, 2, 2, 8, SPAN), f32))
        scratch = scratch * 2
    scratch += [pltpu.VMEM((2, 1024, 256), f32)] * 2 + [pltpu.VMEM((2, 1024, 256), bf16)] * 2
    return pl.pallas_call(
        functools.partial(backward_kernel, with_table),
        grid_spec=pltpu.PrefetchScalarGridSpec(
            num_scalar_prefetch=1,
            grid=(count,),
            in_specs=[
                block,
                *kv_blocks(groups, first),
                block,
                pl.BlockSpec((1, 2, 512), lambda i, s: (i + first, 0, 0)),
                pl.BlockSpec((8, SPAN), lambda i, s: (i + first, 0)),
            ],
            out_specs=out_specs,
            scratch_shapes=scratch,
        ),
        out_shape=out_shape,
        compiler_params=pltpu.CompilerParams(vmem_limit_bytes=36 * MIB),
        cost_estimate=cost(30),
        name="attend_backward",
    )(info, q, kv, kv, kv_other, kv_other, grad, lse, window)


def norm_parts(values):
    centre = jnp.mean(values, -1, keepdims=True)
    centred = values - centre
    scale = lax.rsqrt(jnp.mean(centred * centred, -1, keepdims=True) + EPS)
    return centred * scale, scale


def norm_back(grad, gain, normal, scale):
    scaled = grad * gain
    return scale * (
        scaled
        - jnp.mean(scaled, -1, keepdims=True)
        - normal * jnp.mean(scaled * normal, -1, keepdims=True)
    )


def normal_cdf(units):
    size = jnp.abs(units)
    t = 1.0 / (1.0 + (0.3275911 * 0.5**0.5) * size)
    bell = jnp.exp(-0.5 * units * units)
    poly = 0.5 * 1.061405429
    for coef in (-1.453152027, 1.421413741, -0.284496736, 0.254829592):
        poly = poly * t + 0.5 * coef
    tail = poly * t * bell
    return jnp.where(units >= 0, 1.0 - tail, tail), bell


def ffn_forward_kernel(
    keep,
    att_ref,
    x_ref,
    out_ref,
    up_ref,
    up_far_ref,
    down_ref,
    down_far_ref,
    bias_ref,
    gain_ref,
    shift_ref,
    result_ref,
    *rest,
):
    if keep:
        (
            low_ref,
            active_ref,
            slope_ref,
            n_one_ref,
            s_one_ref,
            n_two_ref,
            s_two_ref,
            normed_low,
            total,
        ) = rest
    else:
        normed_low, total = rest
    i = pl.program_id(0)

    @pl.when(i == 0)
    def _():
        before = x_ref[...].astype(f32) + (dotf(att_ref[...], out_ref[...]) + shift_ref[0:1, :])
        normal, scale = norm_parts(before)
        normed = normal * gain_ref[0:1, :] + shift_ref[1:2, :]
        normed_low[...] = normed.astype(bf16)
        total[...] = normed + shift_ref[2:3, :]
        if keep:
            n_one_ref[...] = normal
            s_one_ref[...] = scale
            low_ref[...] = normed_low[...]

    near = i < 2
    width = up_ref.shape[2]
    step = 256
    add = None
    for first in range(0, width, step):
        cols = slice(first, first + step)
        up = jnp.where(near, up_ref[0, :, cols], up_far_ref[0, :, cols])
        down = jnp.where(near, down_ref[0, cols, :], down_far_ref[0, cols, :])
        units = dotf(normed_low[...], up) + bias_ref[:, cols]
        side, bell = normal_cdf(units)
        active = (units * side).astype(bf16)
        if keep:
            active_ref[:, cols] = active
            slope_ref[:, cols] = (side + units * bell * 0.3989422804014327).astype(bf16)
        part = dotf(active, down)
        add = part if add is None else add + part
    total[...] += add

    @pl.when(i == pl.num_programs(0) - 1)
    def _():
        normal, scale = norm_parts(total[...])
        result = normal * gain_ref[1:2, :] + shift_ref[3:4, :]
        result_ref[...] = result.astype(result_ref.dtype)
        if keep:
            n_two_ref[...] = normal
            s_two_ref[...] = scale


def near_far(rows, cols):
    return [
        pl.BlockSpec((1, rows, cols), lambda i: (jnp.minimum(i, 1), 0, 0)),
        pl.BlockSpec((1, rows, cols), lambda i: (jnp.maximum(i - 2, 0), 0, 0)),
    ]


def ffn_forward(w, attended, inputs, keep, part=0, parts=1):
    rows, model = inputs.shape
    rows //= parts
    width = w["up"][0].shape[2]
    all_of = lambda *shape: pl.BlockSpec(shape, lambda i: (0,) * len(shape))
    by_step = pl.BlockSpec((rows, width), lambda i: (0, i))
    shape = lambda cols, kind: jax.ShapeDtypeStruct((rows, cols), kind)
    out_specs = [all_of(rows, model)]
    out_shape = [shape(model, f32 if keep else bf16)]
    if keep:
        out_specs += [all_of(rows, model), by_step, by_step]
        out_specs += [all_of(rows, model), all_of(rows, 1)] * 2
        out_shape += [shape(model, bf16), shape(4 * width, bf16), shape(4 * width, bf16)]
        out_shape += [shape(model, f32), shape(1, f32)] * 2
    flops = 2 * rows * model * (model + 8 * width)
    return pl.pallas_call(
        functools.partial(ffn_forward_kernel, keep),
        grid=(4,),
        in_specs=[
            pl.BlockSpec((rows, model), lambda i: (part, 0)),
            pl.BlockSpec((rows, model), lambda i: (part, 0)),
            all_of(model, model),
            *near_far(model, width),
            *near_far(width, model),
            pl.BlockSpec((1, width), lambda i: (0, i)),
            all_of(2, model),
            all_of(4, model),
        ],
        out_specs=out_specs,
        out_shape=out_shape,
        scratch_shapes=[pltpu.VMEM((rows, model), bf16), pltpu.VMEM((rows, model), f32)],
        compiler_params=pltpu.CompilerParams(vmem_limit_bytes=32 * MIB),
        cost_estimate=cost(15),
        name="ffn_forward",
    )(
        attended,
        inputs,
        w["out"],
        *w["up"],
        *w["down"],
        w["up_bias"],
        w["gains"],
        w["shifts"],
    )


def top_back_kernel(
    first_ref, came_ref, gy_ref, n_two_ref, s_two_ref, gain_ref, after_ref, second_ref, sums_ref
):
    gy = jnp.where(first_ref[0] == 1, came_ref[...], gy_ref[...]).astype(f32)
    after = norm_back(gy, gain_ref[1:2, :], n_two_ref[...], s_two_ref[...])
    low = after.astype(bf16)
    after_ref[...] = after
    second_ref[...] = low
    sums_ref[0:1, :] = jnp.sum(gy * n_two_ref[...], 0, keepdims=True)
    sums_ref[1:2, :] = jnp.sum(low.astype(f32), 0, keepdims=True)
    sums_ref[2:3, :] = jnp.sum(gy, 0, keepdims=True)
    sums_ref[3:8, :] = jnp.zeros((5, sums_ref.shape[1]), f32)


def top_back(w, saved, first_layer, came, grad_y):
    rows, model = grad_y.shape
    return pl.pallas_call(
        top_back_kernel,
        in_specs=[pl.BlockSpec(memory_space=pltpu.SMEM), *[IN_VMEM] * 5],
        out_specs=[IN_VMEM] * 3,
        out_shape=[
            jax.ShapeDtypeStruct((rows, model), f32),
            jax.ShapeDtypeStruct((rows, model), bf16),
            jax.ShapeDtypeStruct((8, model), f32),
        ],
        compiler_params=pltpu.CompilerParams(vmem_limit_bytes=16 * MIB),
        cost_estimate=cost(2),
        name="top_back",
    )(first_layer, came, grad_y, saved["n_two"], saved["s_two"], w["gains"])


def ffn_backward_kernel(deps, *refs):
    (
        after_ref,
        second_ref,
        slope_ref,
        n_one_ref,
        s_one_ref,
        out_ref,
        up_ref,
        up_far_ref,
        down_ref,
        down_far_ref,
        gain_ref,
    ) = refs[:11]
    hidden_ref, before_ref, branch_ref, att_ref, sums_ref, hidden_sums_ref, total = refs[11 + deps :]
    i = pl.program_id(0)

    def add_up(value):
        return jnp.sum(value, 0, keepdims=True)

    @pl.when(i == 0)
    def _():
        total[...] = after_ref[...]

    near = i < 2
    width = up_ref.shape[2]
    step = 256
    add = None
    for first in range(0, width, step):
        cols = slice(first, first + step)
        up = jnp.where(near, up_ref[0, :, cols], up_far_ref[0, :, cols])
        down = jnp.where(near, down_ref[0, cols, :], down_far_ref[0, cols, :])
        active = dotf(second_ref[...], down, NT)
        hidden = (active * slope_ref[:, cols].astype(f32)).astype(bf16)
        hidden_ref[:, cols] = hidden
        hidden_sums_ref[0, :, cols] = add_up(hidden.astype(f32))
        part = dotf(hidden, up, NT)
        add = part if add is None else add + part
    total[...] += add

    @pl.when(i == pl.num_programs(0) - 1)
    def _():
        normed = total[...]
        before = norm_back(normed, gain_ref[0:1, :], n_one_ref[...], s_one_ref[...])
        low = before.astype(bf16)
        before_ref[...] = before
        branch_ref[...] = low
        att_ref[...] = dotf(low, out_ref[...], NT).astype(bf16)
        sums_ref[0:1, :] = add_up(normed * n_one_ref[...])
        sums_ref[1:2, :] = add_up(low.astype(f32))
        sums_ref[2:3, :] = add_up(normed)
        sums_ref[3:8, :] = jnp.zeros((5, sums_ref.shape[1]), f32)


def ffn_backward(w, saved, after, second, deps=()):
    rows, model = after.shape
    width = w["up"][0].shape[2]
    all_of = lambda *shape: pl.BlockSpec(shape, lambda i: (0,) * len(shape))
    by_step = pl.BlockSpec((rows, width), lambda i: (0, i))
    by_block = pl.BlockSpec((1, 1, width), lambda i: (i, 0, 0))
    shape = lambda cols, kind: jax.ShapeDtypeStruct((rows, cols), kind)
    whole_rows = all_of(rows, model)
    return pl.pallas_call(
        functools.partial(ffn_backward_kernel, len(deps)),
        grid=(4,),
        in_specs=[
            whole_rows,
            whole_rows,
            by_step,
            whole_rows,
            all_of(rows, 1),
            all_of(model, model),
            *near_far(model, width),
            *near_far(width, model),
            all_of(2, model),
            *[pl.BlockSpec(memory_space=pl.ANY)] * len(deps),
        ],
        out_specs=[by_step, whole_rows, whole_rows, whole_rows, all_of(8, model), by_block],
        out_shape=[
            shape(4 * width, bf16),
            shape(model, f32),
            shape(model, bf16),
            shape(model, bf16),
            jax.ShapeDtypeStruct((8, model), f32),
            jax.ShapeDtypeStruct((4, 1, width), f32),
        ],
        scratch_shapes=[pltpu.VMEM((rows, model), f32)],
        compiler_params=pltpu.CompilerParams(vmem_limit_bytes=32 * MIB),
        cost_estimate=cost(15),
        name="ffn_backward",
    )(
        after,
        second,
        saved["slope"],
        saved["n_one"],
        saved["s_one"],
        w["out"],
        *w["up"],
        *w["down"],
        w["gains"],
        *deps,
    )


def weight_grad_kernel(l_ref, lo_ref, r_ref, ro_ref, o_ref):
    total = dotf(l_ref[...], r_ref[...], TN) + dotf(lo_ref[...], ro_ref[...], TN)
    o_ref[...] = total.astype(o_ref.dtype)


def weight_grad(left, left_far, right, right_far, kind, left_cols, right_cols):
    rows = left.shape[0]
    lf, ln, lw = left_cols
    rf, rn, rw = right_cols
    return pl.pallas_call(
        weight_grad_kernel,
        grid=(rn, ln),
        in_specs=[
            pl.BlockSpec((rows, lw), lambda j, i: (0, lf + i)),
            pl.BlockSpec((rows, lw), lambda j, i: (0, lf + i)),
            pl.BlockSpec((rows, rw), lambda j, i: (0, rf + j)),
            pl.BlockSpec((rows, rw), lambda j, i: (0, rf + j)),
        ],
        out_specs=pl.BlockSpec((lw, rw), lambda j, i: (i, j)),
        out_shape=jax.ShapeDtypeStruct((ln * lw, rn * rw), kind),
        compiler_params=pltpu.CompilerParams(vmem_limit_bytes=20 * MIB),
        cost_estimate=cost(4),
        name="weight_grad",
    )(left, left_far, right, right_far)


def split_grad_kernel(l_ref, lo_ref, r_ref, ro_ref, kept_ref, sent_ref):
    total = dotf(l_ref[...], r_ref[...], TN) + dotf(lo_ref[...], ro_ref[...], TN)
    half = total.shape[0] // 2
    kept_ref[...] = total[:half].astype(bf16)
    sent_ref[...] = total[half:].astype(bf16)


def split_grad(left, left_far, right, right_far, width):
    rows, model = right.shape
    count = left_far.shape[1] // width
    left_block = pl.BlockSpec((rows, width), lambda i: (0, i))
    right_block = pl.BlockSpec((rows, model), lambda i: (0, 0))
    made = pl.BlockSpec((width // 2, model), lambda i: (i, 0))
    shape = (count * width // 2, model)
    return pl.pallas_call(
        split_grad_kernel,
        grid=(count,),
        in_specs=[left_block, left_block, right_block, right_block],
        out_specs=[made, made],
        out_shape=[jax.ShapeDtypeStruct(shape, bf16)] * 2,
        compiler_params=pltpu.CompilerParams(vmem_limit_bytes=20 * MIB),
        cost_estimate=cost(4),
        name="split_grad",
    )(left, left_far, right, right_far)


def project_kernel(x_ref, near_ref, far_ref, bias_ref, *refs):
    inputs = x_ref[...]
    *refs, q_ref, kv_ref = refs
    if refs:
        keep_ref, a_ref, b_ref, x1_ref = refs
        inputs = jnp.where(keep_ref[0] == 1, inputs, jnp.concatenate([a_ref[...], b_ref[...]], 0))
        x1_ref[...] = inputs
    half = near_ref.shape[1]
    for which in range(3):
        weight = jnp.concatenate([near_ref[which], far_ref[which]], 0)
        bias = bias_ref[:, 2 * half * which : 2 * half * (which + 1)]
        made = (dotf(inputs, weight, NT) + bias).astype(bf16)
        if which == 0:
            q_ref[...] = made
        else:
            kv_ref[:, 2 * half * (which - 1) : 2 * half * which] = made


def project(inputs, near, far, bias, *instead):
    rows, model = inputs.shape
    shapes = [(rows, model)] * (2 if instead else 1) + [(rows, 2 * model)]
    extra = [pl.BlockSpec(memory_space=pltpu.SMEM), IN_VMEM, IN_VMEM] if instead else []
    return pl.pallas_call(
        project_kernel,
        in_specs=[IN_VMEM] * 4 + extra,
        out_specs=[IN_VMEM] * len(shapes),
        out_shape=[jax.ShapeDtypeStruct(shape, bf16) for shape in shapes],
        compiler_params=pltpu.CompilerParams(vmem_limit_bytes=20 * MIB),
        cost_estimate=cost(4),
        name="project",
    )(inputs, near, far, bias, *instead)


def input_back_kernel(*refs):
    q_ref, k_ref, k_came_ref, v_ref, v_came_ref, before_ref, *weights = refs[:8]
    near_ref, far_ref, grad_ref, low_ref, sums_ref = refs[8:]
    half = near_ref.shape[1] // 3
    total = before_ref[...]
    for which in range(3):
        if which == 0:
            mixed = q_ref[...]
        else:
            own, came = (k_ref, k_came_ref) if which == 1 else (v_ref, v_came_ref)
            other = jnp.concatenate([came[:, half:], came[:, :half]], 1)
            mixed = (own[...] + other.astype(f32)).astype(bf16)
        near_ref[:, half * which : half * which + half] = mixed[:, :half]
        far_ref[:, half * which : half * which + half] = mixed[:, half:]
        sums = jnp.sum(mixed.astype(f32), 0, keepdims=True)
        sums_ref[2 * which] = sums[:, :half]
        sums_ref[2 * which + 1] = sums[:, half:]
        weight = jnp.concatenate([weights[0][which], weights[1][which]], 0)
        total = total + dotf(mixed, weight)
    grad_ref[...] = total
    low_ref[...] = total.astype(bf16)


def input_back(q, k, k_came, v, v_came, before, near, far):
    rows, model = before.shape
    half = model // 2
    return pl.pallas_call(
        input_back_kernel,
        in_specs=[IN_VMEM] * 8,
        out_specs=[IN_VMEM] * 5,
        out_shape=[
            jax.ShapeDtypeStruct((rows, 3 * half), bf16),
            jax.ShapeDtypeStruct((rows, 3 * half), bf16),
            jax.ShapeDtypeStruct((rows, model), f32),
            jax.ShapeDtypeStruct((rows, model), bf16),
            jax.ShapeDtypeStruct((6, 1, half), f32),
        ],
        compiler_params=pltpu.CompilerParams(vmem_limit_bytes=24 * MIB),
        cost_estimate=cost(6),
        name="input_back",
    )(q, k, k_came, v, v_came, before, near, far)


def body(
    hidden,
    cotangent,
    pair_lengths,
    query_lengths,
    buckets,
    qkv_weight,
    qv_bias,
    out_weight,
    up_weight,
    ffn_bias,
    down_weight,
    norm_gains,
    vectors,
    bias_table,
):
    leading = lax.axis_index("section") == 0
    place = lax.axis_index("tensor")
    y, core = place // 2, place % 2
    plane = lax.axis_index("dp")
    planes = lax.axis_size("dp")
    odd = plane % 2
    local, model = hidden.shape[1], hidden.shape[2]
    total = 4 * local
    cols = qkv_weight.shape[3]
    width = up_weight.shape[2]
    heads = bias_table.shape[1]
    kinds = bias_table.shape[2] // 2
    near, far = slice(0, 2 * cols), slice(2 * cols, 4 * cols)

    def swap_z(value):
        return lax.ppermute(value, "dp", [(i, i ^ 1) for i in range(planes)])

    def mine(array):
        return lax.dynamic_index_in_dim(array, y, 0, keepdims=False)

    def theirs(array):
        return lax.dynamic_index_in_dim(array, 1 - y, 0, keepdims=False)

    def in_order(first, own, came, axis=0):
        return jnp.concatenate(
            [jnp.where(first, own, came), jnp.where(first, came, own)], axis
        )

    def own_half(block, axis=0):
        half = block.shape[axis] // 2
        return lax.dynamic_slice_in_dim(block, half * odd, half, axis)

    def edge_blocks(value):
        return value.reshape(2, local, model)

    def stage(work):
        shapes = jax.eval_shape(work)
        return lax.cond(
            pair_lengths[0] > 0,
            work,
            lambda: jax.tree.map(lambda leaf: jnp.zeros(leaf.shape, leaf.dtype), shapes),
        )

    qkv_own = qkv_weight[0].transpose(1, 2, 0)
    out_own, up_own, down_own = out_weight[0], up_weight[0], down_weight[0]
    small = jnp.concatenate([qv_bias[0].reshape(-1), ffn_bias[0], bias_table[0].reshape(-1)])

    x_sent, qkv_sent = theirs(hidden), own_half(qkv_own, 1)

    def first_stage():
        halves = own_half(out_own), own_half(up_own), own_half(down_own)
        return swap_y(small), swap_y(x_sent), swap_y(qkv_sent), halves

    small_y, x_came, qkv_y, (out_sent, up_sent, down_sent) = stage(first_stage)

    def gather_small():
        two = jnp.stack([small, small_y])
        four = jnp.concatenate([two, swap_c(two)])
        table = four[:, 2 * cols + width :].reshape(2 * heads, 4, kinds)
        table = jnp.pad(table, ((0, 0), (0, 4), (0, 0))).reshape(16 * heads, kinds)
        kind = jnp.pad(buckets, (1, 0))
        kind = lax.dynamic_slice_in_dim(kind, 256 * core, SPAN, 0)
        kind = jnp.stack([jnp.pad(kind, (s, 0), constant_values=-1)[:SPAN] for s in range(8)])
        kind = kind.reshape(1, 8 * SPAN)
        onehot = (kind == jnp.arange(kinds, dtype=jnp.int32)[:, None]).astype(bf16)
        window = jnp.dot(
            table, onehot[:, :SPAN].astype(f32), precision=lax.Precision.HIGHEST
        )
        qv_all = four[:, : 2 * cols].reshape(4, 2, cols)
        q_bias, v_bias = qv_all[:, 0].reshape(-1), qv_all[:, 1].reshape(-1)
        bias = jnp.concatenate([q_bias, jnp.zeros((model,), f32), v_bias])
        info = jnp.stack([mine(query_lengths), core, mine(pair_lengths)]).astype(jnp.int32)
        return (
            window,
            onehot,
            bias.reshape(1, 3 * model),
            four[:, 2 * cols : 2 * cols + width].reshape(1, 4 * width),
            info,
            in_order(y == 0, mine(hidden), x_came),
        )

    def second_stage():
        return swap_z(qkv_y), swap_y(out_sent), swap_y(up_sent), stage(gather_small)

    qkv_z, out_y, up_y, found = stage(second_stage)
    window, onehot, bias, up_bias, info, x0 = found
    w = dict(up_bias=up_bias, gains=norm_gains[0], shifts=vectors[0])

    def gather_qkv():
        near = jnp.concatenate([qkv_own, in_order(odd == 0, qkv_y, qkv_z, 1)], 1)
        far = swap_c(near)
        q, kv = project(x0, near, far, bias)
        return (near, far), q, kv, swap_c(kv)

    def third_stage():
        return stage(gather_qkv), swap_y(down_sent), swap_z(out_y), swap_z(up_y)

    (qkv, q, kv, kv_other), down_y, out_z, up_z = stage(third_stage)
    out = jnp.concatenate([out_own, in_order(odd == 0, out_y, out_z)], 0)
    up = jnp.stack([up_own, in_order(odd == 0, up_y, up_z)])

    def fourth_stage():
        found = stage(lambda: attend_forward(info, q, kv, kv_other, window)[0])
        return swap_z(down_y), swap_c(out), swap_c(up), found

    down_z, out_far, up_far, attended = stage(fourth_stage)
    down = jnp.stack([down_own, in_order(odd == 0, down_y, down_z)])
    down_far, w["out"] = stage(lambda: (swap_c(down), jnp.concatenate([out, out_far], 0)))
    w["down"] = down, down_far
    w["up"] = up, up_far

    def to_next(value):
        return lax.ppermute(value, "section", [(0, 1)])

    def to_last(value):
        return lax.ppermute(value, "section", [(1, 0)])

    middle = ffn_forward(w, attended, x0, False, 0, 2)[0]
    came_a, middle = stage(
        lambda: (to_next(middle), ffn_forward(w, attended, x0, False, 1, 2)[0])
    )
    came_b = stage(lambda: to_next(middle))

    first_layer = leading.astype(jnp.int32).reshape(1)

    def project_again():
        x1, q, kv = project(x0, *qkv, bias, first_layer, came_a, came_b)
        return x1, q, kv, swap_c(kv)

    x1, q, kv, kv_other = stage(project_again)
    top_sent = theirs(cotangent)

    def eighth_stage():
        attended, lse = attend_forward(info, q, kv, kv_other, window)
        return swap_y(top_sent), swap_c(x1), attended, lse

    top_came, inputs_far, attended, lse = stage(eighth_stage)
    grad_top = in_order(y == 0, mine(cotangent), top_came)
    result, normed_low, active, slope, n_one, s_one, n_two, s_two = ffn_forward(
        w, attended, x1, True
    )
    saved = dict(slope=slope, n_one=n_one, s_one=s_one, n_two=n_two, s_two=s_two)

    def dense_back(after, second):
        names = ("hidden", "before", "branch", "attended", "low_sums", "hidden_sums")
        return dict(zip(names, ffn_backward(w, saved, after, second)))

    def attention_back(grads, table, first, count):
        return attend_backward(
            info, q, kv, kv_other, grads["attended"], lse, window, table, first, count
        )

    after, second, top_sums = top_back(w, saved, jnp.zeros((1,), jnp.int32), grad_top, grad_top)

    def ninth_stage():
        return (
            swap_c(normed_low),
            swap_c(active[:, 2 * width :]),
            swap_c(attended[:, far]),
            dense_back(after, second),
        )

    normed_far, active_far, attended_far, grads = stage(ninth_stage)
    grad_q, grad_k, grad_v, k_far, v_far = attention_back(grads, False, 0, 6)

    def to_middle():
        k_came, v_came = swap_c(k_far), swap_c(v_far)
        found = input_back(grad_q, grad_k, k_came, grad_v, v_came, grads["before"], *qkv)
        return to_last(found[3])

    grad_middle = stage(to_middle)

    thirds = width // 3

    def down_grad(kind, first):
        return weight_grad(
            active, active_far, second, second_far, kind, (first, 3, thirds), (0, 1, model)
        )

    after, second, top_sums = top_back(w, saved, first_layer, grad_middle, grad_top)
    second_far = stage(lambda: swap_c(second))
    down_sent = down_grad(bf16, 3)

    def through_dense():
        grads = dense_back(after, second)
        hidden, branch = grads["hidden"], grads["branch"]
        hidden_far, branch_far = swap_c(hidden[:, 2 * width :]), swap_c(branch)
        return grads, hidden_far, branch_far, down_grad(bf16, 0)

    def send_dense(grads, hidden_far, branch_far):
        args = normed_low, normed_far, grads["hidden"], hidden_far
        sent = weight_grad(*args, bf16, (0, 3, thirds), (1, 1, width))
        branch = grads["branch"]
        return sent, split_grad(attended, attended_far, branch, branch_far, 2 * cols)

    def dense_and_sends():
        grads, hidden_far, branch_far, down_kept = through_dense()
        return grads, hidden_far, down_kept, send_dense(grads, hidden_far, branch_far)

    down_came, (grads, hidden_far, down_kept, sends) = stage(
        lambda: (swap_y(down_sent), stage(dense_and_sends))
    )
    up_sent, (out_kept, out_sent) = sends
    down = down_kept + down_came

    def through_attention():
        args = normed_low, normed_far, grads["hidden"], hidden_far
        kept = weight_grad(*args, bf16, (0, 3, thirds), (0, 1, width))
        return attention_back(grads, True, 0, 6), kept

    def through_input(q_grad, k_grad, v_grad, k_far, v_far):
        came = swap_c(k_far), swap_c(v_far)
        near, far, grad_input, grad_low, qv_sums = input_back(
            q_grad, k_grad, came[0], v_grad, came[1], grads["before"], *qkv
        )
        rest_kept, rest_sent = split_grad(near, swap_c(far), x1, inputs_far, 2 * cols)
        return rest_kept, rest_sent, grad_input, grad_low, qv_sums

    def after_down():
        up_came, out_came, (found, up_kept) = stage(
            lambda: (swap_y(up_sent), swap_y(out_sent), stage(through_attention))
        )
        *found, held = found
        found = stage(lambda: through_input(*found))
        return found, held, up_kept + up_came, out_kept + out_came

    def over_planes(value, beside):
        if planes != 4:
            return lax.psum(value, "dp"), stage(beside)
        rows = value.shape[0] // 2
        first, second = value[:rows], value[rows:]
        held, sent = jnp.where(odd == 0, first, second), jnp.where(odd == 0, second, first)
        came, found = stage(lambda: (swap_z(sent), stage(beside)))
        held = held + came
        far_planes = [(0, 2), (2, 0), (1, 3), (3, 1)]
        return held + stage(lambda: lax.ppermute(held, "dp", far_planes)), found

    def after_up():
        rest_kept, rest_sent, grad_input, grad_low, qv_sums = input_found

        def own_sums():
            sums = token_sums(held, qv_sums)
            sums = sums[:2] + swap_c(sums[2:])
            if planes == 4:
                sums = sums + swap_z(sums)
                sums = sums + lax.ppermute(sums, "dp", [(0, 2), (2, 0), (1, 3), (3, 1)])
            else:
                sums = lax.psum(sums, "dp")
            return sums, grad_down.astype(f32)[None]

        rest_came, (sums, down_out) = stage(
            lambda: (swap_y(rest_sent), stage(own_sums))
        )
        rest = rest_kept + rest_came
        grad_qkv, found = over_planes(
            rest, lambda: through_sums(sums, grad_input, grad_low)
        )
        return down_out, grad_qkv, found

    def through_sums(sums, grad_input, grad_low):
        edge_low = edge_blocks(jnp.where(leading, grad_low, result.astype(bf16)))
        edge_own = mine(edge_blocks(jnp.where(leading, grad_input, result)))
        edge_came = swap_y(theirs(edge_low)).astype(f32)
        edges = [jnp.where(y == 0, edge_own, edge_came), jnp.where(y == 0, edge_came, edge_own)]
        sums = sums[0] + swap_y(sums[1])
        at = heads * 2 * kinds
        vec_out = sums[at + 2 * cols + width :].reshape(1, 6, share)
        return (
            jnp.stack(edges)[None],
            sums[at : at + 2 * cols].reshape(1, 2, cols),
            sums[at + 2 * cols : at + 2 * cols + width].reshape(1, width),
            vec_out[:, :2],
            vec_out[:, 2:],
            sums[:at].reshape(1, heads, 2 * kinds),
        )

    share = model // 4

    def token_sums(held, qv_sums):
        wide = held.reshape(4 * heads, 2, 8 * SPAN)
        wide = jnp.stack([wide[:, 0] - wide[:, 1], wide[:, 1]], 1).reshape(8 * heads, 8 * SPAN)
        high = wide.astype(bf16)
        low = (wide - high.astype(f32)).astype(bf16)
        grad_table = dotf(high, onehot, NT) + dotf(low, onehot, NT)
        grad_table = grad_table.reshape(4, heads * 2 * kinds)
        q_sums, _, v_sums = qv_sums.reshape(3, 4, cols)
        grad_ffn = grads["hidden_sums"].reshape(4, width)
        low_sums = grads["low_sums"]
        rows = [low_sums[0], top_sums[0], low_sums[1], low_sums[2], top_sums[1], top_sums[2]]
        by_share = jnp.stack(rows).reshape(6, 4, share)
        by_share = by_share.transpose(1, 0, 2).reshape(4, 6 * share)
        by_share = jnp.stack(
            [lax.dynamic_index_in_dim(by_share, place ^ flip, 0, False) for flip in (0, 2, 1, 3)]
        )
        return jnp.concatenate([grad_table, q_sums, v_sums, grad_ffn, by_share], 1)

    grad_down, (input_found, held, *later) = stage(
        lambda: (lax.psum(down, "dp"), stage(after_down))
    )
    summed, (down_out, grad_qkv, found) = stage(lambda: (lax.psum(later, "dp"), stage(after_up)))

    def last_stage():
        back = swap_z(grad_qkv) if planes == 4 else grad_qkv
        return back, *[value.astype(f32)[None] for value in summed]

    back, up_out, out_out = stage(last_stage)
    if planes == 4:
        grad_qkv = in_order(odd == 0, grad_qkv, back)
    qkv_out = grad_qkv.astype(f32).reshape(1, 3, cols, model)
    edges, qv_out, ffn_out, gain_out, vec_out, table_out = found
    return (
        edges,
        qkv_out.transpose(0, 3, 1, 2),
        qv_out,
        out_out,
        up_out,
        ffn_out,
        down_out,
        gain_out,
        vec_out,
        table_out,
    )


def solution(mesh):
    return jax.shard_map(
        body,
        mesh=mesh,
        in_specs=(
            P("dp", "tensor", None),
            P("dp", "tensor", None),
            P("dp"),
            P("dp"),
            P(),
            P("section", None, None, "tensor"),
            P("section", None, "tensor"),
            P("section", "tensor", None),
            P("section", None, "tensor"),
            P("section", "tensor"),
            P("section", "tensor", None),
            P("section", None, None),
            P("section", None, None),
            P("section", "tensor", None),
        ),
        out_specs=(
            P("section", "dp", "tensor", None),
            P("section", None, None, "tensor"),
            P("section", None, "tensor"),
            P("section", "tensor", None),
            P("section", None, "tensor"),
            P("section", "tensor"),
            P("section", "tensor", None),
            P("section", None, "tensor"),
            P("section", None, "tensor"),
            P("section", "tensor", None),
        ),
        check_vma=False,
    )
```

```python
import functools

import jax
import jax.numpy as jnp
from jax import lax
from jax.experimental import pallas as pl
from jax.experimental.pallas import tpu as pltpu
from jax.sharding import PartitionSpec as P


f32 = jnp.float32
bf16 = jnp.bfloat16
EPS = 1e-05
HEAD = 64
NEG = -1e30
SWAP_Y = [(0, 2), (2, 0), (1, 3), (3, 1)]
SWAP_C = [(0, 1), (1, 0), (2, 3), (3, 2)]
NT = (((1,), (1,)), ((), ()))
TN = (((0,), (0,)), ((), ()))
NN = (((1,), (0,)), ((), ()))
KEY_BASE = (0, 512, 256, 768)
TILE_BASE = (0, 128, 512, 640)
STRIP = 1664
SPAN = STRIP + 128
PIECE = 32
MIB = 2**20
IN_VMEM = pl.BlockSpec(memory_space=pltpu.VMEM)


def cost(us, flops=0):
    return pl.CostEstimate(flops=flops, bytes_accessed=int(us * 3.4e6), transcendentals=0)


def dotf(a, b, dims=NN):
    return lax.dot_general(a, b, dims, preferred_element_type=f32)


def swap_y(value):
    return lax.ppermute(value, "tensor", SWAP_Y)


def swap_c(value):
    return lax.ppermute(value, "tensor", SWAP_C)


def make_strip(window_ref, h, kind, strip_ref):
    blocks = STRIP // 128
    lane = lax.broadcasted_iota(jnp.int32, (8, 128), 1)
    row = lax.broadcasted_iota(jnp.int32, (8, 128), 0)

    def rolled(first):
        at = 2 * h + kind
        seg = window_ref[at : at + 1, first : first + 128]
        seg = pltpu.roll(jnp.broadcast_to(seg, (8, 128)), 0, 1, stride=1, stride_axis=0)
        return [pltpu.roll(seg, 8 * q, 1) if q else seg for q in range(16)]

    high = rolled(128 * blocks)
    for a in range(blocks):
        low = rolled(128 * (blocks - 1 - a))
        for q in range(16):
            rows = slice(128 * a + 8 * q, 128 * a + 8 * q + 8)
            strip_ref[h, kind, rows, :] = jnp.where(lane >= row + 8 * q, high[q], low[q])
        high = low


def sum_strip(strip_ref, h, kind, held_ref):
    blocks = STRIP // 128
    lane = lax.broadcasted_iota(jnp.int32, (8, 128), 1)
    carry = jnp.zeros((8, 128), f32)
    for a in reversed(range(blocks)):
        low, high = jnp.zeros((8, 128), f32), jnp.zeros((8, 128), f32)
        for q in range(16):
            part = strip_ref[h, kind, 128 * a + 8 * q : 128 * a + 8 * q + 8, :]
            if q:
                part = pltpu.roll(part, 128 - 8 * q, 1)
            stays = lane < 128 - 8 * q
            high += jnp.where(stays, part, 0.0)
            low += jnp.where(stays, 0.0, part)
        first = 128 * (blocks - 1 - a)
        held_ref[0, h, kind, :, first : first + 128] = low + carry
        carry = high
    held_ref[0, h, kind, :, 128 * blocks : 128 * blocks + 128] = carry


def lane_mask(rows, which):
    lane = lax.broadcasted_iota(jnp.int32, (rows, 128), 1)
    return (lane < HEAD) if which == 0 else (lane >= HEAD)


def cross_mask(info_ref, tile, first):
    key_low = first < 256
    row_low = tile < 2
    if not key_low and not row_low:
        return None
    qlen, core = info_ref[0], info_ref[1]
    shape = (PIECE, 128)
    if row_low:
        row = 256 * core + 128 * tile + lax.broadcasted_iota(jnp.int32, shape, 1)
        row_side = row < qlen
    if key_low:
        key_side = first + lax.broadcasted_iota(jnp.int32, shape, 0) < qlen
    if row_low and key_low:
        return row_side != key_side
    return row_side if row_low else key_side


def pieces(kb):
    for at in range(0, 256, PIECE):
        yield KEY_BASE[kb] + at, slice(256 * kb + at, 256 * kb + at + PIECE), slice(at, at + PIECE)


def strip_rows(tile, first):
    start = first - TILE_BASE[tile] + 640
    return slice(start, start + PIECE)


def piece_scores(info_ref, raw, strip_ref, h, ib, first):
    parts = []
    for u in (0, 1):
        tile = 2 * ib + u
        rows = strip_rows(tile, first)
        bias = strip_ref[h, 0, rows, :]
        cross = cross_mask(info_ref, tile, first)
        if cross is not None:
            bias = jnp.where(cross, strip_ref[h, 1, rows, :], bias)
        parts.append(raw[:, 128 * u : 128 * u + 128] + bias)
    scores = jnp.concatenate(parts, 1)
    if first >= 256:
        live = first + lax.broadcasted_iota(jnp.int32, (PIECE, 256), 0) < info_ref[2]
        scores = jnp.where(live, scores, NEG)
    return scores


def by_eight(value):
    return value.reshape(PIECE // 8, 8, 256)


def whole(core, own, other):
    return jnp.concatenate([jnp.where(core == 0, own, other), jnp.where(core == 0, other, own)], 0)


def forward_kernel(
    info_ref,
    q_ref,
    k_ref,
    v_ref,
    ko_ref,
    vo_ref,
    win_ref,
    o_ref,
    lse_ref,
    strip_ref,
    score_ref,
    prob_ref,
):
    core = info_ref[1]
    for h in range(2):
        for kind in range(2):
            make_strip(win_ref, h, kind, strip_ref)
    keys = whole(core, k_ref[...], ko_ref[...])
    values = whole(core, v_ref[...], vo_ref[...])
    one = jnp.ones_like(values)
    turned = [jnp.where(lane_mask(1024, h), values, one).T for h in range(2)]
    for ib in range(2):
        rows = slice(256 * ib, 256 * ib + 256)
        query = q_ref[rows, :] * jnp.asarray(0.125, bf16)
        outs = []
        for h in range(2):
            one = jnp.where(lane_mask(256, h), query, jnp.zeros_like(query))
            top = None
            for kb in range(4):
                raw = dotf(keys[256 * kb : 256 * kb + 256], one, NT)
                for first, at, within in pieces(kb):
                    scores = piece_scores(info_ref, raw[within], strip_ref, h, ib, first)
                    score_ref[h, at, :] = scores
                    most = jnp.max(by_eight(scores), 0)
                    top = most if top is None else jnp.maximum(top, most)
            top = jnp.max(top, 0, keepdims=True)
            for kb in range(4):
                for _, at, _ in pieces(kb):
                    prob_ref[h, at, :] = jnp.exp(score_ref[h, at, :] - top).astype(bf16)
            mixed = dotf(turned[h], prob_ref[h])
            total = mixed[HEAD * (1 - h) : HEAD * (1 - h) + 1, :]
            lse_ref[0, h : h + 1, rows] = top + jnp.log(total)
            outs.append(mixed[HEAD * h : HEAD * h + HEAD, :] / total)
        o_ref[rows, :] = jnp.concatenate(outs, 0).T.astype(bf16)


def kv_blocks(groups, first=0):
    half = groups // 2
    return [
        pl.BlockSpec((512, 128), lambda i, s: (0, i + first)),
        pl.BlockSpec((512, 128), lambda i, s: (0, i + first + groups)),
        pl.BlockSpec((512, 128), lambda i, s: (0, (i + first + half) % groups)),
        pl.BlockSpec((512, 128), lambda i, s: (0, (i + first + half) % groups + groups)),
    ]


def attend_forward(info, q, kv, kv_other, window):
    groups = q.shape[1] // 128
    block = pl.BlockSpec((512, 128), lambda i, s: (0, i))
    return pl.pallas_call(
        forward_kernel,
        grid_spec=pltpu.PrefetchScalarGridSpec(
            num_scalar_prefetch=1,
            grid=(groups,),
            in_specs=[
                block,
                *kv_blocks(groups),
                pl.BlockSpec((8, SPAN), lambda i, s: (i, 0)),
            ],
            out_specs=[block, pl.BlockSpec((1, 2, 512), lambda i, s: (i, 0, 0))],
            scratch_shapes=[
                pltpu.VMEM((2, 2, STRIP, 128), f32),
                pltpu.VMEM((2, 1024, 256), f32),
                pltpu.VMEM((2, 1024, 256), bf16),
            ],
        ),
        out_shape=[
            jax.ShapeDtypeStruct((512, 128 * groups), bf16),
            jax.ShapeDtypeStruct((groups, 2, 512), f32),
        ],
        compiler_params=pltpu.CompilerParams(vmem_limit_bytes=24 * MIB),
        cost_estimate=cost(17),
        name="attend_forward",
    )(info, q, kv, kv, kv_other, kv_other, window)


def backward_kernel(with_table, *refs):
    info_ref, q_ref, k_ref, v_ref, ko_ref, vo_ref, do_ref, lse_ref, win_ref = refs[:9]
    dq_ref, dk_ref, dv_ref, dko_ref, dvo_ref, *rest = refs[9:]
    core = info_ref[1]
    *rest, strip_ref, wide_ref, term_ref, prob_ref, grad_ref = rest
    for h in range(2):
        for kind in range(2):
            make_strip(win_ref, h, kind, strip_ref)
    if with_table:
        held_ref, strip_grad_ref = rest
        strip_grad_ref[...] = jnp.zeros_like(strip_grad_ref)
    keys = whole(core, k_ref[...], ko_ref[...])
    values = whole(core, v_ref[...], vo_ref[...])
    keys_turned = keys.T
    key_grad = value_grad = 0.0
    for ib in range(2):
        rows = slice(256 * ib, 256 * ib + 256)
        query = q_ref[rows, :] * jnp.asarray(0.125, bf16)
        grad = do_ref[rows, :]
        query_grads = []
        for h in range(2):
            mask = lane_mask(256, h)
            one = jnp.where(mask, query, jnp.zeros_like(query))
            grad_one = jnp.where(mask, grad, jnp.zeros_like(grad))
            log_total = lse_ref[0, h : h + 1, rows]
            row_term = 0.0
            for kb in range(4):
                kr = slice(256 * kb, 256 * kb + 256)
                raw = dotf(keys[kr], one, NT)
                grad_probs = dotf(values[kr], grad_one, NT)
                for first, at, within in pieces(kb):
                    scores = piece_scores(info_ref, raw[within], strip_ref, h, ib, first)
                    probs = jnp.exp(scores - log_total)
                    term = probs * grad_probs[within]
                    wide_ref[h, at, :] = probs
                    term_ref[h, at, :] = term
                    prob_ref[h, at, :] = probs.astype(bf16)
                    row_term = row_term + jnp.sum(by_eight(term), 0)
            row_term = jnp.sum(row_term, 0, keepdims=True)
            for kb in range(4):
                for first, at, _ in pieces(kb):
                    low = (term_ref[h, at, :] - wide_ref[h, at, :] * row_term).astype(bf16)
                    grad_ref[h, at, :] = low
                    if with_table:
                        for u in (0, 1):
                            tile = 2 * ib + u
                            where = strip_rows(tile, first)
                            part = low[:, 128 * u : 128 * u + 128].astype(f32)
                            strip_grad_ref[h, 0, where, :] += part
                            cross = cross_mask(info_ref, tile, first)
                            if cross is not None:
                                strip_grad_ref[h, 1, where, :] += jnp.where(cross, part, 0.0)
            value_grad = value_grad + dotf(prob_ref[h], grad_one)
            key_grad = key_grad + dotf(grad_ref[h], one)
            flat = dotf(keys_turned, grad_ref[h])
            query_grads.append(flat[HEAD * h : HEAD * h + HEAD, :])
        dq_ref[rows, :] = (jnp.concatenate(query_grads, 0).T * 0.125).astype(bf16)
    for grads, own_ref, other_ref in (
        (key_grad, dk_ref, dko_ref),
        (value_grad, dv_ref, dvo_ref),
    ):
        first, second = grads[:512], grads[512:]
        own_ref[...] = jnp.where(core == 0, first, second)
        other_ref[...] = jnp.where(core == 0, second, first).astype(bf16)
    if with_table:
        for h in range(2):
            for kind in range(2):
                sum_strip(strip_grad_ref, h, kind, held_ref)


def attend_backward(info, q, kv, kv_other, grad, lse, window, with_table, first, count):
    groups = q.shape[1] // 128
    block = pl.BlockSpec((512, 128), lambda i, s: (0, i + first))
    rows = lambda kind: jax.ShapeDtypeStruct((512, 128 * count), kind)
    out_specs = [pl.BlockSpec((512, 128), lambda i, s: (0, i))] * 5
    out_shape = [rows(bf16), rows(f32), rows(f32), rows(bf16), rows(bf16)]
    scratch = [pltpu.VMEM((2, 2, STRIP, 128), f32)]
    if with_table:
        out_specs.append(pl.BlockSpec((1, 2, 2, 8, SPAN), lambda i, s: (i, 0, 0, 0, 0)))
        out_shape.append(jax.ShapeDtypeStruct((count, 2, 2, 8, SPAN), f32))
        scratch = scratch * 2
    scratch += [pltpu.VMEM((2, 1024, 256), f32)] * 2 + [pltpu.VMEM((2, 1024, 256), bf16)] * 2
    return pl.pallas_call(
        functools.partial(backward_kernel, with_table),
        grid_spec=pltpu.PrefetchScalarGridSpec(
            num_scalar_prefetch=1,
            grid=(count,),
            in_specs=[
                block,
                *kv_blocks(groups, first),
                block,
                pl.BlockSpec((1, 2, 512), lambda i, s: (i + first, 0, 0)),
                pl.BlockSpec((8, SPAN), lambda i, s: (i + first, 0)),
            ],
            out_specs=out_specs,
            scratch_shapes=scratch,
        ),
        out_shape=out_shape,
        compiler_params=pltpu.CompilerParams(vmem_limit_bytes=36 * MIB),
        cost_estimate=cost(30),
        name="attend_backward",
    )(info, q, kv, kv, kv_other, kv_other, grad, lse, window)


def norm_parts(values):
    centre = jnp.mean(values, -1, keepdims=True)
    centred = values - centre
    scale = lax.rsqrt(jnp.mean(centred * centred, -1, keepdims=True) + EPS)
    return centred * scale, scale


def norm_back(grad, gain, normal, scale):
    scaled = grad * gain
    return scale * (
        scaled
        - jnp.mean(scaled, -1, keepdims=True)
        - normal * jnp.mean(scaled * normal, -1, keepdims=True)
    )


def normal_cdf(units):
    size = jnp.abs(units)
    t = 1.0 / (1.0 + (0.3275911 * 0.5**0.5) * size)
    bell = jnp.exp(-0.5 * units * units)
    poly = 0.5 * 1.061405429
    for coef in (-1.453152027, 1.421413741, -0.284496736, 0.254829592):
        poly = poly * t + 0.5 * coef
    tail = poly * t * bell
    return jnp.where(units >= 0, 1.0 - tail, tail), bell


def ffn_forward_kernel(
    keep,
    att_ref,
    x_ref,
    out_ref,
    up_ref,
    up_far_ref,
    down_ref,
    down_far_ref,
    bias_ref,
    gain_ref,
    shift_ref,
    result_ref,
    *rest,
):
    if keep:
        (
            low_ref,
            active_ref,
            slope_ref,
            n_one_ref,
            s_one_ref,
            n_two_ref,
            s_two_ref,
            normed_low,
            total,
        ) = rest
    else:
        normed_low, total = rest
    i = pl.program_id(0)

    @pl.when(i == 0)
    def _():
        before = x_ref[...].astype(f32) + (dotf(att_ref[...], out_ref[...]) + shift_ref[0:1, :])
        normal, scale = norm_parts(before)
        normed = normal * gain_ref[0:1, :] + shift_ref[1:2, :]
        normed_low[...] = normed.astype(bf16)
        total[...] = normed + shift_ref[2:3, :]
        if keep:
            n_one_ref[...] = normal
            s_one_ref[...] = scale
            low_ref[...] = normed_low[...]

    near = i < 2
    width = up_ref.shape[2]
    step = 256
    add = None
    for first in range(0, width, step):
        cols = slice(first, first + step)
        up = jnp.where(near, up_ref[0, :, cols], up_far_ref[0, :, cols])
        down = jnp.where(near, down_ref[0, cols, :], down_far_ref[0, cols, :])
        units = dotf(normed_low[...], up) + bias_ref[:, cols]
        side, bell = normal_cdf(units)
        active = (units * side).astype(bf16)
        if keep:
            active_ref[:, cols] = active
            slope_ref[:, cols] = (side + units * bell * 0.3989422804014327).astype(bf16)
        part = dotf(active, down)
        add = part if add is None else add + part
    total[...] += add

    @pl.when(i == pl.num_programs(0) - 1)
    def _():
        normal, scale = norm_parts(total[...])
        result = normal * gain_ref[1:2, :] + shift_ref[3:4, :]
        result_ref[...] = result.astype(result_ref.dtype)
        if keep:
            n_two_ref[...] = normal
            s_two_ref[...] = scale


def near_far(rows, cols):
    return [
        pl.BlockSpec((1, rows, cols), lambda i: (jnp.minimum(i, 1), 0, 0)),
        pl.BlockSpec((1, rows, cols), lambda i: (jnp.maximum(i - 2, 0), 0, 0)),
    ]


def ffn_forward(w, attended, inputs, keep, part=0, parts=1):
    rows, model = inputs.shape
    rows //= parts
    width = w["up"][0].shape[2]
    all_of = lambda *shape: pl.BlockSpec(shape, lambda i: (0,) * len(shape))
    by_step = pl.BlockSpec((rows, width), lambda i: (0, i))
    shape = lambda cols, kind: jax.ShapeDtypeStruct((rows, cols), kind)
    out_specs = [all_of(rows, model)]
    out_shape = [shape(model, f32 if keep else bf16)]
    if keep:
        out_specs += [all_of(rows, model), by_step, by_step]
        out_specs += [all_of(rows, model), all_of(rows, 1)] * 2
        out_shape += [shape(model, bf16), shape(4 * width, bf16), shape(4 * width, bf16)]
        out_shape += [shape(model, f32), shape(1, f32)] * 2
    flops = 2 * rows * model * (model + 8 * width)
    return pl.pallas_call(
        functools.partial(ffn_forward_kernel, keep),
        grid=(4,),
        in_specs=[
            pl.BlockSpec((rows, model), lambda i: (part, 0)),
            pl.BlockSpec((rows, model), lambda i: (part, 0)),
            all_of(model, model),
            *near_far(model, width),
            *near_far(width, model),
            pl.BlockSpec((1, width), lambda i: (0, i)),
            all_of(2, model),
            all_of(4, model),
        ],
        out_specs=out_specs,
        out_shape=out_shape,
        scratch_shapes=[pltpu.VMEM((rows, model), bf16), pltpu.VMEM((rows, model), f32)],
        compiler_params=pltpu.CompilerParams(vmem_limit_bytes=32 * MIB),
        cost_estimate=cost(15),
        name="ffn_forward",
    )(
        attended,
        inputs,
        w["out"],
        *w["up"],
        *w["down"],
        w["up_bias"],
        w["gains"],
        w["shifts"],
    )


def top_back_kernel(
    first_ref, came_ref, gy_ref, n_two_ref, s_two_ref, gain_ref, after_ref, second_ref, sums_ref
):
    gy = jnp.where(first_ref[0] == 1, came_ref[...], gy_ref[...]).astype(f32)
    after = norm_back(gy, gain_ref[1:2, :], n_two_ref[...], s_two_ref[...])
    low = after.astype(bf16)
    after_ref[...] = after
    second_ref[...] = low
    sums_ref[0:1, :] = jnp.sum(gy * n_two_ref[...], 0, keepdims=True)
    sums_ref[1:2, :] = jnp.sum(low.astype(f32), 0, keepdims=True)
    sums_ref[2:3, :] = jnp.sum(gy, 0, keepdims=True)
    sums_ref[3:8, :] = jnp.zeros((5, sums_ref.shape[1]), f32)


def top_back(w, saved, first_layer, came, grad_y):
    rows, model = grad_y.shape
    return pl.pallas_call(
        top_back_kernel,
        in_specs=[pl.BlockSpec(memory_space=pltpu.SMEM), *[IN_VMEM] * 5],
        out_specs=[IN_VMEM] * 3,
        out_shape=[
            jax.ShapeDtypeStruct((rows, model), f32),
            jax.ShapeDtypeStruct((rows, model), bf16),
            jax.ShapeDtypeStruct((8, model), f32),
        ],
        compiler_params=pltpu.CompilerParams(vmem_limit_bytes=16 * MIB),
        cost_estimate=cost(2),
        name="top_back",
    )(first_layer, came, grad_y, saved["n_two"], saved["s_two"], w["gains"])


def ffn_backward_kernel(deps, *refs):
    (
        after_ref,
        second_ref,
        slope_ref,
        n_one_ref,
        s_one_ref,
        out_ref,
        up_ref,
        up_far_ref,
        down_ref,
        down_far_ref,
        gain_ref,
    ) = refs[:11]
    hidden_ref, before_ref, branch_ref, att_ref, sums_ref, hidden_sums_ref, total = refs[11 + deps :]
    i = pl.program_id(0)

    def add_up(value):
        return jnp.sum(value, 0, keepdims=True)

    @pl.when(i == 0)
    def _():
        total[...] = after_ref[...]

    near = i < 2
    width = up_ref.shape[2]
    step = 256
    add = None
    for first in range(0, width, step):
        cols = slice(first, first + step)
        up = jnp.where(near, up_ref[0, :, cols], up_far_ref[0, :, cols])
        down = jnp.where(near, down_ref[0, cols, :], down_far_ref[0, cols, :])
        active = dotf(second_ref[...], down, NT)
        hidden = (active * slope_ref[:, cols].astype(f32)).astype(bf16)
        hidden_ref[:, cols] = hidden
        hidden_sums_ref[0, :, cols] = add_up(hidden.astype(f32))
        part = dotf(hidden, up, NT)
        add = part if add is None else add + part
    total[...] += add

    @pl.when(i == pl.num_programs(0) - 1)
    def _():
        normed = total[...]
        before = norm_back(normed, gain_ref[0:1, :], n_one_ref[...], s_one_ref[...])
        low = before.astype(bf16)
        before_ref[...] = before
        branch_ref[...] = low
        att_ref[...] = dotf(low, out_ref[...], NT).astype(bf16)
        sums_ref[0:1, :] = add_up(normed * n_one_ref[...])
        sums_ref[1:2, :] = add_up(low.astype(f32))
        sums_ref[2:3, :] = add_up(normed)
        sums_ref[3:8, :] = jnp.zeros((5, sums_ref.shape[1]), f32)


def ffn_backward(w, saved, after, second, deps=()):
    rows, model = after.shape
    width = w["up"][0].shape[2]
    all_of = lambda *shape: pl.BlockSpec(shape, lambda i: (0,) * len(shape))
    by_step = pl.BlockSpec((rows, width), lambda i: (0, i))
    by_block = pl.BlockSpec((1, 1, width), lambda i: (i, 0, 0))
    shape = lambda cols, kind: jax.ShapeDtypeStruct((rows, cols), kind)
    whole_rows = all_of(rows, model)
    return pl.pallas_call(
        functools.partial(ffn_backward_kernel, len(deps)),
        grid=(4,),
        in_specs=[
            whole_rows,
            whole_rows,
            by_step,
            whole_rows,
            all_of(rows, 1),
            all_of(model, model),
            *near_far(model, width),
            *near_far(width, model),
            all_of(2, model),
            *[pl.BlockSpec(memory_space=pl.ANY)] * len(deps),
        ],
        out_specs=[by_step, whole_rows, whole_rows, whole_rows, all_of(8, model), by_block],
        out_shape=[
            shape(4 * width, bf16),
            shape(model, f32),
            shape(model, bf16),
            shape(model, bf16),
            jax.ShapeDtypeStruct((8, model), f32),
            jax.ShapeDtypeStruct((4, 1, width), f32),
        ],
        scratch_shapes=[pltpu.VMEM((rows, model), f32)],
        compiler_params=pltpu.CompilerParams(vmem_limit_bytes=32 * MIB),
        cost_estimate=cost(15),
        name="ffn_backward",
    )(
        after,
        second,
        saved["slope"],
        saved["n_one"],
        saved["s_one"],
        w["out"],
        *w["up"],
        *w["down"],
        w["gains"],
        *deps,
    )


def weight_grad_kernel(l_ref, lo_ref, r_ref, ro_ref, o_ref):
    total = dotf(l_ref[...], r_ref[...], TN) + dotf(lo_ref[...], ro_ref[...], TN)
    o_ref[...] = total.astype(o_ref.dtype)


def weight_grad(left, left_far, right, right_far, kind, left_cols, right_cols):
    rows = left.shape[0]
    lf, ln, lw = left_cols
    rf, rn, rw = right_cols
    return pl.pallas_call(
        weight_grad_kernel,
        grid=(rn, ln),
        in_specs=[
            pl.BlockSpec((rows, lw), lambda j, i: (0, lf + i)),
            pl.BlockSpec((rows, lw), lambda j, i: (0, lf + i)),
            pl.BlockSpec((rows, rw), lambda j, i: (0, rf + j)),
            pl.BlockSpec((rows, rw), lambda j, i: (0, rf + j)),
        ],
        out_specs=pl.BlockSpec((lw, rw), lambda j, i: (i, j)),
        out_shape=jax.ShapeDtypeStruct((ln * lw, rn * rw), kind),
        compiler_params=pltpu.CompilerParams(vmem_limit_bytes=20 * MIB),
        cost_estimate=cost(4),
        name="weight_grad",
    )(left, left_far, right, right_far)


def split_grad_kernel(l_ref, lo_ref, r_ref, ro_ref, kept_ref, sent_ref):
    total = dotf(l_ref[...], r_ref[...], TN) + dotf(lo_ref[...], ro_ref[...], TN)
    half = total.shape[0] // 2
    kept_ref[...] = total[:half].astype(bf16)
    sent_ref[...] = total[half:].astype(bf16)


def split_grad(left, left_far, right, right_far, width):
    rows, model = right.shape
    count = left_far.shape[1] // width
    left_block = pl.BlockSpec((rows, width), lambda i: (0, i))
    right_block = pl.BlockSpec((rows, model), lambda i: (0, 0))
    made = pl.BlockSpec((width // 2, model), lambda i: (i, 0))
    shape = (count * width // 2, model)
    return pl.pallas_call(
        split_grad_kernel,
        grid=(count,),
        in_specs=[left_block, left_block, right_block, right_block],
        out_specs=[made, made],
        out_shape=[jax.ShapeDtypeStruct(shape, bf16)] * 2,
        compiler_params=pltpu.CompilerParams(vmem_limit_bytes=20 * MIB),
        cost_estimate=cost(4),
        name="split_grad",
    )(left, left_far, right, right_far)


def project_kernel(x_ref, near_ref, far_ref, bias_ref, *refs):
    inputs = x_ref[...]
    *refs, q_ref, kv_ref = refs
    if refs:
        keep_ref, a_ref, b_ref, x1_ref = refs
        inputs = jnp.where(keep_ref[0] == 1, inputs, jnp.concatenate([a_ref[...], b_ref[...]], 0))
        x1_ref[...] = inputs
    half = near_ref.shape[1]
    for which in range(3):
        weight = jnp.concatenate([near_ref[which], far_ref[which]], 0)
        bias = bias_ref[:, 2 * half * which : 2 * half * (which + 1)]
        made = (dotf(inputs, weight, NT) + bias).astype(bf16)
        if which == 0:
            q_ref[...] = made
        else:
            kv_ref[:, 2 * half * (which - 1) : 2 * half * which] = made


def project(inputs, near, far, bias, *instead):
    rows, model = inputs.shape
    shapes = [(rows, model)] * (2 if instead else 1) + [(rows, 2 * model)]
    extra = [pl.BlockSpec(memory_space=pltpu.SMEM), IN_VMEM, IN_VMEM] if instead else []
    return pl.pallas_call(
        project_kernel,
        in_specs=[IN_VMEM] * 4 + extra,
        out_specs=[IN_VMEM] * len(shapes),
        out_shape=[jax.ShapeDtypeStruct(shape, bf16) for shape in shapes],
        compiler_params=pltpu.CompilerParams(vmem_limit_bytes=20 * MIB),
        cost_estimate=cost(4),
        name="project",
    )(inputs, near, far, bias, *instead)


def input_back_kernel(*refs):
    q_ref, k_ref, k_came_ref, v_ref, v_came_ref, before_ref, *weights = refs[:8]
    near_ref, far_ref, grad_ref, low_ref, sums_ref = refs[8:]
    half = near_ref.shape[1] // 3
    total = before_ref[...]
    for which in range(3):
        if which == 0:
            mixed = q_ref[...]
        else:
            own, came = (k_ref, k_came_ref) if which == 1 else (v_ref, v_came_ref)
            other = jnp.concatenate([came[:, half:], came[:, :half]], 1)
            mixed = (own[...] + other.astype(f32)).astype(bf16)
        near_ref[:, half * which : half * which + half] = mixed[:, :half]
        far_ref[:, half * which : half * which + half] = mixed[:, half:]
        sums = jnp.sum(mixed.astype(f32), 0, keepdims=True)
        sums_ref[2 * which] = sums[:, :half]
        sums_ref[2 * which + 1] = sums[:, half:]
        weight = jnp.concatenate([weights[0][which], weights[1][which]], 0)
        total = total + dotf(mixed, weight)
    grad_ref[...] = total
    low_ref[...] = total.astype(bf16)


def input_back(q, k, k_came, v, v_came, before, near, far):
    rows, model = before.shape
    half = model // 2
    return pl.pallas_call(
        input_back_kernel,
        in_specs=[IN_VMEM] * 8,
        out_specs=[IN_VMEM] * 5,
        out_shape=[
            jax.ShapeDtypeStruct((rows, 3 * half), bf16),
            jax.ShapeDtypeStruct((rows, 3 * half), bf16),
            jax.ShapeDtypeStruct((rows, model), f32),
            jax.ShapeDtypeStruct((rows, model), bf16),
            jax.ShapeDtypeStruct((6, 1, half), f32),
        ],
        compiler_params=pltpu.CompilerParams(vmem_limit_bytes=24 * MIB),
        cost_estimate=cost(6),
        name="input_back",
    )(q, k, k_came, v, v_came, before, near, far)


def body(
    hidden,
    cotangent,
    pair_lengths,
    query_lengths,
    buckets,
    qkv_weight,
    qv_bias,
    out_weight,
    up_weight,
    ffn_bias,
    down_weight,
    norm_gains,
    vectors,
    bias_table,
):
    leading = lax.axis_index("section") == 0
    place = lax.axis_index("tensor")
    y, core = place // 2, place % 2
    plane = lax.axis_index("dp")
    planes = lax.axis_size("dp")
    odd = plane % 2
    local, model = hidden.shape[1], hidden.shape[2]
    total = 4 * local
    cols = qkv_weight.shape[3]
    width = up_weight.shape[2]
    heads = bias_table.shape[1]
    kinds = bias_table.shape[2] // 2
    near, far = slice(0, 2 * cols), slice(2 * cols, 4 * cols)

    def swap_z(value):
        return lax.ppermute(value, "dp", [(i, i ^ 1) for i in range(planes)])

    def mine(array):
        return lax.dynamic_index_in_dim(array, y, 0, keepdims=False)

    def theirs(array):
        return lax.dynamic_index_in_dim(array, 1 - y, 0, keepdims=False)

    def in_order(first, own, came, axis=0):
        return jnp.concatenate(
            [jnp.where(first, own, came), jnp.where(first, came, own)], axis
        )

    def own_half(block, axis=0):
        half = block.shape[axis] // 2
        return lax.dynamic_slice_in_dim(block, half * odd, half, axis)

    def edge_blocks(value):
        return value.reshape(2, local, model)

    def stage(work):
        shapes = jax.eval_shape(work)
        return lax.cond(
            pair_lengths[0] > 0,
            work,
            lambda: jax.tree.map(lambda leaf: jnp.zeros(leaf.shape, leaf.dtype), shapes),
        )

    qkv_own = qkv_weight[0].transpose(1, 2, 0)
    out_own, up_own, down_own = out_weight[0], up_weight[0], down_weight[0]
    x_sent, qkv_sent = theirs(hidden), own_half(qkv_own, 1)

    def first_stage():
        halves = own_half(out_own), own_half(up_own), own_half(down_own)
        x_came, qkv_y = swap_y(x_sent), swap_y(qkv_sent)
        small = [qv_bias[0].reshape(-1), ffn_bias[0], bias_table[0].reshape(-1)]
        small = jnp.concatenate(small)
        return small, swap_y(small), x_came, qkv_y, halves

    small, small_y, x_came, qkv_y, (out_sent, up_sent, down_sent) = stage(first_stage)

    def gather_small():
        two = jnp.stack([small, small_y])
        four = jnp.concatenate([two, swap_c(two)])
        table = four[:, 2 * cols + width :].reshape(2 * heads, 4, kinds)
        table = jnp.pad(table, ((0, 0), (0, 4), (0, 0))).reshape(16 * heads, kinds)
        kind = jnp.pad(buckets, (1, 0))
        kind = lax.dynamic_slice_in_dim(kind, 256 * core, SPAN, 0)
        kind = jnp.stack([jnp.pad(kind, (s, 0), constant_values=-1)[:SPAN] for s in range(8)])
        kind = kind.reshape(1, 8 * SPAN)
        onehot = (kind == jnp.arange(kinds, dtype=jnp.int32)[:, None]).astype(bf16)
        window = jnp.dot(
            table, onehot[:, :SPAN].astype(f32), precision=lax.Precision.HIGHEST
        )
        qv_all = four[:, : 2 * cols].reshape(4, 2, cols)
        q_bias, v_bias = qv_all[:, 0].reshape(-1), qv_all[:, 1].reshape(-1)
        bias = jnp.concatenate([q_bias, jnp.zeros((model,), f32), v_bias])
        info = jnp.stack([mine(query_lengths), core, mine(pair_lengths)]).astype(jnp.int32)
        return (
            window,
            onehot,
            bias.reshape(1, 3 * model),
            four[:, 2 * cols : 2 * cols + width].reshape(1, 4 * width),
            info,
            in_order(y == 0, mine(hidden), x_came),
        )

    def second_stage():
        return swap_z(qkv_y), swap_y(out_sent), swap_y(up_sent), stage(gather_small)

    qkv_z, out_y, up_y, found = stage(second_stage)
    window, onehot, bias, up_bias, info, x0 = found
    w = dict(up_bias=up_bias, gains=norm_gains[0], shifts=vectors[0])

    def gather_qkv():
        near = jnp.concatenate([qkv_own, in_order(odd == 0, qkv_y, qkv_z, 1)], 1)
        far = swap_c(near)
        q, kv = project(x0, near, far, bias)
        return (near, far), q, kv, swap_c(kv)

    def third_stage():
        return stage(gather_qkv), swap_y(down_sent), swap_z(out_y), swap_z(up_y)

    (qkv, q, kv, kv_other), down_y, out_z, up_z = stage(third_stage)
    out = jnp.concatenate([out_own, in_order(odd == 0, out_y, out_z)], 0)
    up = jnp.stack([up_own, in_order(odd == 0, up_y, up_z)])

    def fourth_stage():
        found = stage(lambda: attend_forward(info, q, kv, kv_other, window)[0])
        return swap_z(down_y), swap_c(out), swap_c(up), found

    down_z, out_far, up_far, attended = stage(fourth_stage)
    down = jnp.stack([down_own, in_order(odd == 0, down_y, down_z)])
    down_far, w["out"] = stage(lambda: (swap_c(down), jnp.concatenate([out, out_far], 0)))
    w["down"] = down, down_far
    w["up"] = up, up_far

    def to_next(value):
        return lax.ppermute(value, "section", [(0, 1)])

    def to_last(value):
        return lax.ppermute(value, "section", [(1, 0)])

    middle = ffn_forward(w, attended, x0, False, 0, 2)[0]
    came_a, middle = stage(
        lambda: (to_next(middle), ffn_forward(w, attended, x0, False, 1, 2)[0])
    )
    came_b = stage(lambda: to_next(middle))

    first_layer = leading.astype(jnp.int32).reshape(1)

    def project_again():
        x1, q, kv = project(x0, *qkv, bias, first_layer, came_a, came_b)
        return x1, q, kv, swap_c(kv)

    x1, q, kv, kv_other = stage(project_again)
    top_sent = theirs(cotangent)

    def eighth_stage():
        attended, lse = attend_forward(info, q, kv, kv_other, window)
        return swap_y(top_sent), swap_c(x1), attended, lse

    top_came, inputs_far, attended, lse = stage(eighth_stage)
    grad_top = in_order(y == 0, mine(cotangent), top_came)
    result, normed_low, active, slope, n_one, s_one, n_two, s_two = ffn_forward(
        w, attended, x1, True
    )
    saved = dict(slope=slope, n_one=n_one, s_one=s_one, n_two=n_two, s_two=s_two)

    def dense_back(after, second):
        names = ("hidden", "before", "branch", "attended", "low_sums", "hidden_sums")
        return dict(zip(names, ffn_backward(w, saved, after, second)))

    def attention_back(grads, table, first, count):
        return attend_backward(
            info, q, kv, kv_other, grads["attended"], lse, window, table, first, count
        )

    after, second, top_sums = top_back(w, saved, jnp.zeros((1,), jnp.int32), grad_top, grad_top)

    def ninth_stage():
        return (
            swap_c(normed_low),
            swap_c(active[:, 2 * width :]),
            swap_c(attended[:, far]),
            dense_back(after, second),
        )

    normed_far, active_far, attended_far, grads = stage(ninth_stage)
    grad_q, grad_k, grad_v, k_far, v_far = attention_back(grads, False, 0, 6)

    def to_middle():
        k_came, v_came = swap_c(k_far), swap_c(v_far)
        found = input_back(grad_q, grad_k, k_came, grad_v, v_came, grads["before"], *qkv)
        return to_last(found[3])

    grad_middle = stage(to_middle)

    thirds = width // 3

    def down_grad(kind, first):
        return weight_grad(
            active, active_far, second, second_far, kind, (first, 3, thirds), (0, 1, model)
        )

    after, second, top_sums = top_back(w, saved, first_layer, grad_middle, grad_top)
    second_far = stage(lambda: swap_c(second))
    down_sent = down_grad(bf16, 3)

    def through_dense():
        grads = dense_back(after, second)
        hidden, branch = grads["hidden"], grads["branch"]
        hidden_far, branch_far = swap_c(hidden[:, 2 * width :]), swap_c(branch)
        return grads, hidden_far, branch_far, down_grad(bf16, 0)

    def send_dense(grads, hidden_far, branch_far):
        args = normed_low, normed_far, grads["hidden"], hidden_far
        sent = weight_grad(*args, bf16, (0, 3, thirds), (1, 1, width))
        branch = grads["branch"]
        return sent, split_grad(attended, attended_far, branch, branch_far, 2 * cols)

    def dense_and_sends():
        grads, hidden_far, branch_far, down_kept = through_dense()
        return grads, hidden_far, down_kept, send_dense(grads, hidden_far, branch_far)

    down_came, (grads, hidden_far, down_kept, sends) = stage(
        lambda: (swap_y(down_sent), stage(dense_and_sends))
    )
    up_sent, (out_kept, out_sent) = sends
    down = down_kept + down_came

    def through_attention():
        args = normed_low, normed_far, grads["hidden"], hidden_far
        kept = weight_grad(*args, bf16, (0, 3, thirds), (0, 1, width))
        return attention_back(grads, True, 0, 6), kept

    def through_input(q_grad, k_grad, v_grad, k_far, v_far):
        came = swap_c(k_far), swap_c(v_far)
        near, far, grad_input, grad_low, qv_sums = input_back(
            q_grad, k_grad, came[0], v_grad, came[1], grads["before"], *qkv
        )
        rest_kept, rest_sent = split_grad(near, swap_c(far), x1, inputs_far, 2 * cols)
        return rest_kept, rest_sent, grad_input, grad_low, qv_sums

    def after_down():
        up_came, out_came, (found, up_kept) = stage(
            lambda: (swap_y(up_sent), swap_y(out_sent), stage(through_attention))
        )
        *found, held = found
        found = stage(lambda: through_input(*found))
        return found, held, up_kept + up_came, out_kept + out_came

    def over_planes(value, beside):
        if planes != 4:
            return lax.psum(value, "dp"), stage(beside)
        rows = value.shape[0] // 2
        first, second = value[:rows], value[rows:]
        held, sent = jnp.where(odd == 0, first, second), jnp.where(odd == 0, second, first)
        came, found = stage(lambda: (swap_z(sent), stage(beside)))
        held = held + came
        far_planes = [(0, 2), (2, 0), (1, 3), (3, 1)]
        return held + stage(lambda: lax.ppermute(held, "dp", far_planes)), found

    def after_up():
        rest_kept, rest_sent, grad_input, grad_low, qv_sums = input_found

        def own_sums():
            sums = token_sums(held, qv_sums)
            sums = sums[:2] + swap_c(sums[2:])
            if planes == 4:
                sums = sums + swap_z(sums)
                sums = sums + lax.ppermute(sums, "dp", [(0, 2), (2, 0), (1, 3), (3, 1)])
            else:
                sums = lax.psum(sums, "dp")
            return sums, grad_down.astype(f32)[None]

        rest_came, (sums, down_out) = stage(
            lambda: (swap_y(rest_sent), stage(own_sums))
        )
        rest = rest_kept + rest_came
        grad_qkv, found = over_planes(
            rest, lambda: through_sums(sums, grad_input, grad_low)
        )
        return down_out, grad_qkv, found

    def through_sums(sums, grad_input, grad_low):
        edge_low = edge_blocks(jnp.where(leading, grad_low, result.astype(bf16)))
        edge_own = mine(edge_blocks(jnp.where(leading, grad_input, result)))
        edge_came = swap_y(theirs(edge_low)).astype(f32)
        edges = [jnp.where(y == 0, edge_own, edge_came), jnp.where(y == 0, edge_came, edge_own)]
        sums = sums[0] + swap_y(sums[1])
        at = heads * 2 * kinds
        vec_out = sums[at + 2 * cols + width :].reshape(1, 6, share)
        return (
            jnp.stack(edges)[None],
            sums[at : at + 2 * cols].reshape(1, 2, cols),
            sums[at + 2 * cols : at + 2 * cols + width].reshape(1, width),
            vec_out[:, :2],
            vec_out[:, 2:],
            sums[:at].reshape(1, heads, 2 * kinds),
        )

    share = model // 4

    def token_sums(held, qv_sums):
        wide = held.reshape(4 * heads, 2, 8 * SPAN)
        wide = jnp.stack([wide[:, 0] - wide[:, 1], wide[:, 1]], 1).reshape(8 * heads, 8 * SPAN)
        high = wide.astype(bf16)
        low = (wide - high.astype(f32)).astype(bf16)
        grad_table = dotf(high, onehot, NT) + dotf(low, onehot, NT)
        grad_table = grad_table.reshape(4, heads * 2 * kinds)
        q_sums, _, v_sums = qv_sums.reshape(3, 4, cols)
        grad_ffn = grads["hidden_sums"].reshape(4, width)
        low_sums = grads["low_sums"]
        rows = [low_sums[0], top_sums[0], low_sums[1], low_sums[2], top_sums[1], top_sums[2]]
        by_share = jnp.stack(rows).reshape(6, 4, share)
        by_share = by_share.transpose(1, 0, 2).reshape(4, 6 * share)
        by_share = jnp.stack(
            [lax.dynamic_index_in_dim(by_share, place ^ flip, 0, False) for flip in (0, 2, 1, 3)]
        )
        return jnp.concatenate([grad_table, q_sums, v_sums, grad_ffn, by_share], 1)

    grad_down, (input_found, held, *later) = stage(
        lambda: (lax.psum(down, "dp"), stage(after_down))
    )
    summed, (down_out, grad_qkv, found) = stage(lambda: (lax.psum(later, "dp"), stage(after_up)))

    def last_stage():
        back = swap_z(grad_qkv) if planes == 4 else grad_qkv
        return back, *[value.astype(f32)[None] for value in summed]

    back, up_out, out_out = stage(last_stage)
    if planes == 4:
        grad_qkv = in_order(odd == 0, grad_qkv, back)
    qkv_out = grad_qkv.astype(f32).reshape(1, 3, cols, model)
    edges, qv_out, ffn_out, gain_out, vec_out, table_out = found
    return (
        edges,
        qkv_out.transpose(0, 3, 1, 2),
        qv_out,
        out_out,
        up_out,
        ffn_out,
        down_out,
        gain_out,
        vec_out,
        table_out,
    )


def solution(mesh):
    return jax.shard_map(
        body,
        mesh=mesh,
        in_specs=(
            P("dp", "tensor", None),
            P("dp", "tensor", None),
            P("dp"),
            P("dp"),
            P(),
            P("section", None, None, "tensor"),
            P("section", None, "tensor"),
            P("section", "tensor", None),
            P("section", None, "tensor"),
            P("section", "tensor"),
            P("section", "tensor", None),
            P("section", None, None),
            P("section", None, None),
            P("section", "tensor", None),
        ),
        out_specs=(
            P("section", "dp", "tensor", None),
            P("section", None, None, "tensor"),
            P("section", None, "tensor"),
            P("section", "tensor", None),
            P("section", None, "tensor"),
            P("section", "tensor"),
            P("section", "tensor", None),
            P("section", None, "tensor"),
            P("section", None, "tensor"),
            P("section", "tensor", None),
        ),
        check_vma=False,
    )
```
